256 devices in a mesh: owner: 8 (over x, core), dp: 32 (over z, y).
Axes of the slice: x: 4, y: 4, z: 8, core: 2. Of those that a mesh axis runs over, the one named last changes fastest.
Arguments:
- documents: bfloat16 [262144, 768], P(('owner', 'dp')), may hold values from -6 to 6
- enc_weight: bfloat16 [768, 768], replicated, may hold values from -0.21875 to 0.21875
- label_slab: bfloat16 [4096, 768], P('owner'), may hold values from -0.21875 to 0.21875
- row_scale: bfloat16 [4096], P('owner'), may hold values from 0.25 to 4
- shortlist: int32 [262144, 32], P(('owner', 'dp')), may hold values from 0 to 1023, as said below
- positive: int32 [262144, 32], P(('owner', 'dp')), may hold values 0 or 1
- request_ids: int32 [2048, 128], P(('owner', 'dp')), may hold values from 0 to 511
- counts: int32 [256, 8], P(('owner', 'dp')), may hold values from 16 to 128, as said below
Outputs:
- slab_grad: float32 [4096, 768], P(('owner', 'dp'))
- enc_grad: float32 [768, 768], replicated
The draws below stay inside these ranges and needn't reach their ends.
Inputs may be any that keep to these rules, and one draw needn't show every extreme that they name: shortlist[n, k] = p * 128 + j names slot j of owner p among the requests of the device holding document n, with j below that device's count for owner p. `counts`: for each index of dp one owner receives 128 live slots from every device of that index. `request_ids`: slots at or past a count are never named by a shortlist.
All inputs are finite; a program needn't handle non-finite values. No bound on the sum of `positive` on one device may be relied on, other than what follows from the above.
Results may differ from the reference program's by a relative error of at most 0.0018.
Values may be sent and summed in bfloat16 or wider, within the bound.
A program may use at most 64 MiB of HBM per device.

```python
import math
import jax
import jax.numpy as jnp
from jax import lax

D = 768
DOC_DEV = 1024
LAB_DEV = 512
CAP = 128
K = 32
TOKENS = 262144
LABELS = 4096
N_OWNER = 8
N_DP = 32
DEVICES = 256


def count_table(key):
    table_key = jax.random.fold_in(key, 101)
    base_key, shift_key = jax.random.split(table_key)
    base_counts = jax.random.randint(base_key, (DEVICES, N_OWNER), CAP // 8, CAP // 4 + 1)
    offset = jax.random.randint(shift_key, (), 0, N_OWNER)
    device = jnp.arange(DEVICES, dtype=jnp.int32)
    hot_owner = (device % N_DP + offset) % N_OWNER
    is_hot = jnp.arange(N_OWNER, dtype=jnp.int32)[None, :] == hot_owner[:, None]
    return jnp.where(is_hot, CAP, base_counts).astype(jnp.int32)


def draw_counts(key, part):
    return count_table(key)


def draw_shortlist(key, part):
    table = count_table(key)
    key = jax.random.fold_in(key, 7)
    owner_key, slot_key = jax.random.split(key)
    owner_pick = jax.random.randint(owner_key, (TOKENS, K), 0, N_OWNER)
    raw_slot = jax.random.randint(slot_key, (TOKENS, K), 0, 1 << 20)
    device = (jnp.arange(TOKENS, dtype=jnp.int32) // DOC_DEV)[:, None]
    limit = table[device, owner_pick]
    return (owner_pick * CAP + raw_slot % limit).astype(jnp.int32)


def plant(array, key, low, largest):
    longest = array.shape.index(max(array.shape))
    spots = []
    for shift in (0, 1):
        where = [jax.random.randint(jax.random.fold_in(key, axis), (), 0, length) for axis, length in enumerate(array.shape)]
        where[longest] = (where[longest] + shift) % array.shape[longest]
        spots.append(tuple(where))
    return array.at[spots[0]].set(low).at[spots[1]].set(largest)


def levels(rng, extent, cuts, smallest, high):
    loudness, own = 1.0, jax.random.fold_in(rng, 6)
    for position, shards_of in cuts:
        heights = jnp.exp(jax.random.uniform(jax.random.fold_in(own, position), (shards_of,), jnp.float32, smallest / len(cuts), high / len(cuts)))
        loudness = loudness * jnp.repeat(heights, extent[position] // shards_of).reshape([-1 if axis == position else 1 for axis in range(len(extent))])
    return loudness


def bell_draw(key, shape, spread, bound, cuts=(), held_as=jnp.bfloat16):
    factor_of = levels(key, shape, cuts, -0.22, 0.18) if cuts else 1.0
    drawn = jax.random.normal(key, shape, jnp.float32) * spread * factor_of
    return jnp.minimum(jnp.maximum(drawn, -bound), bound).astype(held_as)


def setup_inputs(seed: int = 0) -> dict:
    seeds = jax.random.split(jax.random.key(seed), 9)
    documents = bell_draw(seeds[0], (TOKENS, D), 1.0, 6.0, ((0, 256),))
    enc_weight = bell_draw(seeds[1], (D, D), D ** -0.5, 0.21875)
    label_slab = bell_draw(seeds[2], (LABELS, D), D ** -0.5, 0.21875, ((0, 8),))
    row_scale = jnp.clip(jnp.exp(math.log(4.0) - 2.7725887 * jax.random.uniform(seeds[3], (LABELS,), jnp.float32) ** levels(seeds[3], (LABELS,), ((0, 8),), -0.2, 0.2)), 0.25, 4.0).astype(jnp.bfloat16)
    shortlist = draw_shortlist(jax.random.fold_in(seeds[8], 71), 0)
    positive = plant((jax.random.randint(seeds[5], (TOKENS, K), 0, 4) < 1).astype(jnp.int32), jax.random.fold_in(seeds[5], 1), 0, 1)
    request_ids = plant(jax.random.randint(seeds[6], (DEVICES * N_OWNER, CAP), 0, LAB_DEV), jax.random.fold_in(seeds[6], 1), 0, LAB_DEV - 1).astype(jnp.int32)
    counts = draw_counts(jax.random.fold_in(seeds[8], 71), 0)
    return dict(documents=documents, enc_weight=enc_weight, label_slab=label_slab, row_scale=row_scale, shortlist=shortlist, positive=positive, request_ids=request_ids, counts=counts)


def reference(documents, enc_weight, label_slab, row_scale, shortlist, positive, request_ids, counts):
    docs = documents.reshape(DEVICES, DOC_DEV, D)
    short_all = shortlist.reshape(DEVICES, DOC_DEV, K)
    pos_all = positive.reshape(DEVICES, DOC_DEV, K)
    req_all = request_ids.reshape(DEVICES, N_OWNER, CAP)
    base_rows = (jnp.arange(N_OWNER, dtype=jnp.int32) * LAB_DEV)[:, None]
    slot_count = N_OWNER * CAP
    doc_index = jnp.broadcast_to(jnp.arange(DOC_DEV, dtype=jnp.int32)[:, None], (DOC_DEV, K))

    def one_device(carry, inputs):
        slab_acc, enc_acc = carry
        block, short_ids, pos_block, req_block, count_row = inputs
        pre_act = jnp.dot(block, enc_weight, preferred_element_type=jnp.float32)
        squashed = jnp.tanh(pre_act)
        embedded = (block.astype(jnp.float32) + squashed).astype(jnp.bfloat16)
        flat_ids = (req_block + base_rows).reshape(-1).astype(jnp.int32)
        fetched = label_slab[flat_ids]
        scale_row = row_scale[flat_ids].astype(jnp.float32)
        scores = jnp.dot(embedded, fetched.T, preferred_element_type=jnp.float32)
        logits = scores * scale_row[None, :]
        chance = jax.nn.sigmoid(logits)
        usable = (jnp.arange(CAP, dtype=jnp.int32)[None, :] < count_row[:, None]).reshape(slot_count).astype(jnp.float32)
        hit_count = jnp.zeros((DOC_DEV, slot_count), jnp.float32).at[doc_index, short_ids].add(1.0)
        labels_on = jnp.zeros((DOC_DEV, slot_count), jnp.float32).at[doc_index, short_ids].add(pos_block.astype(jnp.float32))
        dlogit = ((hit_count + usable[None, :]) * chance - labels_on) / K
        dscore = (dlogit * scale_row[None, :]).astype(jnp.bfloat16)
        slot_grads = jnp.dot(dscore.T, embedded, preferred_element_type=jnp.float32).astype(jnp.bfloat16)
        slot_grads = lax.optimization_barrier(slot_grads).astype(jnp.float32)
        emb_grad = jnp.dot(dscore, fetched, preferred_element_type=jnp.float32)
        inner_grad = (emb_grad * (1.0 - squashed * squashed)).astype(jnp.bfloat16)
        enc_local = jnp.dot(block.T, inner_grad, preferred_element_type=jnp.float32)
        return (slab_acc.at[flat_ids].add(slot_grads), enc_acc + enc_local), None

    start = (jnp.zeros((LABELS, D), jnp.float32), jnp.zeros((D, D), jnp.float32))
    (slab_grad, enc_grad), _ = lax.scan(one_device, start, (docs, short_all, pos_all, req_all, counts))
    return slab_grad, enc_grad
```

```python
import functools

import jax
import jax.numpy as jnp
from jax import lax
from jax.experimental import pallas as pl
from jax.experimental.pallas import tpu as pltpu
from jax.sharding import PartitionSpec as P

MESH = pl.DeviceIdType.MESH
F32 = jnp.float32
BF16 = jnp.bfloat16


def torus(mesh):
    owners, groups = mesh.shape["owner"], mesh.shape["dp"]
    nx = owners // 2
    ny = 4 if groups >= 16 else 2
    return nx, ny, groups // ny


def place(ny):
    o, d = lax.axis_index("owner"), lax.axis_index("dp")
    return o // 2, d % ny, d // ny, o % 2


def device(ny, x, y, z, c):
    return {"owner": x * 2 + c, "dp": z * ny + y}


def remote(src, dst, send, recv, target):
    return pltpu.make_async_remote_copy(
        src_ref=src, dst_ref=dst, send_sem=send, recv_sem=recv, device_id=target, device_id_type=MESH
    )


def tail_kernel(dims, own, enc, slab_out, enc_out, sib, accp, accq, gotp, gotq, allp, allq, gota, gotb, acca, accb,
                gota2, gotb2, s_sib, r_sib, s_p, r_p, s_q, r_q, s_p2, r_p2, s_q2, r_q2, s_p3, r_p3, s_q3, r_q3,
                s_a, r_a, s_b, r_b, s_a2, r_a2, s_b2, r_b2, s_end, r_end):
    nx, ny, nz = dims
    x, y, z, c = place(ny)
    plane = [(i, j) for i in range(nx) for j in range(ny) if (i, j) != (0, 0)]
    rings = list(range(1, nz))
    cols = list(range(1, ny))
    here = x * ny + y
    rows_p, rows_q = accp.shape[1], accq.shape[1]
    wide = accp.shape[2]

    def at_plane(i, j):
        return lax.rem(x + i, nx), lax.rem(y + j, ny)

    bar = pltpu.get_barrier_semaphore()
    for i, j in plane:
        px, py = at_plane(i, j)
        pl.semaphore_signal(bar, inc=1, device_id=device(ny, px, py, z, c), device_id_type=MESH)
    for k in rings:
        pl.semaphore_signal(bar, inc=1, device_id=device(ny, x, y, lax.rem(z + k, nz), c), device_id_type=MESH)
    pl.semaphore_signal(bar, inc=1, device_id=device(ny, x, y, z, 1 - c), device_id_type=MESH)
    pl.semaphore_wait(bar, len(plane) + len(rings) + 1)

    swap = remote(enc.at[1 - c], sib, s_sib, r_sib, device(ny, x, y, z, 1 - c))
    swap.start()
    first_a, first_b = [], []
    for j in cols:
        py = lax.rem(y + j, ny)
        first_a.append(remote(own.at[:, py, :, 0:wide], gota.at[j - 1], s_a.at[j - 1], r_a.at[j - 1],
                              device(ny, x, py, z, c)))
    for k in rings:
        pz = lax.rem(z + k, nz)
        first_b.append(remote(own.at[pz, :, :, wide:], gotb.at[k - 1], s_b.at[k - 1], r_b.at[k - 1],
                              device(ny, x, y, pz, c)))
    for copy in first_a + first_b:
        copy.start()
    swap.wait()

    def join_p(q, _):
        rows = pl.ds(pl.multiple_of(q * rows_p, 8), rows_p)
        accp[q] = enc[c, rows, 0:wide] + sib[rows, 0:wide]
        return 0

    def join_q(q, _):
        rows = pl.ds(pl.multiple_of(q * rows_q, 8), rows_q)
        accq[q] = enc[c, rows, wide:] + sib[rows, wide:]
        return 0

    lax.fori_loop(0, nx * ny, join_p, 0)
    lax.fori_loop(0, nz, join_q, 0)
    p1, q1 = [], []
    for n, (i, j) in enumerate(plane):
        px, py = at_plane(i, j)
        p1.append(remote(accp.at[px * ny + py], gotp.at[n], s_p.at[n], r_p.at[n], device(ny, px, py, z, c)))
    for k in rings:
        pz = lax.rem(z + k, nz)
        q1.append(remote(accq.at[pz], gotq.at[k - 1], s_q.at[k - 1], r_q.at[k - 1], device(ny, x, y, pz, c)))
    for copy in p1 + q1:
        copy.start()

    for copy in first_a:
        copy.wait()

    def join_a(q, _):
        total = own[q, y, :, 0:wide]
        for j in cols:
            total += gota[j - 1, q]
        acca[q] = total
        return 0

    lax.fori_loop(0, nz, join_a, 0)
    second_a, second_b = [], []
    for k in rings:
        pz = lax.rem(z + k, nz)
        second_a.append(remote(acca.at[pz], gota2.at[k - 1], s_a2.at[k - 1], r_a2.at[k - 1], device(ny, x, y, pz, c)))
    for copy in second_a:
        copy.start()
    for copy in first_b:
        copy.wait()

    def join_b(q, _):
        total = own[z, q, :, wide:]
        for k in rings:
            total += gotb[k - 1, q]
        accb[q] = total
        return 0

    lax.fori_loop(0, ny, join_b, 0)
    for j in cols:
        py = lax.rem(y + j, ny)
        second_b.append(remote(accb.at[py], gotb2.at[j - 1], s_b2.at[j - 1], r_b2.at[j - 1],
                               device(ny, x, py, z, c)))
    for copy in second_b:
        copy.start()

    for copy in p1:
        copy.wait()
    total = accp[here]
    for n in range(len(plane)):
        total += gotp[n]
    allp[z] = total
    p2, q2 = [], []
    for k in rings:
        pz = lax.rem(z + k, nz)
        p2.append(remote(allp.at[z], allp.at[z], s_p2.at[k - 1], r_p2.at[k - 1], device(ny, x, y, pz, c)))
    for copy in p2:
        copy.start()
    for copy in q1:
        copy.wait()
    total = accq[z]
    for k in rings:
        total += gotq[k - 1]
    allq[here] = total
    for n, (i, j) in enumerate(plane):
        px, py = at_plane(i, j)
        q2.append(remote(allq.at[here], allq.at[here], s_q2.at[n], r_q2.at[n], device(ny, px, py, z, c)))
    for copy in q2:
        copy.start()

    for copy in second_a:
        copy.wait()
    total = acca[z]
    for k in rings:
        total += gota2[k - 1]
    slab_out[:, 0:wide] = total
    for copy in second_b:
        copy.wait()
    total = accb[y]
    for j in cols:
        total += gotb2[j - 1]
    slab_out[:, wide:] = total

    p3, q3 = [], []
    for copy in p2:
        copy.wait()
    total = allp[0]
    for k in range(1, nz):
        total += allp[k]
    rows = pl.ds(pl.multiple_of(here * rows_p, 8), rows_p)
    enc_out[c, rows, 0:wide] = total
    for n, (i, j) in enumerate(plane):
        px, py = at_plane(i, j)
        part = enc_out.at[c, rows, 0:wide]
        p3.append(remote(part, part, s_p3.at[n], r_p3.at[n], device(ny, px, py, z, c)))
    for copy in p3:
        copy.start()
    for copy in q2:
        copy.wait()
    total = allq[0]
    for k in range(1, nx * ny):
        total += allq[k]
    rows = pl.ds(pl.multiple_of(z * rows_q, 8), rows_q)
    enc_out[c, rows, wide:] = total
    for k in rings:
        pz = lax.rem(z + k, nz)
        part = enc_out.at[c, rows, wide:]
        q3.append(remote(part, part, s_q3.at[k - 1], r_q3.at[k - 1], device(ny, x, y, pz, c)))
    for copy in q3:
        copy.start()
    for copy in p3 + q3:
        copy.wait()
    last = remote(enc_out.at[c], enc_out.at[c], s_end, r_end, device(ny, x, y, z, 1 - c))
    last.start()
    last.wait()


def tail(dims, own, enc):
    nx, ny, nz = dims
    half, width = enc.shape[1:]
    depth = own.shape[2]
    plane = nx * ny
    wide = 2 * width // 3
    slim = width - wide
    vm = lambda *shape: pltpu.VMEM(shape, F32)
    dma = lambda n: [pltpu.SemaphoreType.DMA((n,))] * 2
    return pl.pallas_call(
        functools.partial(tail_kernel, dims),
        out_shape=(jax.ShapeDtypeStruct((depth, width), F32), jax.ShapeDtypeStruct((2, half, width), F32)),
        in_specs=[pl.BlockSpec(memory_space=pltpu.VMEM)] * 2,
        out_specs=[pl.BlockSpec(memory_space=pltpu.VMEM)] * 2,
        scratch_shapes=[
            vm(half, width),
            vm(plane, half // plane, wide),
            vm(nz, half // nz, slim),
            vm(plane - 1, half // plane, wide),
            vm(nz - 1, half // nz, slim),
            vm(nz, half // plane, wide),
            vm(plane, half // nz, slim),
            vm(ny - 1, nz, depth, wide),
            vm(nz - 1, ny, depth, slim),
            vm(nz, depth, wide),
            vm(ny, depth, slim),
            vm(nz - 1, depth, wide),
            vm(ny - 1, depth, slim),
            pltpu.SemaphoreType.DMA,
            pltpu.SemaphoreType.DMA,
            *dma(plane - 1), *dma(nz - 1),
            *dma(nz - 1), *dma(plane - 1),
            *dma(plane - 1), *dma(nz - 1),
            *dma(ny - 1), *dma(nz - 1),
            *dma(nz - 1), *dma(ny - 1),
            pltpu.SemaphoreType.DMA,
            pltpu.SemaphoreType.DMA,
        ],
        compiler_params=pltpu.CompilerParams(
            collective_id=1, has_side_effects=True, vmem_limit_bytes=48 * 2**20
        ),
        cost_estimate=pl.CostEstimate(flops=10**8, bytes_accessed=10**7, transcendentals=0),
        name="reduce_gradients",
    )(own, enc)


def body(dims, documents, enc_weight, label_slab, row_scale, shortlist, positive, request_ids, counts):
    owners = lax.axis_size("owner")
    capacity = request_ids.shape[1]
    feature_width = documents.shape[1]
    slot_count = owners * capacity
    pre_act = jnp.dot(documents, enc_weight, preferred_element_type=jnp.float32)
    squashed = jnp.tanh(pre_act)
    embedded = (documents.astype(jnp.float32) + squashed).astype(jnp.bfloat16)
    served = lax.all_to_all(request_ids, "owner", split_axis=0, concat_axis=0, tiled=True)
    flat_ids = served.reshape(-1)
    picked = label_slab[flat_ids].reshape(owners, capacity, feature_width)
    picked_scale = row_scale[flat_ids].reshape(owners, capacity)
    fetched, fetched_scale = (
        lax.all_to_all(picked, "owner", split_axis=0, concat_axis=0, tiled=True),
        lax.all_to_all(picked_scale, "owner", split_axis=0, concat_axis=0, tiled=True),
    )
    fetched = fetched.reshape(slot_count, feature_width)
    scale_row = fetched_scale.reshape(slot_count).astype(jnp.float32)
    scores = lax.dot_general(
        embedded, fetched, (((1,), (1,)), ((), ())), preferred_element_type=jnp.float32
    )
    logits = scores * scale_row[None, :]
    chance = jax.nn.sigmoid(logits)
    usable = (
        (jnp.arange(capacity, dtype=jnp.int32)[None, :] < counts[0][:, None])
        .reshape(slot_count)
        .astype(jnp.float32)
    )
    slot_iota = jnp.arange(slot_count, dtype=jnp.int32)
    matches = shortlist[:, :, None] == slot_iota[None, None, :]
    hit_count = jnp.sum(matches, axis=1, dtype=jnp.float32)
    labels_on = jnp.sum(jnp.where(matches, positive[:, :, None].astype(jnp.float32), 0.0), axis=1)
    dlogit = ((hit_count + usable[None, :]) * chance - labels_on) / shortlist.shape[1]
    dscore = (dlogit * scale_row[None, :]).astype(jnp.bfloat16)
    slot_grads = lax.dot_general(
        dscore, embedded, (((0,), (0,)), ((), ())), preferred_element_type=jnp.float32
    )
    slot_grads = slot_grads.astype(jnp.bfloat16).reshape(owners, capacity, feature_width)
    returned = lax.all_to_all(slot_grads, "owner", split_axis=0, concat_axis=0, tiled=True)
    owner_sum = jnp.zeros((label_slab.shape[0], feature_width), jnp.float32)
    owner_sum = owner_sum.at[flat_ids].add(
        returned.reshape(slot_count, feature_width).astype(jnp.float32)
    )
    emb_grad = jnp.dot(dscore, fetched, preferred_element_type=jnp.float32)
    inner_grad = (emb_grad * (1.0 - squashed * squashed)).astype(jnp.bfloat16)
    enc_local = lax.dot_general(
        documents, inner_grad, (((0,), (0,)), ((), ())), preferred_element_type=jnp.float32
    )
    nx, ny, nz = dims
    slab_grad, enc_grad = tail(
        dims,
        owner_sum.reshape(nz, ny, owner_sum.shape[0] // (nz * ny), feature_width),
        enc_local.reshape(2, feature_width // 2, feature_width),
    )
    enc_grad = enc_grad.reshape(feature_width, feature_width)
    return (slab_grad, enc_grad)


def solution(mesh):
    return jax.shard_map(
        functools.partial(body, torus(mesh)),
        mesh=mesh,
        in_specs=(
            P(("owner", "dp"), None),
            P(),
            P("owner", None),
            P("owner"),
            P(("owner", "dp"), None),
            P(("owner", "dp"), None),
            P(("owner", "dp"), None),
            P(("owner", "dp"), None),
        ),
        out_specs=(P(("owner", "dp"), None), P()),
        check_vma=False,
    )
```

```python
import functools

import jax
import jax.numpy as jnp
from jax import lax
from jax.experimental import pallas as pl
from jax.experimental.pallas import tpu as pltpu
from jax.sharding import PartitionSpec as P

MESH = pl.DeviceIdType.MESH
F32 = jnp.float32
BF16 = jnp.bfloat16
I32 = jnp.int32


def torus(mesh):
    owners, groups = mesh.shape["owner"], mesh.shape["dp"]
    ny = 4 if groups >= 16 else 2
    return owners // 2, ny, groups // ny


def remote(src, dst, send, recv, target):
    return pltpu.make_async_remote_copy(
        src_ref=src, dst_ref=dst, send_sem=send, recv_sem=recv, device_id=target, device_id_type=MESH
    )


def step_kernel(
    dims, docs, weight, slab, scale, ids, slots, marks, counts, slab_out, enc_out,
    emb, slope, onehot, srows, frows, sscale, fscale, gids, tally, dscore, grads, back,
    own, ownb, gota, gotb, acca, accb, gota2, gotb2,
    inner, enc, sib, accp, accq, gotp, gotq, allp, allq,
    s_id, r_id, s_f, r_f, s_c, r_c, s_g, r_g,
    s_a, r_a, s_b, r_b, s_a2, r_a2, s_b2, r_b2,
    s_sib, r_sib, s_p, r_p, s_q, r_q, s_p2, r_p2, s_q2, r_q2, s_p3, r_p3, s_q3, r_q3, s_e, r_e,
):
    nx, ny, nz = dims
    owner, group = lax.axis_index("owner"), lax.axis_index("dp")
    x, c = owner // 2, owner % 2
    y, z = group % ny, group // ny
    here = x * ny + y
    owners = 2 * nx
    cap = srows.shape[1]
    pair = 2 * cap
    documents, width = docs.shape
    rows_held = slab.shape[0]
    wide = gota.shape[-1]
    depth = gota.shape[-2]
    piece = accp.shape[1]
    half = enc.shape[1]
    cut = nx * ny * piece
    tile = min(256, documents)

    plane = [(i, j) for i in range(nx) for j in range(ny) if (i, j) != (0, 0)]
    rings = list(range(1, nz))
    cols = list(range(1, ny))

    def chip(i, j, k, core):
        return {"owner": lax.rem(x + i, nx) * 2 + core, "dp": lax.rem(z + k, nz) * ny + lax.rem(y + j, ny)}

    def spread(r):
        return r + (r // 2) * (5 - 2 * r) if nx == 4 else r

    bar = pltpu.get_barrier_semaphore()
    greeted = 0
    for i, j in plane:
        pl.semaphore_signal(bar, inc=1, device_id=chip(i, j, 0, c), device_id_type=MESH)
        greeted += 1
    for i in range(nx):
        pl.semaphore_signal(bar, inc=1, device_id=chip(i, 0, 0, 1 - c), device_id_type=MESH)
        greeted += 1
    for k in rings:
        pl.semaphore_signal(bar, inc=1, device_id=chip(0, 0, k, c), device_id_type=MESH)
        greeted += 1
    pl.semaphore_wait(bar, greeted)

    def peer(n):
        r, flip = n // 2, n % 2
        core = lax.rem(c + flip, 2)
        to = lax.rem(x + spread(r), nx) * 2 + core
        source = lax.rem(x + nx - spread(r), nx) * 2 + core
        return to, source

    def id_copy(n):
        to, _ = peer(n)
        return remote(ids.at[to], gids.at[owner], s_id.at[n], r_id.at[n], {"owner": to, "dp": group})

    for n in range(1, owners):
        id_copy(n).start()
    gids[owner] = ids[owner]

    def encode(t, _):
        rows = pl.ds(pl.multiple_of(t * tile, tile), tile)
        block = docs[rows, :]
        squashed = jnp.tanh(jnp.dot(block, weight[...], preferred_element_type=F32))
        emb[rows, :] = (block.astype(F32) + squashed).astype(BF16)
        slope[rows, :] = 1.0 - squashed * squashed
        return 0

    lax.fori_loop(0, documents // tile, encode, 0)

    def row_copy(n):
        to, _ = peer(n)
        return remote(srows.at[to], frows.at[owner], s_f.at[n], r_f.at[n], {"owner": to, "dp": group})

    def scale_copy(n):
        to, _ = peer(n)
        return remote(sscale.at[to], fscale.at[owner], s_c.at[n], r_c.at[n], {"owner": to, "dp": group})

    scale_rows = jnp.broadcast_to(scale[...].astype(BF16), (16, rows_held))

    def serve(n, _):
        to, _source = peer(n)

        @pl.when(n > 0)
        def _():
            id_copy(n).wait_send()

        hot = jnp.where(
            lax.broadcasted_iota(I32, (rows_held, cap), 0) == gids[to], 1.0, 0.0
        ).astype(BF16)
        onehot[:, pl.ds(pl.multiple_of(to * cap, cap), cap)] = hot
        rows = lax.dot_general(hot, slab[...], (((0,), (0,)), ((), ())), preferred_element_type=F32).astype(BF16)
        sc = jnp.dot(scale_rows, hot, preferred_element_type=F32).astype(BF16)
        srows[to] = rows
        sscale[to] = sc

        @pl.when(n == 0)
        def _():
            frows[owner] = rows
            fscale[owner] = sc

        @pl.when(n > 0)
        def _():
            row_copy(n).start()
            scale_copy(n).start()

        return 0

    for n in range(1, owners):
        id_copy(n).wait_recv()
    lax.fori_loop(0, owners, serve, 0)

    def grad_copy(n):
        _, source = peer(n)
        return remote(grads.at[source], back.at[owner], s_g.at[n], r_g.at[n], {"owner": source, "dp": group})

    bits = 64
    strip = 64

    def score(r, _):
        first = lax.rem(x + nx - spread(r), nx) * 2
        base = first * cap

        def count(m, _):
            low = pl.multiple_of((m // (documents // tile)) * strip, strip)
            lanes = pl.ds(pl.multiple_of((m % (documents // tile)) * tile, tile), tile)
            index = lax.broadcasted_iota(I32, (strip, tile), 0) + (base + low)
            total = jnp.zeros((strip, tile), I32)
            for k in range(slots.shape[0]):
                total += jnp.where(slots[k : k + 1, lanes] == index, marks[k : k + 1, lanes], 0)
            tally[pl.ds(low, strip), lanes] = total
            return 0

        lax.fori_loop(0, (pair // strip) * (documents // tile), count, 0)

        @pl.when(r > 0)
        def _():
            row_copy(2 * r).wait()
            scale_copy(2 * r).wait()

        row_copy(2 * r + 1).wait()
        scale_copy(2 * r + 1).wait()

        rows = frows[pl.ds(first, 2)].reshape(pair, width)
        factor, live = [], []
        for q in range(2):
            line = fscale[first + q].astype(F32)[0:1]
            factor.append(jnp.broadcast_to(line, (cap, cap)).T[:, 0:1])
            live.append(jnp.where(lax.broadcasted_iota(I32, (cap, 1), 0) < counts[0, first + q], 1.0, 0.0))
        factor = jnp.concatenate(factor, axis=0)
        live = jnp.concatenate(live, axis=0)

        def slice_of(t, _):
            lanes = pl.ds(pl.multiple_of(t * tile, tile), tile)
            logits = lax.dot_general(
                rows, emb[lanes, :], (((1,), (1,)), ((), ())), preferred_element_type=F32
            ) * factor
            chance = 0.5 * jnp.tanh(0.5 * logits) + 0.5
            mark = tally[:, lanes]
            hits = (mark & (bits - 1)).astype(F32)
            on = (mark >> 6).astype(F32)
            dlogit = ((hits + live) * chance - on) * (1.0 / slots.shape[0])
            dscore[pl.ds(pl.multiple_of(base, cap), pair), lanes] = (dlogit * factor).astype(BF16)
            return 0

        lax.fori_loop(0, documents // tile, slice_of, 0)
        mine = dscore[pl.ds(pl.multiple_of(base, cap), pair), :]
        grads[pl.ds(first, 2)] = jnp.dot(mine, emb[...], preferred_element_type=F32).astype(BF16).reshape(2, cap, width)

        @pl.when(r > 0)
        def _():
            grad_copy(2 * r).start()

        grad_copy(2 * r + 1).start()
        return 0

    lax.fori_loop(0, nx, score, 0)
    back[owner] = grads[owner]

    table = frows[...].reshape(owners * cap, width)

    def pull(t, _):
        rows = pl.ds(pl.multiple_of(t * tile, tile), tile)
        emb_grad = lax.dot_general(
            dscore[:, rows], table, (((0,), (0,)), ((), ())), preferred_element_type=F32
        )
        inner[rows, :] = (emb_grad * slope[rows, :]).astype(BF16)
        return 0

    lax.fori_loop(0, documents // tile, pull, 0)

    def outer(which):
        side = docs[:, pl.ds(pl.multiple_of(which * half, half), half)]
        enc[which] = lax.dot_general(side, inner[...], (((0,), (0,)), ((), ())), preferred_element_type=F32)

    outer(1 - c)
    swap = remote(enc.at[1 - c], sib, s_sib, r_sib, chip(0, 0, 0, 1 - c))
    swap.start()
    outer(c)
    swap.wait()

    def join_p(q, _):
        rows = pl.ds(pl.multiple_of(q * piece, piece), piece)
        accp[q] = (enc[c, rows, :] + sib[rows, :]).astype(BF16)
        return 0

    def join_q(q, _):
        rows = pl.ds(pl.multiple_of(cut + q * piece, piece), piece)
        accq[q] = (enc[c, rows, :] + sib[rows, :]).astype(BF16)
        return 0

    lax.fori_loop(0, nx * ny, join_p, 0)
    lax.fori_loop(0, nz, join_q, 0)
    p1, q1 = [], []
    for n, (i, j) in enumerate(plane):
        to = lax.rem(x + i, nx) * ny + lax.rem(y + j, ny)
        p1.append(remote(accp.at[to], gotp.at[n], s_p.at[n], r_p.at[n], chip(i, j, 0, c)))
    for k in rings:
        to = lax.rem(z + k, nz)
        q1.append(remote(accq.at[to], gotq.at[k - 1], s_q.at[k - 1], r_q.at[k - 1], chip(0, 0, k, c)))
    for copy in p1 + q1:
        copy.start()

    for copy in p1:
        copy.wait()
    rows = pl.ds(pl.multiple_of(here * piece, piece), piece)
    total = enc[c, rows, :] + sib[rows, :]
    for n in range(len(plane)):
        total += gotp[n].astype(F32)
    allp[z] = total
    p2, q2 = [], []
    for k in rings:
        p2.append(remote(allp.at[z], allp.at[z], s_p2.at[k - 1], r_p2.at[k - 1], chip(0, 0, k, c)))
    for copy in p2:
        copy.start()
    for copy in q1:
        copy.wait()
    rows = pl.ds(pl.multiple_of(cut + z * piece, piece), piece)
    total = enc[c, rows, :] + sib[rows, :]
    for k in rings:
        total += gotq[k - 1].astype(F32)
    allq[here] = total
    for n, (i, j) in enumerate(plane):
        q2.append(remote(allq.at[here], allq.at[here], s_q2.at[n], r_q2.at[n], chip(i, j, 0, c)))
    for copy in q2:
        copy.start()

    for n in range(1, owners):
        grad_copy(n).wait()
    returned = back[...].reshape(owners * cap, width)
    span = ny * depth

    def gather_rows(k, _):
        rows = pl.ds(pl.multiple_of(k * span, span), span)
        total = jnp.dot(onehot[rows, :], returned, preferred_element_type=F32).reshape(ny, depth, width)
        own[k] = total
        ownb[k] = total.astype(BF16)
        return 0

    lax.fori_loop(0, nz, gather_rows, 0)
    first_a, first_b, second_a, second_b = [], [], [], []
    for j in cols:
        py = lax.rem(y + j, ny)
        first_a.append(remote(ownb.at[:, py, :, 0:wide], gota.at[j - 1], s_a.at[j - 1], r_a.at[j - 1],
                              chip(0, j, 0, c)))
    for k in rings:
        pz = lax.rem(z + k, nz)
        first_b.append(remote(ownb.at[pz, :, :, wide:], gotb.at[k - 1], s_b.at[k - 1], r_b.at[k - 1],
                              chip(0, 0, k, c)))
    for copy in first_a + first_b:
        copy.start()

    p3, q3 = [], []
    for copy in p2:
        copy.wait()
    total = allp[0]
    for k in range(1, nz):
        total += allp[k]
    rows_p = pl.ds(pl.multiple_of(here * piece, piece), piece)
    enc_out[c, rows_p, :] = total
    for n, (i, j) in enumerate(plane):
        part = enc_out.at[c, rows_p, :]
        p3.append(remote(part, part, s_p3.at[n], r_p3.at[n], chip(i, j, 0, c)))
    for copy in p3:
        copy.start()
    for copy in q2:
        copy.wait()
    total = allq[0]
    for k in range(1, nx * ny):
        total += allq[k]
    rows_q = pl.ds(pl.multiple_of(cut + z * piece, piece), piece)
    enc_out[c, rows_q, :] = total
    for k in rings:
        part = enc_out.at[c, rows_q, :]
        q3.append(remote(part, part, s_q3.at[k - 1], r_q3.at[k - 1], chip(0, 0, k, c)))
    for copy in q3:
        copy.start()

    for copy in first_a:
        copy.wait()

    def join_a(q, _):
        total = own[q, y, :, 0:wide]
        for j in cols:
            total += gota[j - 1, q].astype(F32)
        acca[q] = total
        return 0

    lax.fori_loop(0, nz, join_a, 0)
    for k in rings:
        pz = lax.rem(z + k, nz)
        second_a.append(remote(acca.at[pz], gota2.at[k - 1], s_a2.at[k - 1], r_a2.at[k - 1], chip(0, 0, k, c)))
    for copy in second_a:
        copy.start()
    for copy in first_b:
        copy.wait()

    def join_b(q, _):
        total = own[z, q, :, wide:]
        for k in rings:
            total += gotb[k - 1, q].astype(F32)
        accb[q] = total
        return 0

    lax.fori_loop(0, ny, join_b, 0)
    for j in cols:
        py = lax.rem(y + j, ny)
        second_b.append(remote(accb.at[py], gotb2.at[j - 1], s_b2.at[j - 1], r_b2.at[j - 1], chip(0, j, 0, c)))
    for copy in second_b:
        copy.start()

    for copy in p3:
        copy.wait()
    upper = enc_out.at[c, 0:cut, :]
    lower = enc_out.at[c, cut:half, :]
    last_p = remote(upper, upper, s_e.at[0], r_e.at[0], chip(0, 0, 0, 1 - c))
    last_p.start()
    for copy in q3:
        copy.wait()
    last_q = remote(lower, lower, s_e.at[1], r_e.at[1], chip(0, 0, 0, 1 - c))
    last_q.start()

    for copy in second_a:
        copy.wait()
    total = acca[z]
    for k in rings:
        total += gota2[k - 1]
    slab_out[:, 0:wide] = total
    for copy in second_b:
        copy.wait()
    total = accb[y]
    for j in cols:
        total += gotb2[j - 1]
    slab_out[:, wide:] = total
    last_p.wait()
    last_q.wait()


def body(dims, documents, enc_weight, label_slab, row_scale, shortlist, positive, request_ids, counts):
    nx, ny, nz = dims
    docs, width = documents.shape
    held = label_slab.shape[0]
    owners, cap = request_ids.shape
    plane = nx * ny
    depth = held // (ny * nz)
    wide = 2 * width // 3
    slim = width - wide
    half = width // 2
    piece = half // (plane + nz)
    slot_count = owners * cap
    f32 = lambda *shape: pltpu.VMEM(shape, F32)
    b16 = lambda *shape: pltpu.VMEM(shape, BF16)
    i32 = lambda *shape: pltpu.VMEM(shape, I32)
    dma = lambda n: [pltpu.SemaphoreType.DMA((n,))] * 2
    vmem = pl.BlockSpec(memory_space=pltpu.VMEM)
    slab_grad, enc_grad = pl.pallas_call(
        functools.partial(step_kernel, dims),
        out_shape=(jax.ShapeDtypeStruct((depth, width), F32), jax.ShapeDtypeStruct((2, half, width), F32)),
        in_specs=[vmem] * 7 + [pl.BlockSpec(memory_space=pltpu.SMEM)],
        out_specs=[vmem] * 2,
        scratch_shapes=[
            b16(docs, width), f32(docs, width), b16(held, slot_count),
            b16(owners, cap, width), b16(owners, cap, width),
            b16(owners, 16, cap), b16(owners, 16, cap), i32(owners, 1, cap),
            i32(2 * cap, docs), b16(slot_count, docs),
            b16(owners, cap, width), b16(owners, cap, width),
            f32(nz, ny, depth, width), b16(nz, ny, depth, width),
            b16(ny - 1, nz, depth, wide), b16(nz - 1, ny, depth, slim),
            f32(nz, depth, wide), f32(ny, depth, slim),
            f32(nz - 1, depth, wide), f32(ny - 1, depth, slim),
            b16(docs, width), f32(2, half, width), f32(half, width),
            b16(plane, piece, width), b16(nz, piece, width),
            b16(plane - 1, piece, width), b16(nz - 1, piece, width),
            f32(nz, piece, width), f32(plane, piece, width),
            *dma(owners), *dma(owners), *dma(owners), *dma(owners),
            *dma(ny - 1), *dma(nz - 1), *dma(nz - 1), *dma(ny - 1),
            pltpu.SemaphoreType.DMA, pltpu.SemaphoreType.DMA,
            *dma(plane - 1), *dma(nz - 1), *dma(nz - 1), *dma(plane - 1), *dma(plane - 1), *dma(nz - 1),
            *dma(2),
        ],
        compiler_params=pltpu.CompilerParams(
            collective_id=1, has_side_effects=True, vmem_limit_bytes=56 * 2**20
        ),
        cost_estimate=pl.CostEstimate(flops=10**10, bytes_accessed=10**7, transcendentals=2 * 10**6),
        name="classifier_step",
    )(
        documents,
        enc_weight,
        label_slab,
        row_scale.reshape(1, held),
        request_ids.reshape(owners, 1, cap),
        shortlist.T,
        (1 + 64 * positive).T,
        counts,
    )
    return slab_grad, enc_grad.reshape(width, width)


def solution(mesh):
    return jax.shard_map(
        functools.partial(body, torus(mesh)),
        mesh=mesh,
        in_specs=(
            P(("owner", "dp"), None),
            P(),
            P("owner", None),
            P("owner"),
            P(("owner", "dp"), None),
            P(("owner", "dp"), None),
            P(("owner", "dp"), None),
            P(("owner", "dp"), None),
        ),
        out_specs=(P(("owner", "dp"), None), P()),
        check_vma=False,
    )
```

```python
import functools

import jax
import jax.numpy as jnp
from jax import lax
from jax.experimental import pallas as pl
from jax.experimental.pallas import tpu as pltpu
from jax.sharding import PartitionSpec as P

MESH = pl.DeviceIdType.MESH
F32 = jnp.float32
BF16 = jnp.bfloat16
I32 = jnp.int32
I16 = jnp.int16


def torus(mesh):
    owners, groups = mesh.shape["owner"], mesh.shape["dp"]
    ny = 4 if groups >= 16 else 2
    return owners // 2, ny, groups // ny


def remote(src, dst, send, recv, target):
    return pltpu.make_async_remote_copy(
        src_ref=src, dst_ref=dst, send_sem=send, recv_sem=recv, device_id=target, device_id_type=MESH
    )


def step_kernel(
    dims, docs_in, weight_in, slab_in, scale, ids, slots_in, on_in, counts, slab_out, enc_out,
    docs, weight, slab, slots32, on32, slots, marks, emb, slope, push, onehot, srows, frows, sscale, fscale, gids, tally, dscore, grads, back,
    own, ownb, gota, gotb, acca, accb, gota2, gotb2,
    inner, enc, sib, accp, accq, gotp, gotq, allp, allq,
    s_in, s_id, r_id, s_f, r_f, s_c, r_c, s_g, r_g,
    s_a, r_a, s_b, r_b, s_a2, r_a2, s_b2, r_b2,
    s_sib, r_sib, s_p, r_p, s_q, r_q, s_p2, r_p2, s_q2, r_q2, s_p3, r_p3, s_q3, r_q3, s_e, r_e,
):
    nx, ny, nz = dims
    owner, group = lax.axis_index("owner"), lax.axis_index("dp")
    x, c = owner // 2, owner % 2
    y, z = group % ny, group // ny
    here = x * ny + y
    owners = 2 * nx
    cap = srows.shape[1]
    pair = 2 * cap
    documents, width = docs.shape
    rows_held = slab.shape[0]
    wide = gota.shape[-1]
    depth = gota.shape[-2]
    piece = accp.shape[1]
    half = enc.shape[1]
    cut = nx * ny * piece
    strip = min(128, documents)

    plane = [(i, j) for i in range(nx) for j in range(ny) if (i, j) != (0, 0)]
    rings = list(range(1, nz))
    cols = list(range(1, ny))

    def chip(i, j, k, core):
        return {"owner": lax.rem(x + i, nx) * 2 + core, "dp": lax.rem(z + k, nz) * ny + lax.rem(y + j, ny)}

    def spread(r):
        return r + (r // 2) * (5 - 2 * r) if nx == 4 else r

    loads = [
        pltpu.make_async_copy(src, dst, s_in.at[n])
        for n, (src, dst) in enumerate(
            ((docs_in, docs), (weight_in, weight), (slab_in, slab), (slots_in, slots32), (on_in, on32))
        )
    ]
    for load in loads:
        load.start()

    bar = pltpu.get_barrier_semaphore()
    greeted = 0
    for i, j in plane:
        pl.semaphore_signal(bar, inc=1, device_id=chip(i, j, 0, c), device_id_type=MESH)
        greeted += 1
    for i in range(nx):
        pl.semaphore_signal(bar, inc=1, device_id=chip(i, 0, 0, 1 - c), device_id_type=MESH)
        greeted += 1
    for k in rings:
        pl.semaphore_signal(bar, inc=1, device_id=chip(0, 0, k, c), device_id_type=MESH)
        greeted += 1
    pl.semaphore_wait(bar, greeted)

    def peer(n):
        r, flip = n // 2, n % 2
        core = lax.rem(c + flip, 2)
        to = lax.rem(x + spread(r), nx) * 2 + core
        source = lax.rem(x + nx - spread(r), nx) * 2 + core
        return to, source

    def id_copy(n):
        to, _ = peer(n)
        return remote(ids.at[to], gids.at[owner], s_id.at[n], r_id.at[n], {"owner": to, "dp": group})

    for n in range(1, owners):
        id_copy(n).start()
    gids[owner] = ids[owner]

    loads[0].wait()
    loads[1].wait()
    squashed = jnp.tanh(jnp.dot(docs[...], weight[...], preferred_element_type=F32))
    emb[...] = (docs[...].astype(F32) + squashed).astype(BF16)
    slope[...] = 1.0 - squashed * squashed
    loads[2].wait()

    def row_copy(n):
        to, _ = peer(n)
        return remote(srows.at[to], frows.at[owner], s_f.at[n], r_f.at[n], {"owner": to, "dp": group})

    def scale_copy(n):
        to, _ = peer(n)
        return remote(sscale.at[to], fscale.at[owner], s_c.at[n], r_c.at[n], {"owner": to, "dp": group})

    scale_rows = jnp.broadcast_to(scale[...].reshape(1, rows_held), (16, rows_held))

    def serve(m, _):
        n = lax.rem(m + 2, owners)
        to, _source = peer(n)

        @pl.when(n > 0)
        def _():
            id_copy(n).wait_send()

        hot = jnp.where(
            lax.broadcasted_iota(I32, (rows_held, cap), 0) == gids[to], 1.0, 0.0
        ).astype(BF16)
        onehot[:, pl.ds(pl.multiple_of(to * cap, cap), cap)] = hot
        rows = lax.dot_general(hot, slab[...], (((0,), (0,)), ((), ())), preferred_element_type=F32).astype(BF16)
        sc = jnp.dot(scale_rows, hot, preferred_element_type=F32).astype(BF16)
        srows[to] = rows
        sscale[to] = sc

        @pl.when(n == 0)
        def _():
            frows[owner] = rows
            fscale[owner] = sc

        @pl.when(n > 0)
        def _():
            row_copy(n).start()
            scale_copy(n).start()

        return 0

    for n in range(1, owners):
        id_copy(n).wait_recv()
    lax.fori_loop(0, owners, serve, 0)

    def grad_copy(n):
        _, source = peer(n)
        return remote(grads.at[source], back.at[owner], s_g.at[n], r_g.at[n], {"owner": source, "dp": group})

    loads[3].wait()
    loads[4].wait()
    slots[...] = slots32[...].astype(I16)
    marks[...] = (1 + 64 * on32[...]).astype(I16)
    strips = documents // strip

    def count(m, _):
        base = pl.multiple_of((m // strips) * pair, pair)
        lanes = pl.ds(pl.multiple_of((m % strips) * strip, strip), strip)
        index = (lax.broadcasted_iota(I32, (pair, strip), 0) + base).astype(I16)
        total = jnp.zeros((pair, strip), I16)
        for k in range(slots.shape[0]):
            total += jnp.where(slots[k : k + 1, lanes] == index, marks[k : k + 1, lanes], jnp.int16(0))
        tally[pl.ds(base, pair), lanes] = total
        return 0

    lax.fori_loop(0, nx * strips, count, 0)

    def group_of(r):
        first = lax.rem(x + nx - spread(r), nx) * 2
        return first, pl.ds(pl.multiple_of(first * cap, pair), pair)

    def score(r):
        first, span = group_of(r)
        rows = frows[pl.ds(first, 2)].reshape(pair, width)
        factor, live = [], []
        for q in range(2):
            line = fscale[first + q].astype(F32)[0:1]
            factor.append(jnp.broadcast_to(line, (cap, cap)).T[:, 0:1])
            live.append(jnp.where(lax.broadcasted_iota(I32, (cap, 1), 0) < counts[0, first + q], 1.0, 0.0))
        factor = jnp.concatenate(factor, axis=0)
        live = jnp.concatenate(live, axis=0)
        logits = lax.dot_general(rows, emb[...], (((1,), (1,)), ((), ())), preferred_element_type=F32) * factor
        chance = 0.5 * jnp.tanh(0.5 * logits) + 0.5
        mark = tally[span, :].astype(I32)
        hits = (mark & 63).astype(F32)
        on = (mark >> 6).astype(F32)
        dlogit = ((hits + live) * chance - on) * (1.0 / slots.shape[0])
        dscore[span, :] = (dlogit * factor).astype(BF16)

    def row_grads(r):
        first, span = group_of(r)
        grads[pl.ds(first, 2)] = (
            jnp.dot(dscore[span, :], emb[...], preferred_element_type=F32).astype(BF16).reshape(2, cap, width)
        )

    def pulled(r):
        first, span = group_of(r)
        rows = frows[pl.ds(first, 2)].reshape(pair, width)
        return lax.dot_general(dscore[span, :], rows, (((0,), (0,)), ((), ())), preferred_element_type=F32)

    def arrived(n):
        row_copy(n).wait()
        scale_copy(n).wait()

    push[...] = jnp.zeros_like(push)

    def work(r, _):
        @pl.when(r > 0)
        def _():
            arrived(2 * r)

        arrived(2 * r + 1)
        score(r)
        row_grads(r)

        @pl.when(r > 0)
        def _():
            grad_copy(2 * r).start()

        grad_copy(2 * r + 1).start()
        push[...] += pulled(r)
        return 0

    far = nx - 1
    lax.fori_loop(0, far, work, 0)
    back[owner] = grads[owner]
    arrived(2 * far)
    arrived(2 * far + 1)
    score(far)

    inner[...] = ((push[...] + pulled(far)) * slope[...]).astype(BF16)

    def outer(which):
        side = docs[:, pl.ds(pl.multiple_of(which * half, half), half)]
        enc[which] = lax.dot_general(side, inner[...], (((0,), (0,)), ((), ())), preferred_element_type=F32)

    outer(1 - c)
    swap = remote(enc.at[1 - c], sib, s_sib, r_sib, chip(0, 0, 0, 1 - c))
    swap.start()
    outer(c)
    row_grads(far)
    grad_copy(2 * far).start()
    grad_copy(2 * far + 1).start()
    swap.wait()

    def join_p(q, _):
        rows = pl.ds(pl.multiple_of(q * piece, piece), piece)
        accp[q] = (enc[c, rows, :] + sib[rows, :]).astype(BF16)
        return 0

    def join_q(q, _):
        rows = pl.ds(pl.multiple_of(cut + q * piece, piece), piece)
        accq[q] = (enc[c, rows, :] + sib[rows, :]).astype(BF16)
        return 0

    lax.fori_loop(0, nx * ny, join_p, 0)
    lax.fori_loop(0, nz, join_q, 0)
    p1, q1 = [], []
    for n, (i, j) in enumerate(plane):
        to = lax.rem(x + i, nx) * ny + lax.rem(y + j, ny)
        p1.append(remote(accp.at[to], gotp.at[n], s_p.at[n], r_p.at[n], chip(i, j, 0, c)))
    for k in rings:
        to = lax.rem(z + k, nz)
        q1.append(remote(accq.at[to], gotq.at[k - 1], s_q.at[k - 1], r_q.at[k - 1], chip(0, 0, k, c)))
    for copy in p1 + q1:
        copy.start()

    for copy in p1:
        copy.wait()
    rows = pl.ds(pl.multiple_of(here * piece, piece), piece)
    total = enc[c, rows, :] + sib[rows, :]
    for n in range(len(plane)):
        total += gotp[n].astype(F32)
    allp[z] = total
    p2, q2 = [], []
    for k in rings:
        p2.append(remote(allp.at[z], allp.at[z], s_p2.at[k - 1], r_p2.at[k - 1], chip(0, 0, k, c)))
    for copy in p2:
        copy.start()
    for copy in q1:
        copy.wait()
    rows = pl.ds(pl.multiple_of(cut + z * piece, piece), piece)
    total = enc[c, rows, :] + sib[rows, :]
    for k in rings:
        total += gotq[k - 1].astype(F32)
    allq[here] = total
    for n, (i, j) in enumerate(plane):
        q2.append(remote(allq.at[here], allq.at[here], s_q2.at[n], r_q2.at[n], chip(i, j, 0, c)))
    for copy in q2:
        copy.start()

    for n in range(1, owners):
        grad_copy(n).wait()
    total = jnp.dot(onehot[...], back[...].reshape(owners * cap, width), preferred_element_type=F32)
    own[...] = total.reshape(own.shape)
    ownb[...] = total.astype(BF16).reshape(ownb.shape)
    first_a, first_b, second_a, second_b = [], [], [], []
    for j in cols:
        py = lax.rem(y + j, ny)
        first_a.append(remote(ownb.at[:, py, :, 0:wide], gota.at[j - 1], s_a.at[j - 1], r_a.at[j - 1],
                              chip(0, j, 0, c)))
    for k in rings:
        pz = lax.rem(z + k, nz)
        first_b.append(remote(ownb.at[pz, :, :, wide:], gotb.at[k - 1], s_b.at[k - 1], r_b.at[k - 1],
                              chip(0, 0, k, c)))
    for copy in first_a + first_b:
        copy.start()

    p3, q3 = [], []
    for copy in p2:
        copy.wait()
    total = allp[0]
    for k in range(1, nz):
        total += allp[k]
    rows_p = pl.ds(pl.multiple_of(here * piece, piece), piece)
    enc_out[c, rows_p, :] = total
    for n, (i, j) in enumerate(plane):
        part = enc_out.at[c, rows_p, :]
        p3.append(remote(part, part, s_p3.at[n], r_p3.at[n], chip(i, j, 0, c)))
    for copy in p3:
        copy.start()
    for copy in q2:
        copy.wait()
    total = allq[0]
    for k in range(1, nx * ny):
        total += allq[k]
    rows_q = pl.ds(pl.multiple_of(cut + z * piece, piece), piece)
    enc_out[c, rows_q, :] = total
    for k in rings:
        part = enc_out.at[c, rows_q, :]
        q3.append(remote(part, part, s_q3.at[k - 1], r_q3.at[k - 1], chip(0, 0, k, c)))
    for copy in q3:
        copy.start()

    for copy in first_a:
        copy.wait()

    def join_a(q, _):
        total = own[q, y, :, 0:wide]
        for j in cols:
            total += gota[j - 1, q].astype(F32)
        acca[q] = total
        return 0

    lax.fori_loop(0, nz, join_a, 0)
    for k in rings:
        pz = lax.rem(z + k, nz)
        second_a.append(remote(acca.at[pz], gota2.at[k - 1], s_a2.at[k - 1], r_a2.at[k - 1], chip(0, 0, k, c)))
    for copy in second_a:
        copy.start()
    for copy in first_b:
        copy.wait()

    def join_b(q, _):
        total = own[z, q, :, wide:]
        for k in rings:
            total += gotb[k - 1, q].astype(F32)
        accb[q] = total
        return 0

    lax.fori_loop(0, ny, join_b, 0)
    for j in cols:
        py = lax.rem(y + j, ny)
        second_b.append(remote(accb.at[py], gotb2.at[j - 1], s_b2.at[j - 1], r_b2.at[j - 1], chip(0, j, 0, c)))
    for copy in second_b:
        copy.start()

    for copy in p3:
        copy.wait()
    upper = enc_out.at[c, 0:cut, :]
    lower = enc_out.at[c, cut:half, :]
    last_p = remote(upper, upper, s_e.at[0], r_e.at[0], chip(0, 0, 0, 1 - c))
    last_p.start()
    for copy in q3:
        copy.wait()
    last_q = remote(lower, lower, s_e.at[1], r_e.at[1], chip(0, 0, 0, 1 - c))
    last_q.start()

    for copy in second_a:
        copy.wait()
    total = acca[z]
    for k in rings:
        total += gota2[k - 1]
    slab_out[:, 0:wide] = total
    for copy in second_b:
        copy.wait()
    total = accb[y]
    for j in cols:
        total += gotb2[j - 1]
    slab_out[:, wide:] = total
    last_p.wait()
    last_q.wait()


def body(dims, documents, enc_weight, label_slab, row_scale, shortlist, positive, request_ids, counts):
    nx, ny, nz = dims
    docs, width = documents.shape
    held = label_slab.shape[0]
    owners, cap = request_ids.shape
    picks = shortlist.shape[1]
    plane = nx * ny
    depth = held // (ny * nz)
    wide = 2 * width // 3
    slim = width - wide
    half = width // 2
    piece = half // (plane + nz)
    slot_count = owners * cap
    f32 = lambda *shape: pltpu.VMEM(shape, F32)
    b16 = lambda *shape: pltpu.VMEM(shape, BF16)
    i32 = lambda *shape: pltpu.VMEM(shape, I32)
    i16 = lambda *shape: pltpu.VMEM(shape, I16)
    dma = lambda n: [pltpu.SemaphoreType.DMA((n,))] * 2
    vmem = pl.BlockSpec(memory_space=pltpu.VMEM)
    anywhere = pl.BlockSpec(memory_space=pl.ANY)
    slab_grad, enc_grad = pl.pallas_call(
        functools.partial(step_kernel, dims),
        out_shape=(jax.ShapeDtypeStruct((depth, width), F32), jax.ShapeDtypeStruct((2, half, width), F32)),
        in_specs=[anywhere] * 3 + [vmem] * 2 + [anywhere] * 2 + [pl.BlockSpec(memory_space=pltpu.SMEM)],
        out_specs=[vmem] * 2,
        scratch_shapes=[
            b16(docs, width), b16(width, width), b16(held, width), i32(picks, docs), i32(picks, docs),
            i16(picks, docs), i16(picks, docs),
            b16(docs, width), f32(docs, width), f32(docs, width), b16(held, slot_count),
            b16(owners, cap, width), b16(owners, cap, width),
            b16(owners, 16, cap), b16(owners, 16, cap), i32(owners, 1, cap),
            i16(slot_count, docs), b16(slot_count, docs),
            b16(owners, cap, width), b16(owners, cap, width),
            f32(nz, ny, depth, width), b16(nz, ny, depth, width),
            b16(ny - 1, nz, depth, wide), b16(nz - 1, ny, depth, slim),
            f32(nz, depth, wide), f32(ny, depth, slim),
            f32(nz - 1, depth, wide), f32(ny - 1, depth, slim),
            b16(docs, width), f32(2, half, width), f32(half, width),
            b16(plane, piece, width), b16(nz, piece, width),
            b16(plane - 1, piece, width), b16(nz - 1, piece, width),
            f32(nz, piece, width), f32(plane, piece, width),
            pltpu.SemaphoreType.DMA((5,)), *dma(owners), *dma(owners), *dma(owners), *dma(owners),
            *dma(ny - 1), *dma(nz - 1), *dma(nz - 1), *dma(ny - 1),
            pltpu.SemaphoreType.DMA, pltpu.SemaphoreType.DMA,
            *dma(plane - 1), *dma(nz - 1), *dma(nz - 1), *dma(plane - 1), *dma(plane - 1), *dma(nz - 1),
            *dma(2),
        ],
        compiler_params=pltpu.CompilerParams(
            collective_id=1, has_side_effects=True, vmem_limit_bytes=56 * 2**20
        ),
        cost_estimate=pl.CostEstimate(flops=10**10, bytes_accessed=10**7, transcendentals=2 * 10**6),
        name="classifier_step",
    )(
        documents,
        enc_weight,
        label_slab,
        row_scale,
        request_ids.reshape(owners, 1, cap),
        shortlist.T,
        positive.T,
        counts,
    )
    return slab_grad, enc_grad.reshape(width, width)


def solution(mesh):
    return jax.shard_map(
        functools.partial(body, torus(mesh)),
        mesh=mesh,
        in_specs=(
            P(("owner", "dp"), None),
            P(),
            P("owner", None),
            P("owner"),
            P(("owner", "dp"), None),
            P(("owner", "dp"), None),
            P(("owner", "dp"), None),
            P(("owner", "dp"), None),
        ),
        out_specs=(P(("owner", "dp"), None), P()),
        check_vma=False,
    )
```

```python
import functools

import jax
import jax.numpy as jnp
from jax import lax
from jax.experimental import pallas as pl
from jax.experimental.pallas import tpu as pltpu
from jax.sharding import PartitionSpec as P

MESH = pl.DeviceIdType.MESH
F32 = jnp.float32
BF16 = jnp.bfloat16
I32 = jnp.int32
I16 = jnp.int16


def torus(mesh):
    owners, groups = mesh.shape["owner"], mesh.shape["dp"]
    ny = 4 if groups >= 16 else 2
    return owners // 2, ny, groups // ny


def remote(src, dst, send, recv, target):
    return pltpu.make_async_remote_copy(
        src_ref=src, dst_ref=dst, send_sem=send, recv_sem=recv, device_id=target, device_id_type=MESH
    )


def step_kernel(
    dims, docs_in, weight_in, slab_in, scale, ids, slots_in, on_in, counts, slab_out, enc_out,
    docs, weight, slab, slots32, on32, slots, marks, emb, slope, push, onehot, srows, frows, sscale, fscale, gids, tally, dscore, grads, back,
    own, ownb, gota, gotb, acca, accb, gota2, gotb2,
    inner, enc, sib, accp, accq, gotp, gotq, allp, allq,
    s_in, s_id, r_id, s_f, r_f, s_c, r_c, s_g, r_g,
    s_a, r_a, s_b, r_b, s_a2, r_a2, s_b2, r_b2,
    s_sib, r_sib, s_p, r_p, s_q, r_q, s_p2, r_p2, s_q2, r_q2, s_p3, r_p3, s_q3, r_q3, s_e, r_e,
):
    nx, ny, nz = dims
    owner, group = lax.axis_index("owner"), lax.axis_index("dp")
    x, c = owner // 2, owner % 2
    y, z = group % ny, group // ny
    here = x * ny + y
    owners = 2 * nx
    cap = srows.shape[1]
    pair = 2 * cap
    documents, width = docs.shape
    rows_held = slab.shape[0]
    wide = gota.shape[-1]
    depth = gota.shape[-2]
    piece = accp.shape[1]
    half = enc.shape[1]
    cut = nx * ny * piece
    strip = min(128, documents)
    far = nx - 1

    plane = [(i, j) for i in range(nx) for j in range(ny) if (i, j) != (0, 0)]
    rings = list(range(1, nz))
    cols = list(range(1, ny))

    def chip(i, j, k, core):
        return {"owner": lax.rem(x + i, nx) * 2 + core, "dp": lax.rem(z + k, nz) * ny + lax.rem(y + j, ny)}

    def spread(r):
        return r + (r // 2) * (5 - 2 * r) if nx == 4 else r

    loads = [
        pltpu.make_async_copy(src, dst, s_in.at[n])
        for n, (src, dst) in enumerate(
            ((docs_in, docs), (weight_in, weight), (slab_in, slab), (slots_in, slots32), (on_in, on32))
        )
    ]
    for load in loads:
        load.start()

    bar = pltpu.get_barrier_semaphore()
    greeted = 0
    for i, j in plane:
        pl.semaphore_signal(bar, inc=1, device_id=chip(i, j, 0, c), device_id_type=MESH)
        greeted += 1
    for i in range(nx):
        pl.semaphore_signal(bar, inc=1, device_id=chip(i, 0, 0, 1 - c), device_id_type=MESH)
        greeted += 1
    for k in rings:
        pl.semaphore_signal(bar, inc=1, device_id=chip(0, 0, k, c), device_id_type=MESH)
        greeted += 1
    pl.semaphore_wait(bar, greeted)

    def peer(n):
        r, flip = n // 2, n % 2
        core = lax.rem(c + flip, 2)
        to = lax.rem(x + spread(r), nx) * 2 + core
        source = lax.rem(x + nx - spread(r), nx) * 2 + core
        return to, source

    def id_copy(n):
        to, _ = peer(n)
        return remote(ids.at[to], gids.at[owner], s_id.at[n], r_id.at[n], {"owner": to, "dp": group})

    for n in range(1, owners):
        id_copy(n).start()
    gids[owner] = ids[owner]

    loads[0].wait()
    loads[1].wait()
    squashed = jnp.tanh(jnp.dot(docs[...], weight[...], preferred_element_type=F32))
    emb[...] = (docs[...].astype(F32) + squashed).astype(BF16)
    slope[...] = 1.0 - squashed * squashed
    loads[2].wait()

    def row_copy(n):
        to, _ = peer(n)
        return remote(srows.at[to], frows.at[owner], s_f.at[n], r_f.at[n], {"owner": to, "dp": group})

    def scale_copy(n):
        to, _ = peer(n)
        return remote(sscale.at[to], fscale.at[owner], s_c.at[n], r_c.at[n], {"owner": to, "dp": group})

    scale_rows = jnp.broadcast_to(scale[...].reshape(1, rows_held), (16, rows_held))

    def serve(m, _):
        n = lax.rem(m + 2, owners)
        to, _source = peer(n)

        @pl.when(n > 0)
        def _():
            id_copy(n).wait_send()

        hot = jnp.where(
            lax.broadcasted_iota(I32, (rows_held, cap), 0) == gids[to], 1.0, 0.0
        ).astype(BF16)
        onehot[:, pl.ds(pl.multiple_of(to * cap, cap), cap)] = hot
        rows = lax.dot_general(hot, slab[...], (((0,), (0,)), ((), ())), preferred_element_type=F32).astype(BF16)
        sc = jnp.dot(scale_rows, hot, preferred_element_type=F32).astype(BF16)
        srows[to] = rows
        sscale[to] = sc

        @pl.when(n == 0)
        def _():
            frows[owner] = rows
            fscale[owner] = sc

        @pl.when((n > 0) & (n < 2 * far))
        def _():
            row_copy(n).start()
            scale_copy(n).start()

        return 0

    for n in range(1, owners):
        id_copy(n).wait_recv()
    lax.fori_loop(0, owners, serve, 0)

    def grad_copy(n):
        _, source = peer(n)
        return remote(grads.at[source], back.at[owner], s_g.at[n], r_g.at[n], {"owner": source, "dp": group})

    loads[3].wait()
    loads[4].wait()
    slots[...] = slots32[...].astype(I16)
    marks[...] = (1 + 64 * on32[...]).astype(I16)
    strips = documents // strip

    def count(m, _):
        base = pl.multiple_of((m // strips) * pair, pair)
        lanes = pl.ds(pl.multiple_of((m % strips) * strip, strip), strip)
        index = (lax.broadcasted_iota(I32, (pair, strip), 0) + base).astype(I16)
        total = jnp.zeros((pair, strip), I16)
        for k in range(slots.shape[0]):
            total += jnp.where(slots[k : k + 1, lanes] == index, marks[k : k + 1, lanes], jnp.int16(0))
        tally[pl.ds(base, pair), lanes] = total
        return 0

    lax.fori_loop(0, nx * strips, count, 0)

    def group_of(r):
        first = lax.rem(x + nx - spread(r), nx) * 2
        return first, pl.ds(pl.multiple_of(first * cap, pair), pair)

    def score(r):
        first, span = group_of(r)
        rows = frows[pl.ds(first, 2)].reshape(pair, width)
        factor, live = [], []
        for q in range(2):
            line = fscale[first + q].astype(F32)[0:1]
            factor.append(jnp.broadcast_to(line, (cap, cap)).T[:, 0:1])
            live.append(jnp.where(lax.broadcasted_iota(I32, (cap, 1), 0) < counts[0, first + q], 1.0, 0.0))
        factor = jnp.concatenate(factor, axis=0)
        live = jnp.concatenate(live, axis=0)
        logits = lax.dot_general(rows, emb[...], (((1,), (1,)), ((), ())), preferred_element_type=F32) * factor
        chance = 0.5 * jnp.tanh(0.5 * logits) + 0.5
        mark = tally[span, :].astype(I32)
        hits = (mark & 63).astype(F32)
        on = (mark >> 6).astype(F32)
        dlogit = ((hits + live) * chance - on) * (1.0 / slots.shape[0])
        dscore[span, :] = (dlogit * factor).astype(BF16)

    def row_grads(r):
        first, span = group_of(r)
        grads[pl.ds(first, 2)] = (
            jnp.dot(dscore[span, :], emb[...], preferred_element_type=F32).astype(BF16).reshape(2, cap, width)
        )

    def pulled(r):
        first, span = group_of(r)
        rows = frows[pl.ds(first, 2)].reshape(pair, width)
        return lax.dot_general(dscore[span, :], rows, (((0,), (0,)), ((), ())), preferred_element_type=F32)

    def sent(n):
        row_copy(n).wait_send()
        scale_copy(n).wait_send()

    def arrived(n):
        row_copy(n).wait_recv()
        scale_copy(n).wait_recv()

    for n in range(2, 2 * far):
        sent(n)
    for n in (2 * far, 2 * far + 1):
        row_copy(n).start()
        scale_copy(n).start()
    sent(1)

    push[...] = jnp.zeros_like(push)

    def work(r, _):
        @pl.when(r > 0)
        def _():
            arrived(2 * r)

        arrived(2 * r + 1)
        score(r)
        row_grads(r)

        push[...] += pulled(r)
        return 0

    lax.fori_loop(0, far, work, 0)
    back[owner] = grads[owner]
    for n in (2 * far, 2 * far + 1):
        sent(n)
        arrived(n)
    for n in range(1, 2 * far):
        grad_copy(n).start()
    score(far)

    inner[...] = ((push[...] + pulled(far)) * slope[...]).astype(BF16)

    def outer(which):
        side = docs[:, pl.ds(pl.multiple_of(which * half, half), half)]
        enc[which] = lax.dot_general(side, inner[...], (((0,), (0,)), ((), ())), preferred_element_type=F32)

    outer(1 - c)
    swap = remote(enc.at[1 - c], sib, s_sib, r_sib, chip(0, 0, 0, 1 - c))
    swap.start()
    outer(c)
    row_grads(far)
    grad_copy(2 * far).start()
    grad_copy(2 * far + 1).start()
    swap.wait()

    def join_p(q, _):
        rows = pl.ds(pl.multiple_of(q * piece, piece), piece)
        accp[q] = (enc[c, rows, :] + sib[rows, :]).astype(BF16)
        return 0

    def join_q(q, _):
        rows = pl.ds(pl.multiple_of(cut + q * piece, piece), piece)
        accq[q] = (enc[c, rows, :] + sib[rows, :]).astype(BF16)
        return 0

    lax.fori_loop(0, nx * ny, join_p, 0)
    lax.fori_loop(0, nz, join_q, 0)
    p1, q1 = [], []
    for n, (i, j) in enumerate(plane):
        to = lax.rem(x + i, nx) * ny + lax.rem(y + j, ny)
        p1.append(remote(accp.at[to], gotp.at[n], s_p.at[n], r_p.at[n], chip(i, j, 0, c)))
    for k in rings:
        to = lax.rem(z + k, nz)
        q1.append(remote(accq.at[to], gotq.at[k - 1], s_q.at[k - 1], r_q.at[k - 1], chip(0, 0, k, c)))
    for copy in p1 + q1:
        copy.start()

    for n in range(1, owners):
        grad_copy(n).wait()
    total = jnp.dot(onehot[...], back[...].reshape(owners * cap, width), preferred_element_type=F32)
    own[...] = total.reshape(own.shape)
    ownb[...] = total.astype(BF16).reshape(ownb.shape)
    first_a, first_b, second_a, second_b = [], [], [], []
    for j in cols:
        py = lax.rem(y + j, ny)
        first_a.append(remote(ownb.at[:, py, :, 0:wide], gota.at[j - 1], s_a.at[j - 1], r_a.at[j - 1],
                              chip(0, j, 0, c)))
    for k in rings:
        pz = lax.rem(z + k, nz)
        first_b.append(remote(ownb.at[pz, :, :, wide:], gotb.at[k - 1], s_b.at[k - 1], r_b.at[k - 1],
                              chip(0, 0, k, c)))
    for copy in first_a + first_b:
        copy.start()

    for copy in p1:
        copy.wait()
    rows = pl.ds(pl.multiple_of(here * piece, piece), piece)
    total = enc[c, rows, :] + sib[rows, :]
    for n in range(len(plane)):
        total += gotp[n].astype(F32)
    allp[z] = total
    p2, q2 = [], []
    for k in rings:
        p2.append(remote(allp.at[z], allp.at[z], s_p2.at[k - 1], r_p2.at[k - 1], chip(0, 0, k, c)))
    for copy in p2:
        copy.start()
    for copy in q1:
        copy.wait()
    rows = pl.ds(pl.multiple_of(cut + z * piece, piece), piece)
    total = enc[c, rows, :] + sib[rows, :]
    for k in rings:
        total += gotq[k - 1].astype(F32)
    allq[here] = total
    for n, (i, j) in enumerate(plane):
        q2.append(remote(allq.at[here], allq.at[here], s_q2.at[n], r_q2.at[n], chip(i, j, 0, c)))
    for copy in q2:
        copy.start()

    for copy in first_a:
        copy.wait()

    def join_a(q, _):
        total = own[q, y, :, 0:wide]
        for j in cols:
            total += gota[j - 1, q].astype(F32)
        acca[q] = total
        return 0

    lax.fori_loop(0, nz, join_a, 0)
    for k in rings:
        pz = lax.rem(z + k, nz)
        second_a.append(remote(acca.at[pz], gota2.at[k - 1], s_a2.at[k - 1], r_a2.at[k - 1], chip(0, 0, k, c)))
    for copy in second_a:
        copy.start()
    for copy in first_b:
        copy.wait()

    def join_b(q, _):
        total = own[z, q, :, wide:]
        for k in rings:
            total += gotb[k - 1, q].astype(F32)
        accb[q] = total
        return 0

    lax.fori_loop(0, ny, join_b, 0)
    for j in cols:
        py = lax.rem(y + j, ny)
        second_b.append(remote(accb.at[py], gotb2.at[j - 1], s_b2.at[j - 1], r_b2.at[j - 1], chip(0, j, 0, c)))
    for copy in second_b:
        copy.start()

    p3, q3 = [], []
    for copy in p2:
        copy.wait()
    total = allp[0]
    for k in range(1, nz):
        total += allp[k]
    rows_p = pl.ds(pl.multiple_of(here * piece, piece), piece)
    enc_out[c, rows_p, :] = total
    for n, (i, j) in enumerate(plane):
        part = enc_out.at[c, rows_p, :]
        p3.append(remote(part, part, s_p3.at[n], r_p3.at[n], chip(i, j, 0, c)))
    for copy in p3:
        copy.start()
    for copy in q2:
        copy.wait()
    total = allq[0]
    for k in range(1, nx * ny):
        total += allq[k]
    rows_q = pl.ds(pl.multiple_of(cut + z * piece, piece), piece)
    enc_out[c, rows_q, :] = total
    for k in rings:
        part = enc_out.at[c, rows_q, :]
        q3.append(remote(part, part, s_q3.at[k - 1], r_q3.at[k - 1], chip(0, 0, k, c)))
    for copy in q3:
        copy.start()

    def pass_on(first, n):
        part = enc_out.at[c, pl.ds(pl.multiple_of(first, piece), piece), :]
        copy = remote(part, part, s_e.at[n], r_e.at[n], chip(0, 0, 0, 1 - c))
        copy.start()
        return copy

    handed = [pass_on(here * piece, 0), pass_on(cut + z * piece, 1)]
    for k in rings:
        q3[k - 1].wait()
        handed.append(pass_on(cut + lax.rem(z + nz - k, nz) * piece, 1 + k))
    for n, (i, j) in enumerate(plane):
        p3[n].wait()
        source = lax.rem(x + nx - i, nx) * ny + lax.rem(y + ny - j, ny)
        handed.append(pass_on(source * piece, nz + 1 + n))

    for copy in second_a:
        copy.wait()
    total = acca[z]
    for k in rings:
        total += gota2[k - 1]
    slab_out[:, 0:wide] = total
    for copy in second_b:
        copy.wait()
    total = accb[y]
    for j in cols:
        total += gotb2[j - 1]
    slab_out[:, wide:] = total
    for copy in handed:
        copy.wait()


def settle_kernel(slab, enc, slab_out, enc_out, sems):
    rows = enc.shape[0] // 4
    copies = [pltpu.make_async_copy(slab, slab_out, sems.at[4])]
    for n in range(4):
        part = pl.ds(n * rows, rows)
        copies.append(pltpu.make_async_copy(enc.at[part], enc_out.at[part], sems.at[n]))
    for copy in copies:
        copy.start()
    for copy in copies:
        copy.wait()


def settle(slab, enc):
    anywhere = pl.BlockSpec(memory_space=pl.ANY)
    return pl.pallas_call(
        settle_kernel,
        out_shape=(jax.ShapeDtypeStruct(slab.shape, F32), jax.ShapeDtypeStruct(enc.shape, F32)),
        in_specs=[anywhere] * 2,
        out_specs=[anywhere] * 2,
        scratch_shapes=[pltpu.SemaphoreType.DMA((5,))],
        name="settle",
    )(slab, enc)


def body(dims, documents, enc_weight, label_slab, row_scale, shortlist, positive, request_ids, counts):
    nx, ny, nz = dims
    docs, width = documents.shape
    held = label_slab.shape[0]
    owners, cap = request_ids.shape
    picks = shortlist.shape[1]
    plane = nx * ny
    depth = held // (ny * nz)
    wide = 2 * width // 3
    slim = width - wide
    half = width // 2
    piece = half // (plane + nz)
    slot_count = owners * cap
    f32 = lambda *shape: pltpu.VMEM(shape, F32)
    b16 = lambda *shape: pltpu.VMEM(shape, BF16)
    i32 = lambda *shape: pltpu.VMEM(shape, I32)
    i16 = lambda *shape: pltpu.VMEM(shape, I16)
    dma = lambda n: [pltpu.SemaphoreType.DMA((n,))] * 2
    vmem = pl.BlockSpec(memory_space=pltpu.VMEM)
    anywhere = pl.BlockSpec(memory_space=pl.ANY)
    slab_grad, enc_grad = pl.pallas_call(
        functools.partial(step_kernel, dims),
        out_shape=(jax.ShapeDtypeStruct((depth, width), F32), jax.ShapeDtypeStruct((2, half, width), F32)),
        in_specs=[anywhere] * 3 + [vmem] * 2 + [anywhere] * 2 + [pl.BlockSpec(memory_space=pltpu.SMEM)],
        out_specs=[vmem] * 2,
        scratch_shapes=[
            b16(docs, width), b16(width, width), b16(held, width), i32(picks, docs), i32(picks, docs),
            i16(picks, docs), i16(picks, docs),
            b16(docs, width), f32(docs, width), f32(docs, width), b16(held, slot_count),
            b16(owners, cap, width), b16(owners, cap, width),
            b16(owners, 16, cap), b16(owners, 16, cap), i32(owners, 1, cap),
            i16(slot_count, docs), b16(slot_count, docs),
            b16(owners, cap, width), b16(owners, cap, width),
            f32(nz, ny, depth, width), b16(nz, ny, depth, width),
            b16(ny - 1, nz, depth, wide), b16(nz - 1, ny, depth, slim),
            f32(nz, depth, wide), f32(ny, depth, slim),
            f32(nz - 1, depth, wide), f32(ny - 1, depth, slim),
            b16(docs, width), f32(2, half, width), f32(half, width),
            b16(plane, piece, width), b16(nz, piece, width),
            b16(plane - 1, piece, width), b16(nz - 1, piece, width),
            f32(nz, piece, width), f32(plane, piece, width),
            pltpu.SemaphoreType.DMA((5,)), *dma(owners), *dma(owners), *dma(owners), *dma(owners),
            *dma(ny - 1), *dma(nz - 1), *dma(nz - 1), *dma(ny - 1),
            pltpu.SemaphoreType.DMA, pltpu.SemaphoreType.DMA,
            *dma(plane - 1), *dma(nz - 1), *dma(nz - 1), *dma(plane - 1), *dma(plane - 1), *dma(nz - 1),
            *dma(plane + nz),
        ],
        compiler_params=pltpu.CompilerParams(
            collective_id=1, has_side_effects=True, vmem_limit_bytes=56 * 2**20
        ),
        cost_estimate=pl.CostEstimate(flops=10**10, bytes_accessed=10**7, transcendentals=2 * 10**6),
        name="classifier_step",
    )(
        documents,
        enc_weight,
        label_slab,
        row_scale,
        request_ids.reshape(owners, 1, cap),
        shortlist.T,
        positive.T,
        counts,
    )
    return settle(slab_grad, enc_grad.reshape(width, width))


def solution(mesh):
    return jax.shard_map(
        functools.partial(body, torus(mesh)),
        mesh=mesh,
        in_specs=(
            P(("owner", "dp"), None),
            P(),
            P("owner", None),
            P("owner"),
            P(("owner", "dp"), None),
            P(("owner", "dp"), None),
            P(("owner", "dp"), None),
            P(("owner", "dp"), None),
        ),
        out_specs=(P(("owner", "dp"), None), P()),
        check_vma=False,
    )
```

```python
import functools

import jax
import jax.numpy as jnp
from jax import lax
from jax.experimental import pallas as pl
from jax.experimental.pallas import tpu as pltpu
from jax.sharding import PartitionSpec as P

MESH = pl.DeviceIdType.MESH
F32 = jnp.float32
BF16 = jnp.bfloat16
I32 = jnp.int32
I16 = jnp.int16


def torus(mesh):
    owners, groups = mesh.shape["owner"], mesh.shape["dp"]
    ny = 4 if groups >= 16 else 2
    return owners // 2, ny, groups // ny


def remote(src, dst, send, recv, target):
    return pltpu.make_async_remote_copy(
        src_ref=src, dst_ref=dst, send_sem=send, recv_sem=recv, device_id=target, device_id_type=MESH
    )


def step_kernel(
    dims, docs_in, weight_in, slab_in, scale, ids, slots_in, on_in, counts, slab_out, enc_out,
    docs, weight, slab, slots32, on32, slots, marks, emb, slope, push, onehot, srows, frows, sscale, fscale, gids, tally, dscore, grads, back,
    own, ownb, gota, gotb, acca, accb, gota2, gotb2,
    inner, enc, sib, accp, accq, gotp, gotq, allp, allx, ally,
    s_in, s_id, r_id, s_f, r_f, s_c, r_c, s_g, r_g,
    s_a, r_a, s_b, r_b, s_a2, r_a2, s_b2, r_b2,
    s_sib, r_sib, s_p, r_p, s_q, r_q, s_p2, r_p2, s_x, r_x, s_y, r_y, s_p3, r_p3, s_q3, r_q3, s_e, r_e,
):
    nx, ny, nz = dims
    owner, group = lax.axis_index("owner"), lax.axis_index("dp")
    x, c = owner // 2, owner % 2
    y, z = group % ny, group // ny
    here = x * ny + y
    owners = 2 * nx
    cap = srows.shape[1]
    pair = 2 * cap
    documents, width = docs.shape
    rows_held = slab.shape[0]
    wide = gota.shape[-1]
    depth = gota.shape[-2]
    piece = accp.shape[1]
    half = enc.shape[1]
    cut = nx * ny * piece
    strip = min(128, documents)
    far = nx - 1

    plane = [(i, j) for i in range(nx) for j in range(ny) if (i, j) != (0, 0)]
    rings = list(range(1, nz))
    cols = list(range(1, ny))

    def chip(i, j, k, core):
        return {"owner": lax.rem(x + i, nx) * 2 + core, "dp": lax.rem(z + k, nz) * ny + lax.rem(y + j, ny)}

    def spread(r):
        return r + (r // 2) * (5 - 2 * r) if nx == 4 else r

    loads = [
        pltpu.make_async_copy(src, dst, s_in.at[n])
        for n, (src, dst) in enumerate(
            ((docs_in, docs), (weight_in, weight), (slab_in, slab), (slots_in, slots32), (on_in, on32))
        )
    ]
    for load in loads:
        load.start()

    bar = pltpu.get_barrier_semaphore()
    greeted = 0
    for i, j in plane:
        pl.semaphore_signal(bar, inc=1, device_id=chip(i, j, 0, c), device_id_type=MESH)
        greeted += 1
    for i in range(nx):
        pl.semaphore_signal(bar, inc=1, device_id=chip(i, 0, 0, 1 - c), device_id_type=MESH)
        greeted += 1
    for k in rings:
        pl.semaphore_signal(bar, inc=1, device_id=chip(0, 0, k, c), device_id_type=MESH)
        greeted += 1
    pl.semaphore_wait(bar, greeted)

    def peer(n):
        r, flip = n // 2, n % 2
        core = lax.rem(c + flip, 2)
        to = lax.rem(x + spread(r), nx) * 2 + core
        source = lax.rem(x + nx - spread(r), nx) * 2 + core
        return to, source

    def id_copy(n):
        to, _ = peer(n)
        return remote(ids.at[to], gids.at[owner], s_id.at[n], r_id.at[n], {"owner": to, "dp": group})

    for n in range(1, owners):
        id_copy(n).start()
    gids[owner] = ids[owner]

    loads[0].wait()
    loads[1].wait()
    squashed = jnp.tanh(jnp.dot(docs[...], weight[...], preferred_element_type=F32))
    emb[...] = (docs[...].astype(F32) + squashed).astype(BF16)
    slope[...] = 1.0 - squashed * squashed
    loads[2].wait()

    def row_copy(n):
        to, _ = peer(n)
        return remote(srows.at[to], frows.at[owner], s_f.at[n], r_f.at[n], {"owner": to, "dp": group})

    def scale_copy(n):
        to, _ = peer(n)
        return remote(sscale.at[to], fscale.at[owner], s_c.at[n], r_c.at[n], {"owner": to, "dp": group})

    scale_rows = jnp.broadcast_to(scale[...].reshape(1, rows_held), (16, rows_held))

    def serve(m, _):
        n = lax.rem(m + 2, owners)
        to, _source = peer(n)

        @pl.when(n > 0)
        def _():
            id_copy(n).wait_send()

        hot = jnp.where(
            lax.broadcasted_iota(I32, (rows_held, cap), 0) == gids[to], 1.0, 0.0
        ).astype(BF16)
        onehot[:, pl.ds(pl.multiple_of(to * cap, cap), cap)] = hot
        rows = lax.dot_general(hot, slab[...], (((0,), (0,)), ((), ())), preferred_element_type=F32).astype(BF16)
        sc = jnp.dot(scale_rows, hot, preferred_element_type=F32).astype(BF16)
        srows[to] = rows
        sscale[to] = sc

        @pl.when(n == 0)
        def _():
            frows[owner] = rows
            fscale[owner] = sc

        @pl.when(n > 0)
        def _():
            row_copy(n).start()
            scale_copy(n).start()

        return 0

    for n in range(1, owners):
        id_copy(n).wait_recv()
    lax.fori_loop(0, owners, serve, 0)

    def grad_copy(n):
        _, source = peer(n)
        return remote(grads.at[source], back.at[owner], s_g.at[n], r_g.at[n], {"owner": source, "dp": group})

    loads[3].wait()
    loads[4].wait()
    slots[...] = slots32[...].astype(I16)
    marks[...] = (1 + 64 * on32[...]).astype(I16)
    strips = documents // strip

    def count(m, _):
        base = pl.multiple_of((m // strips) * pair, pair)
        lanes = pl.ds(pl.multiple_of((m % strips) * strip, strip), strip)
        index = (lax.broadcasted_iota(I32, (pair, strip), 0) + base).astype(I16)
        total = jnp.zeros((pair, strip), I16)
        for k in range(slots.shape[0]):
            total += jnp.where(slots[k : k + 1, lanes] == index, marks[k : k + 1, lanes], jnp.int16(0))
        tally[pl.ds(base, pair), lanes] = total
        return 0

    lax.fori_loop(0, nx * strips, count, 0)

    def group_of(r):
        first = lax.rem(x + nx - spread(r), nx) * 2
        return first, pl.ds(pl.multiple_of(first * cap, pair), pair)

    def score(r):
        first, span = group_of(r)
        rows = frows[pl.ds(first, 2)].reshape(pair, width)
        factor, live = [], []
        for q in range(2):
            line = fscale[first + q].astype(F32)[0:1]
            factor.append(jnp.broadcast_to(line, (cap, cap)).T[:, 0:1])
            live.append(jnp.where(lax.broadcasted_iota(I32, (cap, 1), 0) < counts[0, first + q], 1.0, 0.0))
        factor = jnp.concatenate(factor, axis=0)
        live = jnp.concatenate(live, axis=0)
        logits = lax.dot_general(rows, emb[...], (((1,), (1,)), ((), ())), preferred_element_type=F32) * factor
        chance = 0.5 * jnp.tanh(0.5 * logits) + 0.5
        mark = tally[span, :].astype(I32)
        hits = (mark & 63).astype(F32)
        on = (mark >> 6).astype(F32)
        dlogit = ((hits + live) * chance - on) * (1.0 / slots.shape[0])
        dscore[span, :] = (dlogit * factor).astype(BF16)

    def row_grads(r):
        first, span = group_of(r)
        grads[pl.ds(first, 2)] = (
            jnp.dot(dscore[span, :], emb[...], preferred_element_type=F32).astype(BF16).reshape(2, cap, width)
        )

    def pulled(r):
        first, span = group_of(r)
        rows = frows[pl.ds(first, 2)].reshape(pair, width)
        return lax.dot_general(dscore[span, :], rows, (((0,), (0,)), ((), ())), preferred_element_type=F32)

    def arrived(n):
        row_copy(n).wait()
        scale_copy(n).wait()

    push[...] = jnp.zeros_like(push)

    def work(r, _):
        @pl.when(r > 0)
        def _():
            arrived(2 * r)

        arrived(2 * r + 1)
        score(r)
        row_grads(r)

        @pl.when(r > 0)
        def _():
            grad_copy(2 * r).start()

        grad_copy(2 * r + 1).start()
        push[...] += pulled(r)
        return 0

    lax.fori_loop(0, far, work, 0)
    back[owner] = grads[owner]
    arrived(2 * far)
    arrived(2 * far + 1)
    score(far)

    inner[...] = ((push[...] + pulled(far)) * slope[...]).astype(BF16)

    def outer(which):
        side = docs[:, pl.ds(pl.multiple_of(which * half, half), half)]
        enc[which] = lax.dot_general(side, inner[...], (((0,), (0,)), ((), ())), preferred_element_type=F32)

    outer(1 - c)
    swap = remote(enc.at[1 - c], sib, s_sib, r_sib, chip(0, 0, 0, 1 - c))
    swap.start()
    outer(c)
    row_grads(far)
    grad_copy(2 * far).start()
    grad_copy(2 * far + 1).start()
    swap.wait()

    def join_p(q, _):
        rows = pl.ds(pl.multiple_of(q * piece, piece), piece)
        accp[q] = (enc[c, rows, :] + sib[rows, :]).astype(BF16)
        return 0

    def join_q(q, _):
        rows = pl.ds(pl.multiple_of(cut + q * piece, piece), piece)
        accq[q] = (enc[c, rows, :] + sib[rows, :]).astype(BF16)
        return 0

    lax.fori_loop(0, nx * ny, join_p, 0)
    lax.fori_loop(0, nz, join_q, 0)
    p1, q1 = [], []
    for n, (i, j) in enumerate(plane):
        to = lax.rem(x + i, nx) * ny + lax.rem(y + j, ny)
        p1.append(remote(accp.at[to], gotp.at[n], s_p.at[n], r_p.at[n], chip(i, j, 0, c)))
    for k in rings:
        to = lax.rem(z + k, nz)
        q1.append(remote(accq.at[to], gotq.at[k - 1], s_q.at[k - 1], r_q.at[k - 1], chip(0, 0, k, c)))
    for copy in p1 + q1:
        copy.start()

    for n in range(1, owners):
        grad_copy(n).wait()
    total = jnp.dot(onehot[...], back[...].reshape(owners * cap, width), preferred_element_type=F32)
    own[...] = total.reshape(own.shape)
    ownb[...] = total.astype(BF16).reshape(ownb.shape)
    first_a, first_b, second_a, second_b = [], [], [], []
    for j in cols:
        py = lax.rem(y + j, ny)
        first_a.append(remote(ownb.at[:, py, :, 0:wide], gota.at[j - 1], s_a.at[j - 1], r_a.at[j - 1],
                              chip(0, j, 0, c)))
    for k in rings:
        pz = lax.rem(z + k, nz)
        first_b.append(remote(ownb.at[pz, :, :, wide:], gotb.at[k - 1], s_b.at[k - 1], r_b.at[k - 1],
                              chip(0, 0, k, c)))
    for copy in first_a + first_b:
        copy.start()

    for copy in p1:
        copy.wait()
    rows = pl.ds(pl.multiple_of(here * piece, piece), piece)
    total = enc[c, rows, :] + sib[rows, :]
    for n in range(len(plane)):
        total += gotp[n].astype(F32)
    allp[z] = total
    p2, q2 = [], []
    for k in rings:
        p2.append(remote(allp.at[z], allp.at[z], s_p2.at[k - 1], r_p2.at[k - 1], chip(0, 0, k, c)))
    for copy in p2:
        copy.start()
    for copy in q1:
        copy.wait()
    rows = pl.ds(pl.multiple_of(cut + z * piece, piece), piece)
    total = enc[c, rows, :] + sib[rows, :]
    for k in rings:
        total += gotq[k - 1].astype(F32)
    allx[x] = total
    for i in range(1, nx):
        q2.append(remote(allx.at[x], allx.at[x], s_x.at[i - 1], r_x.at[i - 1], chip(i, 0, 0, c)))
    for copy in q2:
        copy.start()

    for copy in first_a:
        copy.wait()

    def join_a(q, _):
        total = own[q, y, :, 0:wide]
        for j in cols:
            total += gota[j - 1, q].astype(F32)
        acca[q] = total
        return 0

    lax.fori_loop(0, nz, join_a, 0)
    for k in rings:
        pz = lax.rem(z + k, nz)
        second_a.append(remote(acca.at[pz], gota2.at[k - 1], s_a2.at[k - 1], r_a2.at[k - 1], chip(0, 0, k, c)))
    for copy in second_a:
        copy.start()
    for copy in first_b:
        copy.wait()

    def join_b(q, _):
        total = own[z, q, :, wide:]
        for k in rings:
            total += gotb[k - 1, q].astype(F32)
        accb[q] = total
        return 0

    lax.fori_loop(0, ny, join_b, 0)
    for j in cols:
        py = lax.rem(y + j, ny)
        second_b.append(remote(accb.at[py], gotb2.at[j - 1], s_b2.at[j - 1], r_b2.at[j - 1], chip(0, j, 0, c)))
    for copy in second_b:
        copy.start()

    for copy in q2:
        copy.wait()
    total = allx[0]
    for i in range(1, nx):
        total += allx[i]
    ally[y] = total
    q2 = []
    for j in cols:
        q2.append(remote(ally.at[y], ally.at[y], s_y.at[j - 1], r_y.at[j - 1], chip(0, j, 0, c)))
    for copy in q2:
        copy.start()

    p3, q3 = [], []
    for copy in p2:
        copy.wait()
    total = allp[0]
    for k in range(1, nz):
        total += allp[k]
    rows_p = pl.ds(pl.multiple_of(here * piece, piece), piece)
    enc_out[c, rows_p, :] = total
    for n, (i, j) in enumerate(plane):
        part = enc_out.at[c, rows_p, :]
        p3.append(remote(part, part, s_p3.at[n], r_p3.at[n], chip(i, j, 0, c)))
    for copy in p3:
        copy.start()
    for copy in q2:
        copy.wait()
    total = ally[0]
    for j in cols:
        total += ally[j]
    rows_q = pl.ds(pl.multiple_of(cut + z * piece, piece), piece)
    enc_out[c, rows_q, :] = total
    for k in rings:
        part = enc_out.at[c, rows_q, :]
        q3.append(remote(part, part, s_q3.at[k - 1], r_q3.at[k - 1], chip(0, 0, k, c)))
    for copy in q3:
        copy.start()

    def pass_on(first, n):
        part = enc_out.at[c, pl.ds(pl.multiple_of(first, piece), piece), :]
        copy = remote(part, part, s_e.at[n], r_e.at[n], chip(0, 0, 0, 1 - c))
        copy.start()
        return copy

    handed = [pass_on(here * piece, 0), pass_on(cut + z * piece, 1)]
    for k in rings:
        q3[k - 1].wait()
        handed.append(pass_on(cut + lax.rem(z + nz - k, nz) * piece, 1 + k))
    for n, (i, j) in enumerate(plane):
        p3[n].wait()
        source = lax.rem(x + nx - i, nx) * ny + lax.rem(y + ny - j, ny)
        handed.append(pass_on(source * piece, nz + 1 + n))

    for copy in second_a:
        copy.wait()
    total = acca[z]
    for k in rings:
        total += gota2[k - 1]
    slab_out[:, 0:wide] = total
    for copy in second_b:
        copy.wait()
    total = accb[y]
    for j in cols:
        total += gotb2[j - 1]
    slab_out[:, wide:] = total
    for copy in handed:
        copy.wait()


def settle_kernel(slab, enc, slab_out, enc_out, sems):
    rows = enc.shape[0] // 4
    copies = [pltpu.make_async_copy(slab, slab_out, sems.at[4])]
    for n in range(4):
        part = pl.ds(n * rows, rows)
        copies.append(pltpu.make_async_copy(enc.at[part], enc_out.at[part], sems.at[n]))
    for copy in copies:
        copy.start()
    for copy in copies:
        copy.wait()


def settle(slab, enc):
    anywhere = pl.BlockSpec(memory_space=pl.ANY)
    return pl.pallas_call(
        settle_kernel,
        out_shape=(jax.ShapeDtypeStruct(slab.shape, F32), jax.ShapeDtypeStruct(enc.shape, F32)),
        in_specs=[pl.BlockSpec(memory_space=pltpu.VMEM)] * 2,
        out_specs=[anywhere] * 2,
        scratch_shapes=[pltpu.SemaphoreType.DMA((5,))],
        name="settle",
    )(slab, enc)


def body(dims, documents, enc_weight, label_slab, row_scale, shortlist, positive, request_ids, counts):
    nx, ny, nz = dims
    docs, width = documents.shape
    held = label_slab.shape[0]
    owners, cap = request_ids.shape
    picks = shortlist.shape[1]
    plane = nx * ny
    depth = held // (ny * nz)
    wide = 2 * width // 3
    slim = width - wide
    half = width // 2
    piece = half // (plane + nz)
    slot_count = owners * cap
    f32 = lambda *shape: pltpu.VMEM(shape, F32)
    b16 = lambda *shape: pltpu.VMEM(shape, BF16)
    i32 = lambda *shape: pltpu.VMEM(shape, I32)
    i16 = lambda *shape: pltpu.VMEM(shape, I16)
    dma = lambda n: [pltpu.SemaphoreType.DMA((n,))] * 2
    vmem = pl.BlockSpec(memory_space=pltpu.VMEM)
    anywhere = pl.BlockSpec(memory_space=pl.ANY)
    slab_grad, enc_grad = pl.pallas_call(
        functools.partial(step_kernel, dims),
        out_shape=(jax.ShapeDtypeStruct((depth, width), F32), jax.ShapeDtypeStruct((2, half, width), F32)),
        in_specs=[anywhere] * 3 + [vmem] * 2 + [anywhere] * 2 + [pl.BlockSpec(memory_space=pltpu.SMEM)],
        out_specs=[vmem] * 2,
        scratch_shapes=[
            b16(docs, width), b16(width, width), b16(held, width), i32(picks, docs), i32(picks, docs),
            i16(picks, docs), i16(picks, docs),
            b16(docs, width), f32(docs, width), f32(docs, width), b16(held, slot_count),
            b16(owners, cap, width), b16(owners, cap, width),
            b16(owners, 16, cap), b16(owners, 16, cap), i32(owners, 1, cap),
            i16(slot_count, docs), b16(slot_count, docs),
            b16(owners, cap, width), b16(owners, cap, width),
            f32(nz, ny, depth, width), b16(nz, ny, depth, width),
            b16(ny - 1, nz, depth, wide), b16(nz - 1, ny, depth, slim),
            f32(nz, depth, wide), f32(ny, depth, slim),
            f32(nz - 1, depth, wide), f32(ny - 1, depth, slim),
            b16(docs, width), f32(2, half, width), f32(half, width),
            b16(plane, piece, width), b16(nz, piece, width),
            b16(plane - 1, piece, width), b16(nz - 1, piece, width),
            f32(nz, piece, width), f32(nx, piece, width), f32(ny, piece, width),
            pltpu.SemaphoreType.DMA((5,)), *dma(owners), *dma(owners), *dma(owners), *dma(owners),
            *dma(ny - 1), *dma(nz - 1), *dma(nz - 1), *dma(ny - 1),
            pltpu.SemaphoreType.DMA, pltpu.SemaphoreType.DMA,
            *dma(plane - 1), *dma(nz - 1), *dma(nz - 1), *dma(nx - 1), *dma(ny - 1), *dma(plane - 1), *dma(nz - 1),
            *dma(plane + nz),
        ],
        compiler_params=pltpu.CompilerParams(
            collective_id=1, has_side_effects=True, vmem_limit_bytes=56 * 2**20
        ),
        cost_estimate=pl.CostEstimate(flops=10**10, bytes_accessed=10**7, transcendentals=2 * 10**6),
        name="classifier_step",
    )(
        documents,
        enc_weight,
        label_slab,
        row_scale,
        request_ids.reshape(owners, 1, cap),
        shortlist.T,
        positive.T,
        counts,
    )
    return settle(slab_grad, enc_grad.reshape(width, width))


def solution(mesh):
    return jax.shard_map(
        functools.partial(body, torus(mesh)),
        mesh=mesh,
        in_specs=(
            P(("owner", "dp"), None),
            P(),
            P("owner", None),
            P("owner"),
            P(("owner", "dp"), None),
            P(("owner", "dp"), None),
            P(("owner", "dp"), None),
            P(("owner", "dp"), None),
        ),
        out_specs=(P(("owner", "dp"), None), P()),
        check_vma=False,
    )
```

```python
import functools

import jax
import jax.numpy as jnp
from jax import lax
from jax.experimental import pallas as pl
from jax.experimental.pallas import tpu as pltpu
from jax.sharding import PartitionSpec as P

MESH = pl.DeviceIdType.MESH
F32 = jnp.float32
BF16 = jnp.bfloat16
I32 = jnp.int32
I16 = jnp.int16


def torus(mesh):
    owners, groups = mesh.shape["owner"], mesh.shape["dp"]
    ny = 4 if groups >= 16 else 2
    return owners // 2, ny, groups // ny


def remote(src, dst, send, recv, target):
    return pltpu.make_async_remote_copy(
        src_ref=src, dst_ref=dst, send_sem=send, recv_sem=recv, device_id=target, device_id_type=MESH
    )


def step_kernel(
    dims, docs_in, weight_in, slab_in, scale, ids, slots_in, on_in, counts, slab_out, enc_out,
    docs, weight, slab, slots32, on32, slots, marks, emb, slope, push, onehot, srows, frows, sscale, fscale, gids, tally, dscore, grads, back,
    own, ownb, gota, gotb, acca, accb, gota2, gotb2,
    inner, enc, sib, accp, accq, gotp, gotq, allp, allx, ally,
    s_in, s_id, r_id, s_f, r_f, s_c, r_c, s_g, r_g,
    s_a, r_a, s_b, r_b, s_a2, r_a2, s_b2, r_b2,
    s_sib, r_sib, s_p, r_p, s_q, r_q, s_p2, r_p2, s_x, r_x, s_y, r_y, s_p3, r_p3, s_q3, r_q3, s_e, r_e,
):
    nx, ny, nz = dims
    owner, group = lax.axis_index("owner"), lax.axis_index("dp")
    x, c = owner // 2, owner % 2
    y, z = group % ny, group // ny
    here = x * ny + y
    owners = 2 * nx
    cap = srows.shape[1]
    pair = 2 * cap
    documents, width = docs.shape
    rows_held = slab.shape[0]
    wide = gota.shape[-1]
    depth = gota.shape[-2]
    piece = accp.shape[2]
    half = enc.shape[1]
    cut = nx * ny * piece
    strip = min(128, documents)
    far = nx - 1

    plane = [(i, j) for i in range(nx) for j in range(ny) if (i, j) != (0, 0)]
    rings = list(range(1, nz))
    cols = list(range(1, ny))

    def chip(i, j, k, core):
        return {"owner": lax.rem(x + i, nx) * 2 + core, "dp": lax.rem(z + k, nz) * ny + lax.rem(y + j, ny)}

    def spread(r):
        return r + (r // 2) * (5 - 2 * r) if nx == 4 else r

    loads = [
        pltpu.make_async_copy(src, dst, s_in.at[n])
        for n, (src, dst) in enumerate(
            ((docs_in, docs), (weight_in, weight), (slab_in, slab), (slots_in, slots32), (on_in, on32))
        )
    ]
    for load in loads:
        load.start()

    bar = pltpu.get_barrier_semaphore()
    greeted = 0
    for i, j in plane:
        pl.semaphore_signal(bar, inc=1, device_id=chip(i, j, 0, c), device_id_type=MESH)
        greeted += 1
    for i in range(nx):
        pl.semaphore_signal(bar, inc=1, device_id=chip(i, 0, 0, 1 - c), device_id_type=MESH)
        greeted += 1
    for k in rings:
        pl.semaphore_signal(bar, inc=1, device_id=chip(0, 0, k, c), device_id_type=MESH)
        greeted += 1
    pl.semaphore_wait(bar, greeted)

    def peer(n):
        r, flip = n // 2, n % 2
        core = lax.rem(c + flip, 2)
        to = lax.rem(x + spread(r), nx) * 2 + core
        source = lax.rem(x + nx - spread(r), nx) * 2 + core
        return to, source

    def id_copy(n):
        to, _ = peer(n)
        return remote(ids.at[to], gids.at[owner], s_id.at[n], r_id.at[n], {"owner": to, "dp": group})

    for n in range(1, owners):
        id_copy(n).start()
    gids[owner] = ids[owner]

    loads[0].wait()
    loads[1].wait()
    squashed = jnp.tanh(jnp.dot(docs[...], weight[...], preferred_element_type=F32))
    emb[...] = (docs[...].astype(F32) + squashed).astype(BF16)
    slope[...] = 1.0 - squashed * squashed
    loads[2].wait()

    def row_copy(n):
        to, _ = peer(n)
        return remote(srows.at[to], frows.at[owner], s_f.at[n], r_f.at[n], {"owner": to, "dp": group})

    def scale_copy(n):
        to, _ = peer(n)
        return remote(sscale.at[to], fscale.at[owner], s_c.at[n], r_c.at[n], {"owner": to, "dp": group})

    scale_rows = jnp.broadcast_to(scale[...].reshape(1, rows_held), (16, rows_held))

    def serve(m, _):
        n = lax.rem(m + 2, owners)
        to, _source = peer(n)

        @pl.when(n > 0)
        def _():
            id_copy(n).wait_send()

        hot = jnp.where(
            lax.broadcasted_iota(I32, (rows_held, cap), 0) == gids[to], 1.0, 0.0
        ).astype(BF16)
        onehot[:, pl.ds(pl.multiple_of(to * cap, cap), cap)] = hot
        rows = lax.dot_general(hot, slab[...], (((0,), (0,)), ((), ())), preferred_element_type=F32).astype(BF16)
        sc = jnp.dot(scale_rows, hot, preferred_element_type=F32).astype(BF16)
        srows[to] = rows
        sscale[to] = sc

        @pl.when(n == 0)
        def _():
            frows[owner] = rows
            fscale[owner] = sc

        @pl.when(n > 0)
        def _():
            row_copy(n).start()
            scale_copy(n).start()

        return 0

    for n in range(1, owners):
        id_copy(n).wait_recv()
    lax.fori_loop(0, owners, serve, 0)

    def grad_copy(n):
        _, source = peer(n)
        return remote(grads.at[source], back.at[owner], s_g.at[n], r_g.at[n], {"owner": source, "dp": group})

    loads[3].wait()
    loads[4].wait()
    slots[...] = slots32[...].astype(I16)
    marks[...] = (1 + 64 * on32[...]).astype(I16)
    strips = documents // strip

    def count(m, _):
        base = pl.multiple_of((m // strips) * pair, pair)
        lanes = pl.ds(pl.multiple_of((m % strips) * strip, strip), strip)
        index = (lax.broadcasted_iota(I32, (pair, strip), 0) + base).astype(I16)
        total = jnp.zeros((pair, strip), I16)
        for k in range(slots.shape[0]):
            total += jnp.where(slots[k : k + 1, lanes] == index, marks[k : k + 1, lanes], jnp.int16(0))
        tally[pl.ds(base, pair), lanes] = total
        return 0

    lax.fori_loop(0, nx * strips, count, 0)

    def group_of(r):
        first = lax.rem(x + nx - spread(r), nx) * 2
        return first, pl.ds(pl.multiple_of(first * cap, pair), pair)

    def score(r):
        first, span = group_of(r)
        rows = frows[pl.ds(first, 2)].reshape(pair, width)
        factor, live = [], []
        for q in range(2):
            line = fscale[first + q].astype(F32)[0:1]
            factor.append(jnp.broadcast_to(line, (cap, cap)).T[:, 0:1])
            live.append(jnp.where(lax.broadcasted_iota(I32, (cap, 1), 0) < counts[0, first + q], 1.0, 0.0))
        factor = jnp.concatenate(factor, axis=0)
        live = jnp.concatenate(live, axis=0)
        logits = lax.dot_general(rows, emb[...], (((1,), (1,)), ((), ())), preferred_element_type=F32) * factor
        chance = 0.5 * jnp.tanh(0.5 * logits) + 0.5
        mark = tally[span, :].astype(I32)
        hits = (mark & 63).astype(F32)
        on = (mark >> 6).astype(F32)
        dlogit = ((hits + live) * chance - on) * (1.0 / slots.shape[0])
        dscore[span, :] = (dlogit * factor).astype(BF16)

    def row_grads(r):
        first, span = group_of(r)
        grads[pl.ds(first, 2)] = (
            jnp.dot(dscore[span, :], emb[...], preferred_element_type=F32).astype(BF16).reshape(2, cap, width)
        )

    def pulled(r):
        first, span = group_of(r)
        rows = frows[pl.ds(first, 2)].reshape(pair, width)
        return lax.dot_general(dscore[span, :], rows, (((0,), (0,)), ((), ())), preferred_element_type=F32)

    def arrived(n):
        row_copy(n).wait()
        scale_copy(n).wait()

    push[...] = jnp.zeros_like(push)

    def work(r, _):
        @pl.when(r > 0)
        def _():
            arrived(2 * r)

        arrived(2 * r + 1)
        score(r)
        row_grads(r)

        @pl.when(r > 0)
        def _():
            grad_copy(2 * r).start()

        grad_copy(2 * r + 1).start()
        push[...] += pulled(r)
        return 0

    lax.fori_loop(0, far, work, 0)
    back[owner] = grads[owner]
    arrived(2 * far)
    arrived(2 * far + 1)
    score(far)

    inner[...] = ((push[...] + pulled(far)) * slope[...]).astype(BF16)

    parts = range(2)
    part_width = width // 2

    def columns(h):
        return pl.ds(h * part_width, part_width)

    def outer(which, h):
        side = docs[:, pl.ds(pl.multiple_of(which * half, half), half)]
        enc[which, :, columns(h)] = lax.dot_general(
            side, inner[:, columns(h)], (((0,), (0,)), ((), ())), preferred_element_type=F32
        )

    swaps = [
        remote(enc.at[1 - c, :, columns(h)], sib.at[:, columns(h)], s_sib.at[h], r_sib.at[h], chip(0, 0, 0, 1 - c))
        for h in parts
    ]
    for h in parts:
        outer(1 - c, h)
        swaps[h].start()
    for h in parts:
        outer(c, h)
    row_grads(far)
    grad_copy(2 * far).start()
    grad_copy(2 * far + 1).start()

    def summed(first, h):
        rows = pl.ds(pl.multiple_of(first, piece), piece)
        return enc[c, rows, columns(h)] + sib[rows, columns(h)]

    p1, q1 = [[], []], [[], []]
    for h in parts:
        swaps[h].wait()

        def join_p(q, _):
            accp[h, q] = summed(q * piece, h).astype(BF16)
            return 0

        def join_q(q, _):
            accq[h, q] = summed(cut + q * piece, h).astype(BF16)
            return 0

        lax.fori_loop(0, nx * ny, join_p, 0)
        lax.fori_loop(0, nz, join_q, 0)
        for n, (i, j) in enumerate(plane):
            to = lax.rem(x + i, nx) * ny + lax.rem(y + j, ny)
            p1[h].append(remote(accp.at[h, to], gotp.at[h, n], s_p.at[h, n], r_p.at[h, n], chip(i, j, 0, c)))
        for k in rings:
            to = lax.rem(z + k, nz)
            q1[h].append(
                remote(accq.at[h, to], gotq.at[h, k - 1], s_q.at[h, k - 1], r_q.at[h, k - 1], chip(0, 0, k, c))
            )
        for copy in p1[h] + q1[h]:
            copy.start()

    p2, qx, qy = [[], []], [[], []], [[], []]
    for h in parts:
        for copy in p1[h]:
            copy.wait()
        total = summed(here * piece, h)
        for n in range(len(plane)):
            total += gotp[h, n].astype(F32)
        allp[h, z] = total
        for k in rings:
            p2[h].append(
                remote(allp.at[h, z], allp.at[h, z], s_p2.at[h, k - 1], r_p2.at[h, k - 1], chip(0, 0, k, c))
            )
        for copy in p2[h]:
            copy.start()
        for copy in q1[h]:
            copy.wait()
        total = summed(cut + z * piece, h)
        for k in rings:
            total += gotq[h, k - 1].astype(F32)
        allx[h, x] = total
        for i in range(1, nx):
            qx[h].append(remote(allx.at[h, x], allx.at[h, x], s_x.at[h, i - 1], r_x.at[h, i - 1], chip(i, 0, 0, c)))
        for copy in qx[h]:
            copy.start()

    for n in range(1, owners):
        grad_copy(n).wait()
    total = jnp.dot(onehot[...], back[...].reshape(owners * cap, width), preferred_element_type=F32)
    own[...] = total.reshape(own.shape)
    ownb[...] = total.astype(BF16).reshape(ownb.shape)

    def cols_a(h):
        return pl.ds(h * part_width, wide)

    def cols_b(h):
        return pl.ds(h * part_width + wide, part_width - wide)

    first_a, first_b, second_a, second_b = [[], []], [[], []], [[], []], [[], []]
    for h in parts:
        for j in cols:
            py = lax.rem(y + j, ny)
            first_a[h].append(remote(ownb.at[:, py, :, cols_a(h)], gota.at[h, j - 1], s_a.at[h, j - 1],
                                     r_a.at[h, j - 1], chip(0, j, 0, c)))
        for k in rings:
            pz = lax.rem(z + k, nz)
            first_b[h].append(remote(ownb.at[pz, :, :, cols_b(h)], gotb.at[h, k - 1], s_b.at[h, k - 1],
                                     r_b.at[h, k - 1], chip(0, 0, k, c)))
        for copy in first_a[h] + first_b[h]:
            copy.start()

    for h in parts:
        for copy in qx[h]:
            copy.wait()
        total = allx[h, 0]
        for i in range(1, nx):
            total += allx[h, i]
        ally[h, y] = total
        for j in cols:
            qy[h].append(remote(ally.at[h, y], ally.at[h, y], s_y.at[h, j - 1], r_y.at[h, j - 1], chip(0, j, 0, c)))
        for copy in qy[h]:
            copy.start()

    p3, q3 = [[], []], [[], []]
    rows_p = pl.ds(pl.multiple_of(here * piece, piece), piece)
    rows_q = pl.ds(pl.multiple_of(cut + z * piece, piece), piece)
    for h in parts:
        for copy in p2[h]:
            copy.wait()
        total = allp[h, 0]
        for k in range(1, nz):
            total += allp[h, k]
        enc_out[c, rows_p, columns(h)] = total
        part = enc_out.at[c, rows_p, columns(h)]
        for n, (i, j) in enumerate(plane):
            p3[h].append(remote(part, part, s_p3.at[h, n], r_p3.at[h, n], chip(i, j, 0, c)))
        for copy in p3[h]:
            copy.start()
        for copy in qy[h]:
            copy.wait()
        total = ally[h, 0]
        for j in cols:
            total += ally[h, j]
        enc_out[c, rows_q, columns(h)] = total
        part = enc_out.at[c, rows_q, columns(h)]
        for k in rings:
            q3[h].append(remote(part, part, s_q3.at[h, k - 1], r_q3.at[h, k - 1], chip(0, 0, k, c)))
        for copy in q3[h]:
            copy.start()

    for h in parts:
        for copy in first_a[h]:
            copy.wait()

        def join_a(q, _):
            total = own[q, y, :, cols_a(h)]
            for j in cols:
                total += gota[h, j - 1, q].astype(F32)
            acca[h, q] = total
            return 0

        lax.fori_loop(0, nz, join_a, 0)
        for k in rings:
            pz = lax.rem(z + k, nz)
            second_a[h].append(remote(acca.at[h, pz], gota2.at[h, k - 1], s_a2.at[h, k - 1], r_a2.at[h, k - 1],
                                      chip(0, 0, k, c)))
        for copy in second_a[h]:
            copy.start()
        for copy in first_b[h]:
            copy.wait()

        def join_b(q, _):
            total = own[z, q, :, cols_b(h)]
            for k in rings:
                total += gotb[h, k - 1, q].astype(F32)
            accb[h, q] = total
            return 0

        lax.fori_loop(0, ny, join_b, 0)
        for j in cols:
            py = lax.rem(y + j, ny)
            second_b[h].append(remote(accb.at[h, py], gotb2.at[h, j - 1], s_b2.at[h, j - 1], r_b2.at[h, j - 1],
                                      chip(0, j, 0, c)))
        for copy in second_b[h]:
            copy.start()

    handed = []

    def pass_on(first, h, n):
        part = enc_out.at[c, pl.ds(pl.multiple_of(first, piece), piece), columns(h)]
        copy = remote(part, part, s_e.at[h, n], r_e.at[h, n], chip(0, 0, 0, 1 - c))
        copy.start()
        handed.append(copy)

    for h in parts:
        pass_on(here * piece, h, 0)
        pass_on(cut + z * piece, h, 1)
        for k in rings:
            q3[h][k - 1].wait()
            pass_on(cut + lax.rem(z + nz - k, nz) * piece, h, 1 + k)
        for n, (i, j) in enumerate(plane):
            p3[h][n].wait()
            source = lax.rem(x + nx - i, nx) * ny + lax.rem(y + ny - j, ny)
            pass_on(source * piece, h, nz + 1 + n)

    for h in parts:
        for copy in second_a[h]:
            copy.wait()
        total = acca[h, z]
        for k in rings:
            total += gota2[h, k - 1]
        slab_out[:, cols_a(h)] = total
        for copy in second_b[h]:
            copy.wait()
        total = accb[h, y]
        for j in cols:
            total += gotb2[h, j - 1]
        slab_out[:, cols_b(h)] = total
    for copy in handed:
        copy.wait()


def settle_kernel(slab, enc, slab_out, enc_out, sems):
    rows = enc.shape[0] // 4
    copies = [pltpu.make_async_copy(slab, slab_out, sems.at[4])]
    for n in range(4):
        part = pl.ds(n * rows, rows)
        copies.append(pltpu.make_async_copy(enc.at[part], enc_out.at[part], sems.at[n]))
    for copy in copies:
        copy.start()
    for copy in copies:
        copy.wait()


def settle(slab, enc):
    anywhere = pl.BlockSpec(memory_space=pl.ANY)
    return pl.pallas_call(
        settle_kernel,
        out_shape=(jax.ShapeDtypeStruct(slab.shape, F32), jax.ShapeDtypeStruct(enc.shape, F32)),
        in_specs=[pl.BlockSpec(memory_space=pltpu.VMEM)] * 2,
        out_specs=[anywhere] * 2,
        scratch_shapes=[pltpu.SemaphoreType.DMA((5,))],
        name="settle",
    )(slab, enc)


def body(dims, documents, enc_weight, label_slab, row_scale, shortlist, positive, request_ids, counts):
    nx, ny, nz = dims
    docs, width = documents.shape
    held = label_slab.shape[0]
    owners, cap = request_ids.shape
    picks = shortlist.shape[1]
    plane = nx * ny
    depth = held // (ny * nz)
    part = width // 2
    wide = 2 * part // 3
    slim = part - wide
    half = width // 2
    piece = half // (plane + nz)
    slot_count = owners * cap
    f32 = lambda *shape: pltpu.VMEM(shape, F32)
    b16 = lambda *shape: pltpu.VMEM(shape, BF16)
    i32 = lambda *shape: pltpu.VMEM(shape, I32)
    i16 = lambda *shape: pltpu.VMEM(shape, I16)
    dma = lambda n: [pltpu.SemaphoreType.DMA((n,))] * 2
    two = lambda n: [pltpu.SemaphoreType.DMA((2, n))] * 2
    vmem = pl.BlockSpec(memory_space=pltpu.VMEM)
    anywhere = pl.BlockSpec(memory_space=pl.ANY)
    slab_grad, enc_grad = pl.pallas_call(
        functools.partial(step_kernel, dims),
        out_shape=(jax.ShapeDtypeStruct((depth, width), F32), jax.ShapeDtypeStruct((2, half, width), F32)),
        in_specs=[anywhere] * 3 + [vmem] * 2 + [anywhere] * 2 + [pl.BlockSpec(memory_space=pltpu.SMEM)],
        out_specs=[vmem] * 2,
        scratch_shapes=[
            b16(docs, width), b16(width, width), b16(held, width), i32(picks, docs), i32(picks, docs),
            i16(picks, docs), i16(picks, docs),
            b16(docs, width), f32(docs, width), f32(docs, width), b16(held, slot_count),
            b16(owners, cap, width), b16(owners, cap, width),
            b16(owners, 16, cap), b16(owners, 16, cap), i32(owners, 1, cap),
            i16(slot_count, docs), b16(slot_count, docs),
            b16(owners, cap, width), b16(owners, cap, width),
            f32(nz, ny, depth, width), b16(nz, ny, depth, width),
            b16(2, ny - 1, nz, depth, wide), b16(2, nz - 1, ny, depth, slim),
            f32(2, nz, depth, wide), f32(2, ny, depth, slim),
            f32(2, nz - 1, depth, wide), f32(2, ny - 1, depth, slim),
            b16(docs, width), f32(2, half, width), f32(half, width),
            b16(2, plane, piece, part), b16(2, nz, piece, part),
            b16(2, plane - 1, piece, part), b16(2, nz - 1, piece, part),
            f32(2, nz, piece, part), f32(2, nx, piece, part), f32(2, ny, piece, part),
            pltpu.SemaphoreType.DMA((5,)), *dma(owners), *dma(owners), *dma(owners), *dma(owners),
            *two(ny - 1), *two(nz - 1), *two(nz - 1), *two(ny - 1), *dma(2),
            *two(plane - 1), *two(nz - 1), *two(nz - 1), *two(nx - 1), *two(ny - 1), *two(plane - 1), *two(nz - 1),
            *two(plane + nz),
        ],
        compiler_params=pltpu.CompilerParams(
            collective_id=1, has_side_effects=True, vmem_limit_bytes=56 * 2**20
        ),
        cost_estimate=pl.CostEstimate(flops=10**10, bytes_accessed=10**7, transcendentals=2 * 10**6),
        name="classifier_step",
    )(
        documents,
        enc_weight,
        label_slab,
        row_scale,
        request_ids.reshape(owners, 1, cap),
        shortlist.T,
        positive.T,
        counts,
    )
    return settle(slab_grad, enc_grad.reshape(width, width))


def solution(mesh):
    return jax.shard_map(
        functools.partial(body, torus(mesh)),
        mesh=mesh,
        in_specs=(
            P(("owner", "dp"), None),
            P(),
            P("owner", None),
            P("owner"),
            P(("owner", "dp"), None),
            P(("owner", "dp"), None),
            P(("owner", "dp"), None),
            P(("owner", "dp"), None),
        ),
        out_specs=(P(("owner", "dp"), None), P()),
        check_vma=False,
    )
```

```python
import functools

import jax
import jax.numpy as jnp
from jax import lax
from jax.experimental import pallas as pl
from jax.experimental.pallas import tpu as pltpu
from jax.sharding import PartitionSpec as P

MESH = pl.DeviceIdType.MESH
F32 = jnp.float32
BF16 = jnp.bfloat16
I32 = jnp.int32
I16 = jnp.int16


def torus(mesh):
    owners, groups = mesh.shape["owner"], mesh.shape["dp"]
    ny = 4 if groups >= 16 else 2
    return owners // 2, ny, groups // ny


def remote(src, dst, send, recv, target):
    return pltpu.make_async_remote_copy(
        src_ref=src, dst_ref=dst, send_sem=send, recv_sem=recv, device_id=target, device_id_type=MESH
    )


def step_kernel(
    dims, docs_in, weight_in, slab_in, scale, ids, slots_in, on_in, counts, slab_out, enc_out,
    docs, weight, slab, slots32, on32, slots, marks, emb, slope, push, onehot, srows, frows, sscale, fscale, gids, tally, dscore, grads, back,
    own, ownb, gota, gotb, acca, accb, gota2, gotb2,
    inner, enc, sib, accp, accq, gotp, gotq, shares, gots, done, allx, ally,
    s_in, s_id, r_id, s_f, r_f, s_c, r_c, s_g, r_g,
    s_a, r_a, s_b, r_b, s_a2, r_a2, s_b2, r_b2,
    s_sib, r_sib, s_p, r_p, s_q, r_q, s_p2, r_p2, s_ag, r_ag, s_x, r_x, s_y, r_y, s_p3, r_p3, s_q3, r_q3, s_e, r_e,
):
    nx, ny, nz = dims
    owner, group = lax.axis_index("owner"), lax.axis_index("dp")
    x, c = owner // 2, owner % 2
    y, z = group % ny, group // ny
    here = x * ny + y
    owners = 2 * nx
    cap = srows.shape[1]
    pair = 2 * cap
    documents, width = docs.shape
    rows_held = slab.shape[0]
    wide = gota.shape[-1]
    depth = gota.shape[-2]
    piece = accp.shape[1]
    share = shares.shape[1]
    half = enc.shape[1]
    cut = nx * ny * piece
    strip = min(128, documents)
    far = nx - 1

    plane = [(i, j) for i in range(nx) for j in range(ny) if (i, j) != (0, 0)]
    rings = list(range(1, nz))
    cols = list(range(1, ny))

    def chip(i, j, k, core):
        return {"owner": lax.rem(x + i, nx) * 2 + core, "dp": lax.rem(z + k, nz) * ny + lax.rem(y + j, ny)}

    def spread(r):
        return r + (r // 2) * (5 - 2 * r) if nx == 4 else r

    loads = [
        pltpu.make_async_copy(src, dst, s_in.at[n])
        for n, (src, dst) in enumerate(
            ((docs_in, docs), (weight_in, weight), (slab_in, slab), (slots_in, slots32), (on_in, on32))
        )
    ]
    for load in loads:
        load.start()

    bar = pltpu.get_barrier_semaphore()
    greeted = 0
    for i, j in plane:
        pl.semaphore_signal(bar, inc=1, device_id=chip(i, j, 0, c), device_id_type=MESH)
        greeted += 1
    for i in range(nx):
        pl.semaphore_signal(bar, inc=1, device_id=chip(i, 0, 0, 1 - c), device_id_type=MESH)
        greeted += 1
    for k in rings:
        pl.semaphore_signal(bar, inc=1, device_id=chip(0, 0, k, c), device_id_type=MESH)
        greeted += 1
    pl.semaphore_wait(bar, greeted)

    def peer(n):
        r, flip = n // 2, n % 2
        core = lax.rem(c + flip, 2)
        to = lax.rem(x + spread(r), nx) * 2 + core
        source = lax.rem(x + nx - spread(r), nx) * 2 + core
        return to, source

    def id_copy(n):
        to, _ = peer(n)
        return remote(ids.at[to], gids.at[owner], s_id.at[n], r_id.at[n], {"owner": to, "dp": group})

    for n in range(1, owners):
        id_copy(n).start()
    gids[owner] = ids[owner]

    loads[0].wait()
    loads[1].wait()
    squashed = jnp.tanh(jnp.dot(docs[...], weight[...], preferred_element_type=F32))
    emb[...] = (docs[...].astype(F32) + squashed).astype(BF16)
    slope[...] = 1.0 - squashed * squashed
    loads[2].wait()

    def row_copy(n):
        to, _ = peer(n)
        return remote(srows.at[to], frows.at[owner], s_f.at[n], r_f.at[n], {"owner": to, "dp": group})

    def scale_copy(n):
        to, _ = peer(n)
        return remote(sscale.at[to], fscale.at[owner], s_c.at[n], r_c.at[n], {"owner": to, "dp": group})

    scale_rows = jnp.broadcast_to(scale[...].reshape(1, rows_held), (16, rows_held))

    def serve(m, _):
        n = lax.rem(m + 2, owners)
        to, _source = peer(n)

        @pl.when(n > 0)
        def _():
            id_copy(n).wait_send()

        hot = jnp.where(
            lax.broadcasted_iota(I32, (rows_held, cap), 0) == gids[to], 1.0, 0.0
        ).astype(BF16)
        onehot[:, pl.ds(pl.multiple_of(to * cap, cap), cap)] = hot
        rows = lax.dot_general(hot, slab[...], (((0,), (0,)), ((), ())), preferred_element_type=F32).astype(BF16)
        sc = jnp.dot(scale_rows, hot, preferred_element_type=F32).astype(BF16)
        srows[to] = rows
        sscale[to] = sc

        @pl.when(n == 0)
        def _():
            frows[owner] = rows
            fscale[owner] = sc

        @pl.when(n > 0)
        def _():
            row_copy(n).start()
            scale_copy(n).start()

        return 0

    for n in range(1, owners):
        id_copy(n).wait_recv()
    lax.fori_loop(0, owners, serve, 0)

    def grad_copy(n):
        _, source = peer(n)
        return remote(grads.at[source], back.at[owner], s_g.at[n], r_g.at[n], {"owner": source, "dp": group})

    loads[3].wait()
    loads[4].wait()
    slots[...] = slots32[...].astype(I16)
    marks[...] = (1 + 64 * on32[...]).astype(I16)
    strips = documents // strip

    def count(m, _):
        base = pl.multiple_of((m // strips) * pair, pair)
        lanes = pl.ds(pl.multiple_of((m % strips) * strip, strip), strip)
        index = (lax.broadcasted_iota(I32, (pair, strip), 0) + base).astype(I16)
        total = jnp.zeros((pair, strip), I16)
        for k in range(slots.shape[0]):
            total += jnp.where(slots[k : k + 1, lanes] == index, marks[k : k + 1, lanes], jnp.int16(0))
        tally[pl.ds(base, pair), lanes] = total
        return 0

    lax.fori_loop(0, nx * strips, count, 0)

    def group_of(r):
        first = lax.rem(x + nx - spread(r), nx) * 2
        return first, pl.ds(pl.multiple_of(first * cap, pair), pair)

    def score(r):
        first, span = group_of(r)
        rows = frows[pl.ds(first, 2)].reshape(pair, width)
        factor, live = [], []
        for q in range(2):
            line = fscale[first + q].astype(F32)[0:1]
            factor.append(jnp.broadcast_to(line, (cap, cap)).T[:, 0:1])
            live.append(jnp.where(lax.broadcasted_iota(I32, (cap, 1), 0) < counts[0, first + q], 1.0, 0.0))
        factor = jnp.concatenate(factor, axis=0)
        live = jnp.concatenate(live, axis=0)
        logits = lax.dot_general(rows, emb[...], (((1,), (1,)), ((), ())), preferred_element_type=F32) * factor
        chance = 0.5 * jnp.tanh(0.5 * logits) + 0.5
        mark = tally[span, :].astype(I32)
        hits = (mark & 63).astype(F32)
        on = (mark >> 6).astype(F32)
        dlogit = ((hits + live) * chance - on) * (1.0 / slots.shape[0])
        dscore[span, :] = (dlogit * factor).astype(BF16)

    def row_grads(r):
        first, span = group_of(r)
        grads[pl.ds(first, 2)] = (
            jnp.dot(dscore[span, :], emb[...], preferred_element_type=F32).astype(BF16).reshape(2, cap, width)
        )

    def pulled(r):
        first, span = group_of(r)
        rows = frows[pl.ds(first, 2)].reshape(pair, width)
        return lax.dot_general(dscore[span, :], rows, (((0,), (0,)), ((), ())), preferred_element_type=F32)

    def arrived(n):
        row_copy(n).wait()
        scale_copy(n).wait()

    push[...] = jnp.zeros_like(push)

    def work(r, _):
        @pl.when(r > 0)
        def _():
            arrived(2 * r)

        arrived(2 * r + 1)
        score(r)
        row_grads(r)

        @pl.when(r > 0)
        def _():
            grad_copy(2 * r).start()

        grad_copy(2 * r + 1).start()
        push[...] += pulled(r)
        return 0

    lax.fori_loop(0, far, work, 0)
    back[owner] = grads[owner]
    arrived(2 * far)
    arrived(2 * far + 1)
    score(far)

    inner[...] = ((push[...] + pulled(far)) * slope[...]).astype(BF16)

    def outer(which):
        side = docs[:, pl.ds(pl.multiple_of(which * half, half), half)]
        enc[which] = lax.dot_general(side, inner[...], (((0,), (0,)), ((), ())), preferred_element_type=F32)

    outer(1 - c)
    swap = remote(enc.at[1 - c], sib, s_sib, r_sib, chip(0, 0, 0, 1 - c))
    swap.start()
    outer(c)
    row_grads(far)
    grad_copy(2 * far).start()
    grad_copy(2 * far + 1).start()
    swap.wait()

    def join_p(q, _):
        rows = pl.ds(pl.multiple_of(q * piece, piece), piece)
        accp[q] = (enc[c, rows, :] + sib[rows, :]).astype(BF16)
        return 0

    def join_q(q, _):
        rows = pl.ds(pl.multiple_of(cut + q * piece, piece), piece)
        accq[q] = (enc[c, rows, :] + sib[rows, :]).astype(BF16)
        return 0

    lax.fori_loop(0, nx * ny, join_p, 0)
    lax.fori_loop(0, nz, join_q, 0)
    p1, q1 = [], []
    for n, (i, j) in enumerate(plane):
        to = lax.rem(x + i, nx) * ny + lax.rem(y + j, ny)
        p1.append(remote(accp.at[to], gotp.at[n], s_p.at[n], r_p.at[n], chip(i, j, 0, c)))
    for k in rings:
        to = lax.rem(z + k, nz)
        q1.append(remote(accq.at[to], gotq.at[k - 1], s_q.at[k - 1], r_q.at[k - 1], chip(0, 0, k, c)))
    for copy in p1 + q1:
        copy.start()

    for copy in p1:
        copy.wait()
    rows = pl.ds(pl.multiple_of(here * piece, piece), piece)
    total = enc[c, rows, :] + sib[rows, :]
    for n in range(len(plane)):
        total += gotp[n].astype(F32)
    for k in range(nz):
        shares[k] = total[k * share : (k + 1) * share, :]
    p2, q2 = [], []
    for k in rings:
        pz = lax.rem(z + k, nz)
        p2.append(remote(shares.at[pz], gots.at[k - 1], s_p2.at[k - 1], r_p2.at[k - 1], chip(0, 0, k, c)))
    for copy in p2:
        copy.start()
    for copy in q1:
        copy.wait()
    rows = pl.ds(pl.multiple_of(cut + z * piece, piece), piece)
    total = enc[c, rows, :] + sib[rows, :]
    for k in rings:
        total += gotq[k - 1].astype(F32)
    allx[x] = total
    for i in range(1, nx):
        q2.append(remote(allx.at[x], allx.at[x], s_x.at[i - 1], r_x.at[i - 1], chip(i, 0, 0, c)))
    for copy in q2:
        copy.start()

    for n in range(1, owners):
        grad_copy(n).wait()
    total = jnp.dot(onehot[...], back[...].reshape(owners * cap, width), preferred_element_type=F32)
    own[...] = total.reshape(own.shape)
    ownb[...] = total.astype(BF16).reshape(ownb.shape)
    first_a, first_b, second_a, second_b = [], [], [], []
    for j in cols:
        py = lax.rem(y + j, ny)
        first_a.append(remote(ownb.at[:, py, :, 0:wide], gota.at[j - 1], s_a.at[j - 1], r_a.at[j - 1],
                              chip(0, j, 0, c)))
    for k in rings:
        pz = lax.rem(z + k, nz)
        first_b.append(remote(ownb.at[pz, :, :, wide:], gotb.at[k - 1], s_b.at[k - 1], r_b.at[k - 1],
                              chip(0, 0, k, c)))
    for copy in first_a + first_b:
        copy.start()

    for copy in p2:
        copy.wait()
    total = shares[z]
    for k in rings:
        total += gots[k - 1]
    done[z] = total
    p2 = []
    for k in rings:
        p2.append(remote(done.at[z], done.at[z], s_ag.at[k - 1], r_ag.at[k - 1], chip(0, 0, k, c)))
    for copy in p2:
        copy.start()
    for copy in q2:
        copy.wait()
    total = allx[0]
    for i in range(1, nx):
        total += allx[i]
    ally[y] = total
    q2 = []
    for j in cols:
        q2.append(remote(ally.at[y], ally.at[y], s_y.at[j - 1], r_y.at[j - 1], chip(0, j, 0, c)))
    for copy in q2:
        copy.start()

    p3, q3 = [], []
    for copy in p2:
        copy.wait()
    rows_p = pl.ds(pl.multiple_of(here * piece, piece), piece)
    enc_out[c, rows_p, :] = jnp.concatenate([done[k] for k in range(nz)], axis=0)
    for n, (i, j) in enumerate(plane):
        part = enc_out.at[c, rows_p, :]
        p3.append(remote(part, part, s_p3.at[n], r_p3.at[n], chip(i, j, 0, c)))
    for copy in p3:
        copy.start()
    for copy in q2:
        copy.wait()
    total = ally[0]
    for j in cols:
        total += ally[j]
    rows_q = pl.ds(pl.multiple_of(cut + z * piece, piece), piece)
    enc_out[c, rows_q, :] = total
    for k in rings:
        part = enc_out.at[c, rows_q, :]
        q3.append(remote(part, part, s_q3.at[k - 1], r_q3.at[k - 1], chip(0, 0, k, c)))
    for copy in q3:
        copy.start()

    for copy in first_a:
        copy.wait()

    def join_a(q, _):
        total = own[q, y, :, 0:wide]
        for j in cols:
            total += gota[j - 1, q].astype(F32)
        acca[q] = total
        return 0

    lax.fori_loop(0, nz, join_a, 0)
    for k in rings:
        pz = lax.rem(z + k, nz)
        second_a.append(remote(acca.at[pz], gota2.at[k - 1], s_a2.at[k - 1], r_a2.at[k - 1], chip(0, 0, k, c)))
    for copy in second_a:
        copy.start()
    for copy in first_b:
        copy.wait()

    def join_b(q, _):
        total = own[z, q, :, wide:]
        for k in rings:
            total += gotb[k - 1, q].astype(F32)
        accb[q] = total
        return 0

    lax.fori_loop(0, ny, join_b, 0)
    for j in cols:
        py = lax.rem(y + j, ny)
        second_b.append(remote(accb.at[py], gotb2.at[j - 1], s_b2.at[j - 1], r_b2.at[j - 1], chip(0, j, 0, c)))
    for copy in second_b:
        copy.start()

    def pass_on(first, n):
        part = enc_out.at[c, pl.ds(pl.multiple_of(first, piece), piece), :]
        copy = remote(part, part, s_e.at[n], r_e.at[n], chip(0, 0, 0, 1 - c))
        copy.start()
        return copy

    handed = [pass_on(here * piece, 0), pass_on(cut + z * piece, 1)]
    for k in rings:
        q3[k - 1].wait()
        handed.append(pass_on(cut + lax.rem(z + nz - k, nz) * piece, 1 + k))
    for n, (i, j) in enumerate(plane):
        p3[n].wait()
        source = lax.rem(x + nx - i, nx) * ny + lax.rem(y + ny - j, ny)
        handed.append(pass_on(source * piece, nz + 1 + n))

    for copy in second_a:
        copy.wait()
    total = acca[z]
    for k in rings:
        total += gota2[k - 1]
    slab_out[:, 0:wide] = total
    for copy in second_b:
        copy.wait()
    total = accb[y]
    for j in cols:
        total += gotb2[j - 1]
    slab_out[:, wide:] = total
    for copy in handed:
        copy.wait()


def body(dims, documents, enc_weight, label_slab, row_scale, shortlist, positive, request_ids, counts):
    nx, ny, nz = dims
    docs, width = documents.shape
    held = label_slab.shape[0]
    owners, cap = request_ids.shape
    picks = shortlist.shape[1]
    plane = nx * ny
    depth = held // (ny * nz)
    wide = 2 * width // 3
    slim = width - wide
    half = width // 2
    piece = half // (plane + nz)
    share = piece // nz
    slot_count = owners * cap
    f32 = lambda *shape: pltpu.VMEM(shape, F32)
    b16 = lambda *shape: pltpu.VMEM(shape, BF16)
    i32 = lambda *shape: pltpu.VMEM(shape, I32)
    i16 = lambda *shape: pltpu.VMEM(shape, I16)
    dma = lambda n: [pltpu.SemaphoreType.DMA((n,))] * 2
    vmem = pl.BlockSpec(memory_space=pltpu.VMEM)
    anywhere = pl.BlockSpec(memory_space=pl.ANY)
    slab_grad, enc_grad = pl.pallas_call(
        functools.partial(step_kernel, dims),
        out_shape=(jax.ShapeDtypeStruct((depth, width), F32), jax.ShapeDtypeStruct((2, half, width), F32)),
        in_specs=[anywhere] * 3 + [vmem] * 2 + [anywhere] * 2 + [pl.BlockSpec(memory_space=pltpu.SMEM)],
        out_specs=[vmem] * 2,
        scratch_shapes=[
            b16(docs, width), b16(width, width), b16(held, width), i32(picks, docs), i32(picks, docs),
            i16(picks, docs), i16(picks, docs),
            b16(docs, width), f32(docs, width), f32(docs, width), b16(held, slot_count),
            b16(owners, cap, width), b16(owners, cap, width),
            b16(owners, 16, cap), b16(owners, 16, cap), i32(owners, 1, cap),
            i16(slot_count, docs), b16(slot_count, docs),
            b16(owners, cap, width), b16(owners, cap, width),
            f32(nz, ny, depth, width), b16(nz, ny, depth, width),
            b16(ny - 1, nz, depth, wide), b16(nz - 1, ny, depth, slim),
            f32(nz, depth, wide), f32(ny, depth, slim),
            f32(nz - 1, depth, wide), f32(ny - 1, depth, slim),
            b16(docs, width), f32(2, half, width), f32(half, width),
            b16(plane, piece, width), b16(nz, piece, width),
            b16(plane - 1, piece, width), b16(nz - 1, piece, width),
            f32(nz, share, width), f32(nz - 1, share, width), f32(nz, share, width),
            f32(nx, piece, width), f32(ny, piece, width),
            pltpu.SemaphoreType.DMA((5,)), *dma(owners), *dma(owners), *dma(owners), *dma(owners),
            *dma(ny - 1), *dma(nz - 1), *dma(nz - 1), *dma(ny - 1),
            pltpu.SemaphoreType.DMA, pltpu.SemaphoreType.DMA,
            *dma(plane - 1), *dma(nz - 1), *dma(nz - 1), *dma(nz - 1), *dma(nx - 1), *dma(ny - 1), *dma(plane - 1), *dma(nz - 1),
            *dma(plane + nz),
        ],
        compiler_params=pltpu.CompilerParams(
            collective_id=1, has_side_effects=True, vmem_limit_bytes=44 * 2**20
        ),
        cost_estimate=pl.CostEstimate(flops=10**10, bytes_accessed=10**7, transcendentals=2 * 10**6),
        name="classifier_step",
    )(
        documents,
        enc_weight,
        label_slab,
        row_scale,
        request_ids.reshape(owners, 1, cap),
        shortlist.T,
        positive.T,
        counts,
    )
    return slab_grad, enc_grad.reshape(width, width)


def solution(mesh):
    return jax.shard_map(
        functools.partial(body, torus(mesh)),
        mesh=mesh,
        in_specs=(
            P(("owner", "dp"), None),
            P(),
            P("owner", None),
            P("owner"),
            P(("owner", "dp"), None),
            P(("owner", "dp"), None),
            P(("owner", "dp"), None),
            P(("owner", "dp"), None),
        ),
        out_specs=(P(("owner", "dp"), None), P()),
        check_vma=False,
    )
```

```python
import functools

import jax
import jax.numpy as jnp
from jax import lax
from jax.experimental import pallas as pl
from jax.experimental.pallas import tpu as pltpu
from jax.sharding import PartitionSpec as P

MESH = pl.DeviceIdType.MESH
F32 = jnp.float32
BF16 = jnp.bfloat16
I32 = jnp.int32
I16 = jnp.int16


def torus(mesh):
    owners, groups = mesh.shape["owner"], mesh.shape["dp"]
    ny = 4 if groups >= 16 else 2
    return owners // 2, ny, groups // ny


def remote(src, dst, send, recv, target):
    return pltpu.make_async_remote_copy(
        src_ref=src, dst_ref=dst, send_sem=send, recv_sem=recv, device_id=target, device_id_type=MESH
    )


def step_kernel(
    dims, docs_in, weight_in, slab_in, scale_in, ids_in, slots_in, on_in, counts_in, slab_out, enc_out,
    ids, counts, scale, docs, weight, slab, slots32, on32, slots, marks, emb, slope, push, onehot, srows, frows, sscale, fscale, gids, tally, dscore, grads, back,
    own, ownb, gota, gotb, acca, accb, gota2, gotb2,
    inner, enc, sib, accp, accq, gotp, gotq, shares, gots, done, allx, ally,
    s_in, s_id, r_id, s_f, r_f, s_c, r_c, s_g, r_g,
    s_a, r_a, s_b, r_b, s_a2, r_a2, s_b2, r_b2,
    s_sib, r_sib, s_p, r_p, s_q, r_q, s_p2, r_p2, s_ag, r_ag, s_x, r_x, s_y, r_y, s_p3, r_p3, s_q3, r_q3, s_e, r_e,
):
    nx, ny, nz = dims
    owner, group = lax.axis_index("owner"), lax.axis_index("dp")
    x, c = owner // 2, owner % 2
    y, z = group % ny, group // ny
    here = x * ny + y
    owners = 2 * nx
    cap = srows.shape[1]
    pair = 2 * cap
    documents, width = docs.shape
    rows_held = slab.shape[0]
    wide = gota.shape[-1]
    depth = gota.shape[-2]
    piece = accp.shape[1]
    share = shares.shape[1]
    half = enc.shape[1]
    cut = nx * ny * piece
    strip = min(128, documents)
    far = nx - 1

    plane = [(i, j) for i in range(nx) for j in range(ny) if (i, j) != (0, 0)]
    rings = list(range(1, nz))
    cols = list(range(1, ny))

    def chip(i, j, k, core):
        return {"owner": lax.rem(x + i, nx) * 2 + core, "dp": lax.rem(z + k, nz) * ny + lax.rem(y + j, ny)}

    def spread(r):
        return r + (r // 2) * (5 - 2 * r) if nx == 4 else r

    loads = [
        pltpu.make_async_copy(src, dst, s_in.at[n])
        for n, (src, dst) in enumerate(
            (
                (docs_in, docs), (weight_in, weight), (slab_in, slab), (slots_in, slots32), (on_in, on32),
                (ids_in, ids), (counts_in, counts), (scale_in, scale),
            )
        )
    ]
    for load in loads[5:] + loads[:5]:
        load.start()

    bar = pltpu.get_barrier_semaphore()
    greeted = 0
    for i, j in plane:
        pl.semaphore_signal(bar, inc=1, device_id=chip(i, j, 0, c), device_id_type=MESH)
        greeted += 1
    for i in range(nx):
        pl.semaphore_signal(bar, inc=1, device_id=chip(i, 0, 0, 1 - c), device_id_type=MESH)
        greeted += 1
    for k in rings:
        pl.semaphore_signal(bar, inc=1, device_id=chip(0, 0, k, c), device_id_type=MESH)
        greeted += 1
    pl.semaphore_wait(bar, greeted)

    def peer(n):
        r, flip = n // 2, n % 2
        core = lax.rem(c + flip, 2)
        to = lax.rem(x + spread(r), nx) * 2 + core
        source = lax.rem(x + nx - spread(r), nx) * 2 + core
        return to, source

    def id_copy(n):
        to, _ = peer(n)
        return remote(ids.at[to], gids.at[owner], s_id.at[n], r_id.at[n], {"owner": to, "dp": group})

    loads[5].wait()
    for n in range(1, owners):
        id_copy(n).start()
    gids[owner] = ids[owner]

    loads[0].wait()
    loads[1].wait()
    squashed = jnp.tanh(jnp.dot(docs[...], weight[...], preferred_element_type=F32))
    emb[...] = (docs[...].astype(F32) + squashed).astype(BF16)
    slope[...] = 1.0 - squashed * squashed
    loads[2].wait()
    loads[6].wait()
    loads[7].wait()

    def row_copy(n):
        to, _ = peer(n)
        return remote(srows.at[to], frows.at[owner], s_f.at[n], r_f.at[n], {"owner": to, "dp": group})

    def scale_copy(n):
        to, _ = peer(n)
        return remote(sscale.at[to], fscale.at[owner], s_c.at[n], r_c.at[n], {"owner": to, "dp": group})

    scale_rows = jnp.broadcast_to(scale[...].reshape(1, rows_held), (16, rows_held))

    def serve(m, _):
        n = lax.rem(m + 2, owners)
        to, _source = peer(n)

        @pl.when(n > 0)
        def _():
            id_copy(n).wait_send()

        hot = jnp.where(
            lax.broadcasted_iota(I32, (rows_held, cap), 0) == gids[to], 1.0, 0.0
        ).astype(BF16)
        onehot[:, pl.ds(pl.multiple_of(to * cap, cap), cap)] = hot
        rows = lax.dot_general(hot, slab[...], (((0,), (0,)), ((), ())), preferred_element_type=F32).astype(BF16)
        sc = jnp.dot(scale_rows, hot, preferred_element_type=F32).astype(BF16)
        srows[to] = rows
        sscale[to] = sc

        @pl.when(n == 0)
        def _():
            frows[owner] = rows
            fscale[owner] = sc

        @pl.when(n > 0)
        def _():
            row_copy(n).start()
            scale_copy(n).start()

        return 0

    for n in range(1, owners):
        id_copy(n).wait_recv()
    lax.fori_loop(0, owners, serve, 0)

    def grad_copy(n):
        _, source = peer(n)
        return remote(grads.at[source], back.at[owner], s_g.at[n], r_g.at[n], {"owner": source, "dp": group})

    loads[3].wait()
    loads[4].wait()
    slots[...] = slots32[...].astype(I16)
    marks[...] = (1 + 64 * on32[...]).astype(I16)
    strips = documents // strip

    def count(m, _):
        base = pl.multiple_of((m // strips) * pair, pair)
        lanes = pl.ds(pl.multiple_of((m % strips) * strip, strip), strip)
        index = (lax.broadcasted_iota(I32, (pair, strip), 0) + base).astype(I16)
        total = jnp.zeros((pair, strip), I16)
        for k in range(slots.shape[0]):
            total += jnp.where(slots[k : k + 1, lanes] == index, marks[k : k + 1, lanes], jnp.int16(0))
        tally[pl.ds(base, pair), lanes] = total
        return 0

    lax.fori_loop(0, nx * strips, count, 0)

    def group_of(r):
        first = lax.rem(x + nx - spread(r), nx) * 2
        return first, pl.ds(pl.multiple_of(first * cap, pair), pair)

    def score(r):
        first, span = group_of(r)
        rows = frows[pl.ds(first, 2)].reshape(pair, width)
        factor, live = [], []
        for q in range(2):
            line = fscale[first + q].astype(F32)[0:1]
            factor.append(jnp.broadcast_to(line, (cap, cap)).T[:, 0:1])
            lane = lax.broadcasted_iota(I32, (1, owners), 1)
            asked = jnp.sum(jnp.where(lane == first + q, counts[...].astype(F32), 0.0), axis=1, keepdims=True)
            live.append(jnp.where(lax.broadcasted_iota(I32, (cap, 1), 0).astype(F32) < asked, 1.0, 0.0))
        factor = jnp.concatenate(factor, axis=0)
        live = jnp.concatenate(live, axis=0)
        logits = lax.dot_general(rows, emb[...], (((1,), (1,)), ((), ())), preferred_element_type=F32) * factor
        chance = 0.5 * jnp.tanh(0.5 * logits) + 0.5
        mark = tally[span, :].astype(I32)
        hits = (mark & 63).astype(F32)
        on = (mark >> 6).astype(F32)
        dlogit = ((hits + live) * chance - on) * (1.0 / slots.shape[0])
        dscore[span, :] = (dlogit * factor).astype(BF16)

    def row_grads(r):
        first, span = group_of(r)
        grads[pl.ds(first, 2)] = (
            jnp.dot(dscore[span, :], emb[...], preferred_element_type=F32).astype(BF16).reshape(2, cap, width)
        )

    def pulled(r):
        first, span = group_of(r)
        rows = frows[pl.ds(first, 2)].reshape(pair, width)
        return lax.dot_general(dscore[span, :], rows, (((0,), (0,)), ((), ())), preferred_element_type=F32)

    def arrived(n):
        row_copy(n).wait()
        scale_copy(n).wait()

    push[...] = jnp.zeros_like(push)

    def work(r, _):
        @pl.when(r > 0)
        def _():
            arrived(2 * r)

        arrived(2 * r + 1)
        score(r)
        row_grads(r)

        @pl.when(r > 0)
        def _():
            grad_copy(2 * r).start()

        grad_copy(2 * r + 1).start()
        push[...] += pulled(r)
        return 0

    lax.fori_loop(0, far, work, 0)
    back[owner] = grads[owner]
    arrived(2 * far)
    arrived(2 * far + 1)
    score(far)

    inner[...] = ((push[...] + pulled(far)) * slope[...]).astype(BF16)

    def outer(which):
        side = docs[:, pl.ds(pl.multiple_of(which * half, half), half)]
        enc[which] = lax.dot_general(side, inner[...], (((0,), (0,)), ((), ())), preferred_element_type=F32)

    outer(1 - c)
    swap = remote(enc.at[1 - c], sib, s_sib, r_sib, chip(0, 0, 0, 1 - c))
    swap.start()
    outer(c)
    row_grads(far)
    grad_copy(2 * far).start()
    grad_copy(2 * far + 1).start()
    swap.wait()

    def join_p(q, _):
        rows = pl.ds(pl.multiple_of(q * piece, piece), piece)
        accp[q] = (enc[c, rows, :] + sib[rows, :]).astype(BF16)
        return 0

    def join_q(q, _):
        rows = pl.ds(pl.multiple_of(cut + q * piece, piece), piece)
        accq[q] = (enc[c, rows, :] + sib[rows, :]).astype(BF16)
        return 0

    lax.fori_loop(0, nx * ny, join_p, 0)
    lax.fori_loop(0, nz, join_q, 0)
    p1, q1 = [], []
    for n, (i, j) in enumerate(plane):
        to = lax.rem(x + i, nx) * ny + lax.rem(y + j, ny)
        p1.append(remote(accp.at[to], gotp.at[n], s_p.at[n], r_p.at[n], chip(i, j, 0, c)))
    for k in rings:
        to = lax.rem(z + k, nz)
        q1.append(remote(accq.at[to], gotq.at[k - 1], s_q.at[k - 1], r_q.at[k - 1], chip(0, 0, k, c)))
    for copy in p1 + q1:
        copy.start()

    for copy in p1:
        copy.wait()
    rows = pl.ds(pl.multiple_of(here * piece, piece), piece)
    total = enc[c, rows, :] + sib[rows, :]
    for n in range(len(plane)):
        total += gotp[n].astype(F32)
    for k in range(nz):
        shares[k] = total[k * share : (k + 1) * share, :]
    p2, q2 = [], []
    for k in rings:
        pz = lax.rem(z + k, nz)
        p2.append(remote(shares.at[pz], gots.at[k - 1], s_p2.at[k - 1], r_p2.at[k - 1], chip(0, 0, k, c)))
    for copy in p2:
        copy.start()
    for copy in q1:
        copy.wait()
    rows = pl.ds(pl.multiple_of(cut + z * piece, piece), piece)
    total = enc[c, rows, :] + sib[rows, :]
    for k in rings:
        total += gotq[k - 1].astype(F32)
    allx[x] = total
    for i in range(1, nx):
        q2.append(remote(allx.at[x], allx.at[x], s_x.at[i - 1], r_x.at[i - 1], chip(i, 0, 0, c)))
    for copy in q2:
        copy.start()

    for n in range(1, owners):
        grad_copy(n).wait()
    total = jnp.dot(onehot[...], back[...].reshape(owners * cap, width), preferred_element_type=F32)
    own[...] = total.reshape(own.shape)
    ownb[...] = total.astype(BF16).reshape(ownb.shape)
    first_a, first_b, second_a, second_b = [], [], [], []
    for j in cols:
        py = lax.rem(y + j, ny)
        first_a.append(remote(ownb.at[:, py, :, 0:wide], gota.at[j - 1], s_a.at[j - 1], r_a.at[j - 1],
                              chip(0, j, 0, c)))
    for k in rings:
        pz = lax.rem(z + k, nz)
        first_b.append(remote(ownb.at[pz, :, :, wide:], gotb.at[k - 1], s_b.at[k - 1], r_b.at[k - 1],
                              chip(0, 0, k, c)))
    for copy in first_a + first_b:
        copy.start()

    for copy in p2:
        copy.wait()
    total = shares[z]
    for k in rings:
        total += gots[k - 1]
    done[z] = total
    p2 = []
    for k in rings:
        p2.append(remote(done.at[z], done.at[z], s_ag.at[k - 1], r_ag.at[k - 1], chip(0, 0, k, c)))
    for copy in p2:
        copy.start()
    for copy in q2:
        copy.wait()
    total = allx[0]
    for i in range(1, nx):
        total += allx[i]
    ally[y] = total
    q2 = []
    for j in cols:
        q2.append(remote(ally.at[y], ally.at[y], s_y.at[j - 1], r_y.at[j - 1], chip(0, j, 0, c)))
    for copy in q2:
        copy.start()

    p3, q3 = [], []
    for copy in p2:
        copy.wait()
    rows_p = pl.ds(pl.multiple_of(here * piece, piece), piece)
    enc_out[c, rows_p, :] = jnp.concatenate([done[k] for k in range(nz)], axis=0)
    for n, (i, j) in enumerate(plane):
        part = enc_out.at[c, rows_p, :]
        p3.append(remote(part, part, s_p3.at[n], r_p3.at[n], chip(i, j, 0, c)))
    for copy in p3:
        copy.start()
    for copy in q2:
        copy.wait()
    total = ally[0]
    for j in cols:
        total += ally[j]
    rows_q = pl.ds(pl.multiple_of(cut + z * piece, piece), piece)
    enc_out[c, rows_q, :] = total
    for k in rings:
        part = enc_out.at[c, rows_q, :]
        q3.append(remote(part, part, s_q3.at[k - 1], r_q3.at[k - 1], chip(0, 0, k, c)))
    for copy in q3:
        copy.start()

    for copy in first_a:
        copy.wait()

    def join_a(q, _):
        total = own[q, y, :, 0:wide]
        for j in cols:
            total += gota[j - 1, q].astype(F32)
        acca[q] = total
        return 0

    lax.fori_loop(0, nz, join_a, 0)
    for k in rings:
        pz = lax.rem(z + k, nz)
        second_a.append(remote(acca.at[pz], gota2.at[k - 1], s_a2.at[k - 1], r_a2.at[k - 1], chip(0, 0, k, c)))
    for copy in second_a:
        copy.start()
    for copy in first_b:
        copy.wait()

    def join_b(q, _):
        total = own[z, q, :, wide:]
        for k in rings:
            total += gotb[k - 1, q].astype(F32)
        accb[q] = total
        return 0

    lax.fori_loop(0, ny, join_b, 0)
    for j in cols:
        py = lax.rem(y + j, ny)
        second_b.append(remote(accb.at[py], gotb2.at[j - 1], s_b2.at[j - 1], r_b2.at[j - 1], chip(0, j, 0, c)))
    for copy in second_b:
        copy.start()

    def pass_on(first, n):
        part = enc_out.at[c, pl.ds(pl.multiple_of(first, piece), piece), :]
        copy = remote(part, part, s_e.at[n], r_e.at[n], chip(0, 0, 0, 1 - c))
        copy.start()
        return copy

    handed = [pass_on(here * piece, 0), pass_on(cut + z * piece, 1)]
    for k in rings:
        q3[k - 1].wait()
        handed.append(pass_on(cut + lax.rem(z + nz - k, nz) * piece, 1 + k))
    for n, (i, j) in enumerate(plane):
        p3[n].wait()
        source = lax.rem(x + nx - i, nx) * ny + lax.rem(y + ny - j, ny)
        handed.append(pass_on(source * piece, nz + 1 + n))

    for copy in second_a:
        copy.wait()
    total = acca[z]
    for k in rings:
        total += gota2[k - 1]
    slab_out[:, 0:wide] = total
    for copy in second_b:
        copy.wait()
    total = accb[y]
    for j in cols:
        total += gotb2[j - 1]
    slab_out[:, wide:] = total
    for copy in handed:
        copy.wait()


def body(dims, documents, enc_weight, label_slab, row_scale, shortlist, positive, request_ids, counts):
    nx, ny, nz = dims
    docs, width = documents.shape
    held = label_slab.shape[0]
    owners, cap = request_ids.shape
    picks = shortlist.shape[1]
    plane = nx * ny
    depth = held // (ny * nz)
    wide = 2 * width // 3
    slim = width - wide
    half = width // 2
    piece = half // (plane + nz)
    share = piece // nz
    slot_count = owners * cap
    f32 = lambda *shape: pltpu.VMEM(shape, F32)
    b16 = lambda *shape: pltpu.VMEM(shape, BF16)
    i32 = lambda *shape: pltpu.VMEM(shape, I32)
    i16 = lambda *shape: pltpu.VMEM(shape, I16)
    dma = lambda n: [pltpu.SemaphoreType.DMA((n,))] * 2
    vmem = pl.BlockSpec(memory_space=pltpu.VMEM)
    slab_grad, enc_grad = pl.pallas_call(
        functools.partial(step_kernel, dims),
        out_shape=(jax.ShapeDtypeStruct((depth, width), F32), jax.ShapeDtypeStruct((2, half, width), F32)),
        in_specs=[pl.BlockSpec(memory_space=pltpu.HBM)] * 8,
        out_specs=[vmem] * 2,
        scratch_shapes=[
            i32(owners, 1, cap), i32(1, owners), b16(held), b16(docs, width), b16(width, width), b16(held, width), i32(picks, docs), i32(picks, docs),
            i16(picks, docs), i16(picks, docs),
            b16(docs, width), f32(docs, width), f32(docs, width), b16(held, slot_count),
            b16(owners, cap, width), b16(owners, cap, width),
            b16(owners, 16, cap), b16(owners, 16, cap), i32(owners, 1, cap),
            i16(slot_count, docs), b16(slot_count, docs),
            b16(owners, cap, width), b16(owners, cap, width),
            f32(nz, ny, depth, width), b16(nz, ny, depth, width),
            b16(ny - 1, nz, depth, wide), b16(nz - 1, ny, depth, slim),
            f32(nz, depth, wide), f32(ny, depth, slim),
            f32(nz - 1, depth, wide), f32(ny - 1, depth, slim),
            b16(docs, width), f32(2, half, width), f32(half, width),
            b16(plane, piece, width), b16(nz, piece, width),
            b16(plane - 1, piece, width), b16(nz - 1, piece, width),
            f32(nz, share, width), f32(nz - 1, share, width), f32(nz, share, width),
            f32(nx, piece, width), f32(ny, piece, width),
            pltpu.SemaphoreType.DMA((8,)), *dma(owners), *dma(owners), *dma(owners), *dma(owners),
            *dma(ny - 1), *dma(nz - 1), *dma(nz - 1), *dma(ny - 1),
            pltpu.SemaphoreType.DMA, pltpu.SemaphoreType.DMA,
            *dma(plane - 1), *dma(nz - 1), *dma(nz - 1), *dma(nz - 1), *dma(nx - 1), *dma(ny - 1), *dma(plane - 1), *dma(nz - 1),
            *dma(plane + nz),
        ],
        compiler_params=pltpu.CompilerParams(
            collective_id=1, has_side_effects=True, vmem_limit_bytes=44 * 2**20
        ),
        cost_estimate=pl.CostEstimate(flops=10**10, bytes_accessed=10**7, transcendentals=2 * 10**6),
        name="classifier_step",
    )(*(pltpu.with_memory_space_constraint(operand, pltpu.HBM) for operand in (
        documents,
        enc_weight,
        label_slab,
        row_scale,
        request_ids.reshape(owners, 1, cap),
        shortlist.T,
        positive.T,
        counts,
    )))
    return slab_grad, enc_grad.reshape(width, width)


def solution(mesh):
    return jax.shard_map(
        functools.partial(body, torus(mesh)),
        mesh=mesh,
        in_specs=(
            P(("owner", "dp"), None),
            P(),
            P("owner", None),
            P("owner"),
            P(("owner", "dp"), None),
            P(("owner", "dp"), None),
            P(("owner", "dp"), None),
            P(("owner", "dp"), None),
        ),
        out_specs=(P(("owner", "dp"), None), P()),
        check_vma=False,
    )
```

```python
import functools

import jax
import jax.numpy as jnp
from jax import lax
from jax.experimental import pallas as pl
from jax.experimental.pallas import tpu as pltpu
from jax.sharding import PartitionSpec as P

MESH = pl.DeviceIdType.MESH
F32 = jnp.float32
BF16 = jnp.bfloat16
I32 = jnp.int32
I16 = jnp.int16


def torus(mesh):
    owners, groups = mesh.shape["owner"], mesh.shape["dp"]
    ny = 4 if groups >= 16 else 2
    return owners // 2, ny, groups // ny


def remote(src, dst, send, recv, target):
    return pltpu.make_async_remote_copy(
        src_ref=src, dst_ref=dst, send_sem=send, recv_sem=recv, device_id=target, device_id_type=MESH
    )


def step_kernel(
    dims, docs_in, weight_in, slab_in, scale_in, ids_in, slots_in, on_in, counts_in, slab_out, enc_out,
    ids, counts, scale, docs, weight, slab, slots32, on32, slots, marks, emb, slope, push, onehot, srows, frows, sscale, fscale, gids, tally, dscore, grads, back,
    own, ownb, gota, gotb, acca, accb, gota2, gotb2,
    inner, enc, sib, accp, accq, gotp, gotq, shares, gots, done, allx, ally,
    s_in, s_id, r_id, s_f, r_f, s_c, r_c, s_g, r_g,
    s_a, r_a, s_b, r_b, s_a2, r_a2, s_b2, r_b2,
    s_sib, r_sib, s_p, r_p, s_q, r_q, s_p2, r_p2, s_ag, r_ag, s_x, r_x, s_y, r_y, s_p3, r_p3, s_q3, r_q3, s_e, r_e,
):
    nx, ny, nz = dims
    owner, group = lax.axis_index("owner"), lax.axis_index("dp")
    x, c = owner // 2, owner % 2
    y, z = group % ny, group // ny
    here = x * ny + y
    owners = 2 * nx
    cap = srows.shape[1]
    pair = 2 * cap
    documents, width = docs.shape
    rows_held = slab.shape[0]
    wide = gota.shape[-1]
    depth = gota.shape[-2]
    piece = accp.shape[1]
    share = shares.shape[1]
    half = enc.shape[1]
    cut = nx * ny * piece
    strip = min(128, documents)
    far = nx - 1

    plane = [(i, j) for i in range(nx) for j in range(ny) if (i, j) != (0, 0)]
    rings = list(range(1, nz))
    cols = list(range(1, ny))

    def chip(i, j, k, core):
        return {"owner": lax.rem(x + i, nx) * 2 + core, "dp": lax.rem(z + k, nz) * ny + lax.rem(y + j, ny)}

    def spread(r):
        return r + (r // 2) * (5 - 2 * r) if nx == 4 else r

    loads = [
        pltpu.make_async_copy(src, dst, s_in.at[n])
        for n, (src, dst) in enumerate(
            (
                (docs_in, docs), (weight_in, weight), (slab_in, slab), (slots_in, slots32), (on_in, on32),
                (ids_in, ids), (counts_in, counts), (scale_in, scale),
            )
        )
    ]
    for load in loads[5:] + loads[:5]:
        load.start()

    bar = pltpu.get_barrier_semaphore()
    greeted = 0
    for i, j in plane:
        pl.semaphore_signal(bar, inc=1, device_id=chip(i, j, 0, c), device_id_type=MESH)
        greeted += 1
    for i in range(nx):
        pl.semaphore_signal(bar, inc=1, device_id=chip(i, 0, 0, 1 - c), device_id_type=MESH)
        greeted += 1
    for k in rings:
        pl.semaphore_signal(bar, inc=1, device_id=chip(0, 0, k, c), device_id_type=MESH)
        greeted += 1
    pl.semaphore_wait(bar, greeted)

    def peer(n):
        r, flip = n // 2, n % 2
        core = lax.rem(c + flip, 2)
        to = lax.rem(x + spread(r), nx) * 2 + core
        source = lax.rem(x + nx - spread(r), nx) * 2 + core
        return to, source

    def id_copy(n):
        to, _ = peer(n)
        return remote(ids.at[to], gids.at[owner], s_id.at[n], r_id.at[n], {"owner": to, "dp": group})

    loads[5].wait()
    for n in range(1, owners):
        id_copy(n).start()
    gids[owner] = ids[owner]

    loads[0].wait()
    loads[1].wait()
    squashed = jnp.tanh(jnp.dot(docs[...], weight[...], preferred_element_type=F32))
    emb[...] = (docs[...].astype(F32) + squashed).astype(BF16)
    slope[...] = 1.0 - squashed * squashed
    loads[2].wait()
    loads[6].wait()
    loads[7].wait()

    def row_copy(n):
        to, _ = peer(n)
        return remote(srows.at[to], frows.at[owner], s_f.at[n], r_f.at[n], {"owner": to, "dp": group})

    def scale_copy(n):
        to, _ = peer(n)
        return remote(sscale.at[to], fscale.at[owner], s_c.at[n], r_c.at[n], {"owner": to, "dp": group})

    scale_rows = jnp.broadcast_to(scale[...].reshape(1, rows_held), (16, rows_held))

    def serve(m, _):
        n = lax.rem(m + 2, owners)
        to, _source = peer(n)

        @pl.when(n > 0)
        def _():
            id_copy(n).wait_send()

        hot = jnp.where(
            lax.broadcasted_iota(I32, (rows_held, cap), 0) == gids[to], 1.0, 0.0
        ).astype(BF16)
        onehot[:, pl.ds(pl.multiple_of(to * cap, cap), cap)] = hot
        rows = lax.dot_general(hot, slab[...], (((0,), (0,)), ((), ())), preferred_element_type=F32).astype(BF16)
        sc = jnp.dot(scale_rows, hot, preferred_element_type=F32).astype(BF16)
        srows[to] = rows
        sscale[to] = sc

        @pl.when(n == 0)
        def _():
            frows[owner] = rows
            fscale[owner] = sc

        @pl.when(n > 0)
        def _():
            row_copy(n).start()
            scale_copy(n).start()

        return 0

    for n in range(1, owners):
        id_copy(n).wait_recv()
    lax.fori_loop(0, owners, serve, 0)

    parts = range(2)
    part_width = width // 2

    def grad_copy(h, n):
        _, source = peer(n)
        return remote(
            grads.at[h, source], back.at[h, owner], s_g.at[h, n], r_g.at[h, n], {"owner": source, "dp": group}
        )

    loads[3].wait()
    loads[4].wait()
    slots[...] = slots32[...].astype(I16)
    marks[...] = (1 + 64 * on32[...]).astype(I16)
    strips = documents // strip

    def count(m, _):
        base = pl.multiple_of((m // strips) * pair, pair)
        lanes = pl.ds(pl.multiple_of((m % strips) * strip, strip), strip)
        index = (lax.broadcasted_iota(I32, (pair, strip), 0) + base).astype(I16)
        total = jnp.zeros((pair, strip), I16)
        for k in range(slots.shape[0]):
            total += jnp.where(slots[k : k + 1, lanes] == index, marks[k : k + 1, lanes], jnp.int16(0))
        tally[pl.ds(base, pair), lanes] = total
        return 0

    lax.fori_loop(0, nx * strips, count, 0)

    def group_of(r):
        first = lax.rem(x + nx - spread(r), nx) * 2
        return first, pl.ds(pl.multiple_of(first * cap, pair), pair)

    def score(r):
        first, span = group_of(r)
        rows = frows[pl.ds(first, 2)].reshape(pair, width)
        factor, live = [], []
        for q in range(2):
            line = fscale[first + q].astype(F32)[0:1]
            factor.append(jnp.broadcast_to(line, (cap, cap)).T[:, 0:1])
            lane = lax.broadcasted_iota(I32, (1, owners), 1)
            asked = jnp.sum(jnp.where(lane == first + q, counts[...].astype(F32), 0.0), axis=1, keepdims=True)
            live.append(jnp.where(lax.broadcasted_iota(I32, (cap, 1), 0).astype(F32) < asked, 1.0, 0.0))
        factor = jnp.concatenate(factor, axis=0)
        live = jnp.concatenate(live, axis=0)
        logits = lax.dot_general(rows, emb[...], (((1,), (1,)), ((), ())), preferred_element_type=F32) * factor
        chance = 0.5 * jnp.tanh(0.5 * logits) + 0.5
        mark = tally[span, :].astype(I32)
        hits = (mark & 63).astype(F32)
        on = (mark >> 6).astype(F32)
        dlogit = ((hits + live) * chance - on) * (1.0 / slots.shape[0])
        dscore[span, :] = (dlogit * factor).astype(BF16)

    def row_grads(r):
        first, span = group_of(r)
        product = jnp.dot(dscore[span, :], emb[...], preferred_element_type=F32).astype(BF16)
        for h in parts:
            grads[h, pl.ds(first, 2)] = product[:, h * part_width : (h + 1) * part_width].reshape(2, cap, part_width)

    def pulled(r):
        first, span = group_of(r)
        rows = frows[pl.ds(first, 2)].reshape(pair, width)
        return lax.dot_general(dscore[span, :], rows, (((0,), (0,)), ((), ())), preferred_element_type=F32)

    def arrived(n):
        row_copy(n).wait()
        scale_copy(n).wait()

    push[...] = jnp.zeros_like(push)

    def work(r, _):
        @pl.when(r > 0)
        def _():
            arrived(2 * r)

        arrived(2 * r + 1)
        score(r)
        row_grads(r)

        @pl.when(r > 0)
        def _():
            grad_copy(0, 2 * r).start()

        grad_copy(0, 2 * r + 1).start()
        push[...] += pulled(r)
        return 0

    lax.fori_loop(0, far, work, 0)
    for h in parts:
        back[h, owner] = grads[h, owner]
    arrived(2 * far)
    arrived(2 * far + 1)
    score(far)
    row_grads(far)
    grad_copy(0, 2 * far).start()
    grad_copy(0, 2 * far + 1).start()

    inner[...] = ((push[...] + pulled(far)) * slope[...]).astype(BF16)

    def outer(which):
        side = docs[:, pl.ds(pl.multiple_of(which * half, half), half)]
        enc[which] = lax.dot_general(side, inner[...], (((0,), (0,)), ((), ())), preferred_element_type=F32)

    outer(1 - c)
    swap = remote(enc.at[1 - c], sib, s_sib, r_sib, chip(0, 0, 0, 1 - c))
    swap.start()
    outer(c)
    swap.wait()

    def join_p(q, _):
        rows = pl.ds(pl.multiple_of(q * piece, piece), piece)
        accp[q] = (enc[c, rows, :] + sib[rows, :]).astype(BF16)
        return 0

    def join_q(q, _):
        rows = pl.ds(pl.multiple_of(cut + q * piece, piece), piece)
        accq[q] = (enc[c, rows, :] + sib[rows, :]).astype(BF16)
        return 0

    lax.fori_loop(0, nx * ny, join_p, 0)
    lax.fori_loop(0, nz, join_q, 0)
    p1, q1 = [], []
    for n, (i, j) in enumerate(plane):
        to = lax.rem(x + i, nx) * ny + lax.rem(y + j, ny)
        p1.append(remote(accp.at[to], gotp.at[n], s_p.at[n], r_p.at[n], chip(i, j, 0, c)))
    for k in rings:
        to = lax.rem(z + k, nz)
        q1.append(remote(accq.at[to], gotq.at[k - 1], s_q.at[k - 1], r_q.at[k - 1], chip(0, 0, k, c)))
    for copy in p1 + q1:
        copy.start()

    for n in range(1, owners):
        grad_copy(1, n).start()

    def cols_a(h):
        return pl.ds(h * part_width, wide)

    def cols_b(h):
        return pl.ds(h * part_width + wide, part_width - wide)

    first_a, first_b, second_a, second_b = [[], []], [[], []], [[], []], [[], []]

    def sum_rows(h):
        for n in range(1, owners):
            grad_copy(h, n).wait()
        total = jnp.dot(onehot[...], back[h].reshape(owners * cap, part_width), preferred_element_type=F32)
        here_cols = pl.ds(h * part_width, part_width)
        own[:, :, :, here_cols] = total.reshape(nz, ny, depth, part_width)
        ownb[:, :, :, here_cols] = total.astype(BF16).reshape(nz, ny, depth, part_width)
        for j in cols:
            py = lax.rem(y + j, ny)
            first_a[h].append(remote(ownb.at[:, py, :, cols_a(h)], gota.at[h, j - 1], s_a.at[h, j - 1],
                                     r_a.at[h, j - 1], chip(0, j, 0, c)))
        for k in rings:
            pz = lax.rem(z + k, nz)
            first_b[h].append(remote(ownb.at[pz, :, :, cols_b(h)], gotb.at[h, k - 1], s_b.at[h, k - 1],
                                     r_b.at[h, k - 1], chip(0, 0, k, c)))
        for copy in first_a[h] + first_b[h]:
            copy.start()

    def second_rows(h):
        for copy in first_a[h]:
            copy.wait()

        def join_a(q, _):
            total = own[q, y, :, cols_a(h)]
            for j in cols:
                total += gota[h, j - 1, q].astype(F32)
            acca[h, q] = total
            return 0

        lax.fori_loop(0, nz, join_a, 0)
        for k in rings:
            pz = lax.rem(z + k, nz)
            second_a[h].append(remote(acca.at[h, pz], gota2.at[h, k - 1], s_a2.at[h, k - 1], r_a2.at[h, k - 1],
                                      chip(0, 0, k, c)))
        for copy in second_a[h]:
            copy.start()
        for copy in first_b[h]:
            copy.wait()

        def join_b(q, _):
            total = own[z, q, :, cols_b(h)]
            for k in rings:
                total += gotb[h, k - 1, q].astype(F32)
            accb[h, q] = total
            return 0

        lax.fori_loop(0, ny, join_b, 0)
        for j in cols:
            py = lax.rem(y + j, ny)
            second_b[h].append(remote(accb.at[h, py], gotb2.at[h, j - 1], s_b2.at[h, j - 1], r_b2.at[h, j - 1],
                                      chip(0, j, 0, c)))
        for copy in second_b[h]:
            copy.start()

    def finish_rows(h):
        for copy in second_a[h]:
            copy.wait()
        total = acca[h, z]
        for k in rings:
            total += gota2[h, k - 1]
        slab_out[:, cols_a(h)] = total
        for copy in second_b[h]:
            copy.wait()
        total = accb[h, y]
        for j in cols:
            total += gotb2[h, j - 1]
        slab_out[:, cols_b(h)] = total

    sum_rows(0)

    for copy in p1:
        copy.wait()
    rows = pl.ds(pl.multiple_of(here * piece, piece), piece)
    total = enc[c, rows, :] + sib[rows, :]
    for n in range(len(plane)):
        total += gotp[n].astype(F32)
    for k in range(nz):
        shares[k] = total[k * share : (k + 1) * share, :]
    p2, q2 = [], []
    for k in rings:
        pz = lax.rem(z + k, nz)
        p2.append(remote(shares.at[pz], gots.at[k - 1], s_p2.at[k - 1], r_p2.at[k - 1], chip(0, 0, k, c)))
    for copy in p2:
        copy.start()
    for copy in q1:
        copy.wait()
    rows = pl.ds(pl.multiple_of(cut + z * piece, piece), piece)
    total = enc[c, rows, :] + sib[rows, :]
    for k in rings:
        total += gotq[k - 1].astype(F32)
    allx[x] = total
    for i in range(1, nx):
        q2.append(remote(allx.at[x], allx.at[x], s_x.at[i - 1], r_x.at[i - 1], chip(i, 0, 0, c)))
    for copy in q2:
        copy.start()

    second_rows(0)
    for copy in p2:
        copy.wait()
    total = shares[z]
    for k in rings:
        total += gots[k - 1]
    done[z] = total
    p2 = []
    for k in rings:
        p2.append(remote(done.at[z], done.at[z], s_ag.at[k - 1], r_ag.at[k - 1], chip(0, 0, k, c)))
    for copy in p2:
        copy.start()
    for copy in q2:
        copy.wait()
    total = allx[0]
    for i in range(1, nx):
        total += allx[i]
    ally[y] = total
    q2 = []
    for j in cols:
        q2.append(remote(ally.at[y], ally.at[y], s_y.at[j - 1], r_y.at[j - 1], chip(0, j, 0, c)))
    for copy in q2:
        copy.start()

    sum_rows(1)

    p3, q3 = [], []
    for copy in p2:
        copy.wait()
    rows_p = pl.ds(pl.multiple_of(here * piece, piece), piece)
    enc_out[c, rows_p, :] = jnp.concatenate([done[k] for k in range(nz)], axis=0)
    for n, (i, j) in enumerate(plane):
        part = enc_out.at[c, rows_p, :]
        p3.append(remote(part, part, s_p3.at[n], r_p3.at[n], chip(i, j, 0, c)))
    for copy in p3:
        copy.start()
    for copy in q2:
        copy.wait()
    total = ally[0]
    for j in cols:
        total += ally[j]
    rows_q = pl.ds(pl.multiple_of(cut + z * piece, piece), piece)
    enc_out[c, rows_q, :] = total
    for k in rings:
        part = enc_out.at[c, rows_q, :]
        q3.append(remote(part, part, s_q3.at[k - 1], r_q3.at[k - 1], chip(0, 0, k, c)))
    for copy in q3:
        copy.start()

    second_rows(1)
    finish_rows(0)

    def pass_on(first, n):
        part = enc_out.at[c, pl.ds(pl.multiple_of(first, piece), piece), :]
        copy = remote(part, part, s_e.at[n], r_e.at[n], chip(0, 0, 0, 1 - c))
        copy.start()
        return copy

    handed = [pass_on(here * piece, 0), pass_on(cut + z * piece, 1)]
    for k in rings:
        q3[k - 1].wait()
        handed.append(pass_on(cut + lax.rem(z + nz - k, nz) * piece, 1 + k))
    for n, (i, j) in enumerate(plane):
        p3[n].wait()
        source = lax.rem(x + nx - i, nx) * ny + lax.rem(y + ny - j, ny)
        handed.append(pass_on(source * piece, nz + 1 + n))

    finish_rows(1)
    for copy in handed:
        copy.wait()


def body(dims, documents, enc_weight, label_slab, row_scale, shortlist, positive, request_ids, counts):
    nx, ny, nz = dims
    docs, width = documents.shape
    held = label_slab.shape[0]
    owners, cap = request_ids.shape
    picks = shortlist.shape[1]
    plane = nx * ny
    depth = held // (ny * nz)
    part = width // 2
    wide = 2 * part // 3
    slim = part - wide
    half = width // 2
    piece = half // (plane + nz)
    share = piece // nz
    slot_count = owners * cap
    f32 = lambda *shape: pltpu.VMEM(shape, F32)
    b16 = lambda *shape: pltpu.VMEM(shape, BF16)
    i32 = lambda *shape: pltpu.VMEM(shape, I32)
    i16 = lambda *shape: pltpu.VMEM(shape, I16)
    dma = lambda n: [pltpu.SemaphoreType.DMA((n,))] * 2
    two = lambda n: [pltpu.SemaphoreType.DMA((2, n))] * 2
    vmem = pl.BlockSpec(memory_space=pltpu.VMEM)
    slab_grad, enc_grad = pl.pallas_call(
        functools.partial(step_kernel, dims),
        out_shape=(jax.ShapeDtypeStruct((depth, width), F32), jax.ShapeDtypeStruct((2, half, width), F32)),
        in_specs=[pl.BlockSpec(memory_space=pltpu.HBM)] * 8,
        out_specs=[vmem] * 2,
        scratch_shapes=[
            i32(owners, 1, cap), i32(1, owners), b16(held), b16(docs, width), b16(width, width), b16(held, width), i32(picks, docs), i32(picks, docs),
            i16(picks, docs), i16(picks, docs),
            b16(docs, width), f32(docs, width), f32(docs, width), b16(held, slot_count),
            b16(owners, cap, width), b16(owners, cap, width),
            b16(owners, 16, cap), b16(owners, 16, cap), i32(owners, 1, cap),
            i16(slot_count, docs), b16(slot_count, docs),
            b16(2, owners, cap, part), b16(2, owners, cap, part),
            f32(nz, ny, depth, width), b16(nz, ny, depth, width),
            b16(2, ny - 1, nz, depth, wide), b16(2, nz - 1, ny, depth, slim),
            f32(2, nz, depth, wide), f32(2, ny, depth, slim),
            f32(2, nz - 1, depth, wide), f32(2, ny - 1, depth, slim),
            b16(docs, width), f32(2, half, width), f32(half, width),
            b16(plane, piece, width), b16(nz, piece, width),
            b16(plane - 1, piece, width), b16(nz - 1, piece, width),
            f32(nz, share, width), f32(nz - 1, share, width), f32(nz, share, width),
            f32(nx, piece, width), f32(ny, piece, width),
            pltpu.SemaphoreType.DMA((8,)), *dma(owners), *dma(owners), *dma(owners), *two(owners),
            *two(ny - 1), *two(nz - 1), *two(nz - 1), *two(ny - 1),
            pltpu.SemaphoreType.DMA, pltpu.SemaphoreType.DMA,
            *dma(plane - 1), *dma(nz - 1), *dma(nz - 1), *dma(nz - 1), *dma(nx - 1), *dma(ny - 1), *dma(plane - 1), *dma(nz - 1),
            *dma(plane + nz),
        ],
        compiler_params=pltpu.CompilerParams(
            collective_id=1, has_side_effects=True, vmem_limit_bytes=44 * 2**20
        ),
        cost_estimate=pl.CostEstimate(flops=10**10, bytes_accessed=10**7, transcendentals=2 * 10**6),
        name="classifier_step",
    )(*(pltpu.with_memory_space_constraint(operand, pltpu.HBM) for operand in (
        documents,
        enc_weight,
        label_slab,
        row_scale,
        request_ids.reshape(owners, 1, cap),
        shortlist.T,
        positive.T,
        counts,
    )))
    return slab_grad, enc_grad.reshape(width, width)


def solution(mesh):
    return jax.shard_map(
        functools.partial(body, torus(mesh)),
        mesh=mesh,
        in_specs=(
            P(("owner", "dp"), None),
            P(),
            P("owner", None),
            P("owner"),
            P(("owner", "dp"), None),
            P(("owner", "dp"), None),
            P(("owner", "dp"), None),
            P(("owner", "dp"), None),
        ),
        out_specs=(P(("owner", "dp"), None), P()),
        check_vma=False,
    )
```

```python
import functools

import jax
import jax.numpy as jnp
from jax import lax
from jax.experimental import pallas as pl
from jax.experimental.pallas import tpu as pltpu
from jax.sharding import PartitionSpec as P

MESH = pl.DeviceIdType.MESH
F32 = jnp.float32
BF16 = jnp.bfloat16
I32 = jnp.int32
I16 = jnp.int16


def torus(mesh):
    owners, groups = mesh.shape["owner"], mesh.shape["dp"]
    ny = 4 if groups >= 16 else 2
    return owners // 2, ny, groups // ny


def remote(src, dst, send, recv, target):
    return pltpu.make_async_remote_copy(
        src_ref=src, dst_ref=dst, send_sem=send, recv_sem=recv, device_id=target, device_id_type=MESH
    )


def step_kernel(
    dims, docs_in, weight_in, slab_in, scale_in, ids_in, slots_in, on_in, counts_in, slab_out, enc_out,
    ids, counts, scale, docs, weight, slab, slots32, on32, slots, marks, emb, slope, push, onehot, srows, frows, sscale, fscale, gids, tally, dscore, grads0, grads1, back0, back1,
    own, ownb, gota0, gota1, gotb0, gotb1, acca0, acca1, accb0, accb1, gota20, gota21, gotb20, gotb21,
    inner, enc, sib, accp, accq, gotp, gotq, shares, gots, done, allx, ally,
    s_in, s_id, r_id, s_f, r_f, s_c, r_c, s_g, r_g,
    s_a, r_a, s_b, r_b, s_a2, r_a2, s_b2, r_b2,
    s_sib, r_sib, s_p, r_p, s_q, r_q, s_p2, r_p2, s_ag, r_ag, s_x, r_x, s_y, r_y, s_p3, r_p3, s_q3, r_q3, s_e, r_e,
):
    nx, ny, nz = dims
    owner, group = lax.axis_index("owner"), lax.axis_index("dp")
    x, c = owner // 2, owner % 2
    y, z = group % ny, group // ny
    here = x * ny + y
    owners = 2 * nx
    cap = srows.shape[1]
    pair = 2 * cap
    documents, width = docs.shape
    rows_held = slab.shape[0]
    depth = own.shape[-2]
    grads, back = (grads0, grads1), (back0, back1)
    gota, gotb, acca, accb = (gota0, gota1), (gotb0, gotb1), (acca0, acca1), (accb0, accb1)
    gota2, gotb2 = (gota20, gota21), (gotb20, gotb21)
    piece = accp.shape[1]
    share = shares.shape[1]
    half = enc.shape[1]
    cut = nx * ny * piece
    strip = min(128, documents)
    far = nx - 1

    plane = [(i, j) for i in range(nx) for j in range(ny) if (i, j) != (0, 0)]
    rings = list(range(1, nz))
    cols = list(range(1, ny))

    def chip(i, j, k, core):
        return {"owner": lax.rem(x + i, nx) * 2 + core, "dp": lax.rem(z + k, nz) * ny + lax.rem(y + j, ny)}

    def spread(r):
        return r + (r // 2) * (5 - 2 * r) if nx == 4 else r

    loads = [
        pltpu.make_async_copy(src, dst, s_in.at[n])
        for n, (src, dst) in enumerate(
            (
                (docs_in, docs), (weight_in, weight), (slab_in, slab), (slots_in, slots32), (on_in, on32),
                (ids_in, ids), (counts_in, counts), (scale_in, scale),
            )
        )
    ]
    for load in loads[5:] + loads[:5]:
        load.start()

    bar = pltpu.get_barrier_semaphore()
    greeted = 0
    for i, j in plane:
        pl.semaphore_signal(bar, inc=1, device_id=chip(i, j, 0, c), device_id_type=MESH)
        greeted += 1
    for i in range(nx):
        pl.semaphore_signal(bar, inc=1, device_id=chip(i, 0, 0, 1 - c), device_id_type=MESH)
        greeted += 1
    for k in rings:
        pl.semaphore_signal(bar, inc=1, device_id=chip(0, 0, k, c), device_id_type=MESH)
        greeted += 1
    pl.semaphore_wait(bar, greeted)

    def peer(n):
        r, flip = n // 2, n % 2
        core = lax.rem(c + flip, 2)
        to = lax.rem(x + spread(r), nx) * 2 + core
        source = lax.rem(x + nx - spread(r), nx) * 2 + core
        return to, source

    def id_copy(n):
        to, _ = peer(n)
        return remote(ids.at[to], gids.at[owner], s_id.at[n], r_id.at[n], {"owner": to, "dp": group})

    loads[5].wait()
    for n in range(1, owners):
        id_copy(n).start()
    gids[owner] = ids[owner]

    loads[0].wait()
    loads[1].wait()
    squashed = jnp.tanh(jnp.dot(docs[...], weight[...], preferred_element_type=F32))
    emb[...] = (docs[...].astype(F32) + squashed).astype(BF16)
    slope[...] = 1.0 - squashed * squashed
    loads[2].wait()
    loads[6].wait()
    loads[7].wait()

    def row_copy(n):
        to, _ = peer(n)
        return remote(srows.at[to], frows.at[owner], s_f.at[n], r_f.at[n], {"owner": to, "dp": group})

    def scale_copy(n):
        to, _ = peer(n)
        return remote(sscale.at[to], fscale.at[owner], s_c.at[n], r_c.at[n], {"owner": to, "dp": group})

    scale_rows = jnp.broadcast_to(scale[...].reshape(1, rows_held), (16, rows_held))

    def serve(m, _):
        n = lax.rem(m + 2, owners)
        to, _source = peer(n)

        @pl.when(n > 0)
        def _():
            id_copy(n).wait_send()

        hot = jnp.where(
            lax.broadcasted_iota(I32, (rows_held, cap), 0) == gids[to], 1.0, 0.0
        ).astype(BF16)
        onehot[:, pl.ds(pl.multiple_of(to * cap, cap), cap)] = hot
        rows = lax.dot_general(hot, slab[...], (((0,), (0,)), ((), ())), preferred_element_type=F32).astype(BF16)
        sc = jnp.dot(scale_rows, hot, preferred_element_type=F32).astype(BF16)
        srows[to] = rows
        sscale[to] = sc

        @pl.when(n == 0)
        def _():
            frows[owner] = rows
            fscale[owner] = sc

        @pl.when(n > 0)
        def _():
            row_copy(n).start()
            scale_copy(n).start()

        return 0

    for n in range(1, owners):
        id_copy(n).wait_recv()
    lax.fori_loop(0, owners, serve, 0)

    parts = range(2)
    starts, widths = (0, grads0.shape[-1]), (grads0.shape[-1], grads1.shape[-1])

    def grad_copy(h, n):
        _, source = peer(n)
        return remote(
            grads[h].at[source], back[h].at[owner], s_g.at[h, n], r_g.at[h, n], {"owner": source, "dp": group}
        )

    loads[3].wait()
    loads[4].wait()
    slots[...] = slots32[...].astype(I16)
    marks[...] = (1 + 64 * on32[...]).astype(I16)
    strips = documents // strip

    def count(m, _):
        base = pl.multiple_of((m // strips) * pair, pair)
        lanes = pl.ds(pl.multiple_of((m % strips) * strip, strip), strip)
        index = (lax.broadcasted_iota(I32, (pair, strip), 0) + base).astype(I16)
        total = jnp.zeros((pair, strip), I16)
        for k in range(slots.shape[0]):
            total += jnp.where(slots[k : k + 1, lanes] == index, marks[k : k + 1, lanes], jnp.int16(0))
        tally[pl.ds(base, pair), lanes] = total
        return 0

    lax.fori_loop(0, nx * strips, count, 0)

    def group_of(r):
        first = lax.rem(x + nx - spread(r), nx) * 2
        return first, pl.ds(pl.multiple_of(first * cap, pair), pair)

    def score(r):
        first, span = group_of(r)
        rows = frows[pl.ds(first, 2)].reshape(pair, width)
        factor, live = [], []
        for q in range(2):
            line = fscale[first + q].astype(F32)[0:1]
            factor.append(jnp.broadcast_to(line, (cap, cap)).T[:, 0:1])
            lane = lax.broadcasted_iota(I32, (1, owners), 1)
            asked = jnp.sum(jnp.where(lane == first + q, counts[...].astype(F32), 0.0), axis=1, keepdims=True)
            live.append(jnp.where(lax.broadcasted_iota(I32, (cap, 1), 0).astype(F32) < asked, 1.0, 0.0))
        factor = jnp.concatenate(factor, axis=0)
        live = jnp.concatenate(live, axis=0)
        logits = lax.dot_general(rows, emb[...], (((1,), (1,)), ((), ())), preferred_element_type=F32) * factor
        chance = 0.5 * jnp.tanh(0.5 * logits) + 0.5
        mark = tally[span, :].astype(I32)
        hits = (mark & 63).astype(F32)
        on = (mark >> 6).astype(F32)
        dlogit = ((hits + live) * chance - on) * (1.0 / slots.shape[0])
        dscore[span, :] = (dlogit * factor).astype(BF16)

    def row_grads(r):
        first, span = group_of(r)
        product = jnp.dot(dscore[span, :], emb[...], preferred_element_type=F32).astype(BF16)
        for h in parts:
            mine = product[:, starts[h] : starts[h] + widths[h]]
            grads[h][pl.ds(first, 2)] = mine.reshape(2, cap, widths[h])

    def pulled(r):
        first, span = group_of(r)
        rows = frows[pl.ds(first, 2)].reshape(pair, width)
        return lax.dot_general(dscore[span, :], rows, (((0,), (0,)), ((), ())), preferred_element_type=F32)

    def arrived(n):
        row_copy(n).wait()
        scale_copy(n).wait()

    push[...] = jnp.zeros_like(push)

    def work(r, _):
        @pl.when(r > 0)
        def _():
            arrived(2 * r)

        arrived(2 * r + 1)
        score(r)
        row_grads(r)

        @pl.when(r > 0)
        def _():
            grad_copy(0, 2 * r).start()

        grad_copy(0, 2 * r + 1).start()
        push[...] += pulled(r)
        return 0

    lax.fori_loop(0, far, work, 0)
    for h in parts:
        back[h][owner] = grads[h][owner]
    arrived(2 * far)
    arrived(2 * far + 1)
    score(far)
    row_grads(far)
    grad_copy(0, 2 * far).start()
    grad_copy(0, 2 * far + 1).start()

    inner[...] = ((push[...] + pulled(far)) * slope[...]).astype(BF16)

    def outer(which):
        side = docs[:, pl.ds(pl.multiple_of(which * half, half), half)]
        enc[which] = lax.dot_general(side, inner[...], (((0,), (0,)), ((), ())), preferred_element_type=F32)

    outer(1 - c)
    swap = remote(enc.at[1 - c], sib, s_sib, r_sib, chip(0, 0, 0, 1 - c))
    swap.start()
    outer(c)
    swap.wait()

    def join_p(q, _):
        rows = pl.ds(pl.multiple_of(q * piece, piece), piece)
        accp[q] = (enc[c, rows, :] + sib[rows, :]).astype(BF16)
        return 0

    def join_q(q, _):
        rows = pl.ds(pl.multiple_of(cut + q * piece, piece), piece)
        accq[q] = (enc[c, rows, :] + sib[rows, :]).astype(BF16)
        return 0

    lax.fori_loop(0, nx * ny, join_p, 0)
    lax.fori_loop(0, nz, join_q, 0)
    p1, q1 = [], []
    for n, (i, j) in enumerate(plane):
        to = lax.rem(x + i, nx) * ny + lax.rem(y + j, ny)
        p1.append(remote(accp.at[to], gotp.at[n], s_p.at[n], r_p.at[n], chip(i, j, 0, c)))
    for k in rings:
        to = lax.rem(z + k, nz)
        q1.append(remote(accq.at[to], gotq.at[k - 1], s_q.at[k - 1], r_q.at[k - 1], chip(0, 0, k, c)))
    for copy in p1 + q1:
        copy.start()

    for n in range(1, owners):
        grad_copy(1, n).start()

    def cols_a(h):
        return pl.ds(starts[h], gota[h].shape[-1])

    def cols_b(h):
        return pl.ds(starts[h] + gota[h].shape[-1], gotb[h].shape[-1])

    first_a, first_b, second_a, second_b = [[], []], [[], []], [[], []], [[], []]

    def sum_rows(h):
        for n in range(1, owners):
            grad_copy(h, n).wait()
        total = jnp.dot(onehot[...], back[h][...].reshape(owners * cap, widths[h]), preferred_element_type=F32)
        here_cols = pl.ds(starts[h], widths[h])
        own[:, :, :, here_cols] = total.reshape(nz, ny, depth, widths[h])
        ownb[:, :, :, here_cols] = total.astype(BF16).reshape(nz, ny, depth, widths[h])
        for j in cols:
            py = lax.rem(y + j, ny)
            first_a[h].append(remote(ownb.at[:, py, :, cols_a(h)], gota[h].at[j - 1], s_a.at[h, j - 1],
                                     r_a.at[h, j - 1], chip(0, j, 0, c)))
        for k in rings:
            pz = lax.rem(z + k, nz)
            first_b[h].append(remote(ownb.at[pz, :, :, cols_b(h)], gotb[h].at[k - 1], s_b.at[h, k - 1],
                                     r_b.at[h, k - 1], chip(0, 0, k, c)))
        for copy in first_a[h] + first_b[h]:
            copy.start()

    def second_rows(h):
        for copy in first_a[h]:
            copy.wait()

        def join_a(q, _):
            total = own[q, y, :, cols_a(h)]
            for j in cols:
                total += gota[h][j - 1, q].astype(F32)
            acca[h][q] = total
            return 0

        lax.fori_loop(0, nz, join_a, 0)
        for k in rings:
            pz = lax.rem(z + k, nz)
            second_a[h].append(remote(acca[h].at[pz], gota2[h].at[k - 1], s_a2.at[h, k - 1], r_a2.at[h, k - 1],
                                      chip(0, 0, k, c)))
        for copy in second_a[h]:
            copy.start()
        for copy in first_b[h]:
            copy.wait()

        def join_b(q, _):
            total = own[z, q, :, cols_b(h)]
            for k in rings:
                total += gotb[h][k - 1, q].astype(F32)
            accb[h][q] = total
            return 0

        lax.fori_loop(0, ny, join_b, 0)
        for j in cols:
            py = lax.rem(y + j, ny)
            second_b[h].append(remote(accb[h].at[py], gotb2[h].at[j - 1], s_b2.at[h, j - 1], r_b2.at[h, j - 1],
                                      chip(0, j, 0, c)))
        for copy in second_b[h]:
            copy.start()

    def finish_rows(h):
        for copy in second_a[h]:
            copy.wait()
        total = acca[h][z]
        for k in rings:
            total += gota2[h][k - 1]
        slab_out[:, cols_a(h)] = total
        for copy in second_b[h]:
            copy.wait()
        total = accb[h][y]
        for j in cols:
            total += gotb2[h][j - 1]
        slab_out[:, cols_b(h)] = total

    sum_rows(0)

    for copy in p1:
        copy.wait()
    rows = pl.ds(pl.multiple_of(here * piece, piece), piece)
    total = enc[c, rows, :] + sib[rows, :]
    for n in range(len(plane)):
        total += gotp[n].astype(F32)
    for k in range(nz):
        shares[k] = total[k * share : (k + 1) * share, :]
    p2, q2 = [], []
    for k in rings:
        pz = lax.rem(z + k, nz)
        p2.append(remote(shares.at[pz], gots.at[k - 1], s_p2.at[k - 1], r_p2.at[k - 1], chip(0, 0, k, c)))
    for copy in p2:
        copy.start()
    for copy in q1:
        copy.wait()
    rows = pl.ds(pl.multiple_of(cut + z * piece, piece), piece)
    total = enc[c, rows, :] + sib[rows, :]
    for k in rings:
        total += gotq[k - 1].astype(F32)
    allx[x] = total
    for i in range(1, nx):
        q2.append(remote(allx.at[x], allx.at[x], s_x.at[i - 1], r_x.at[i - 1], chip(i, 0, 0, c)))
    for copy in q2:
        copy.start()

    second_rows(0)
    for copy in p2:
        copy.wait()
    total = shares[z]
    for k in rings:
        total += gots[k - 1]
    done[z] = total
    p2 = []
    for k in rings:
        p2.append(remote(done.at[z], done.at[z], s_ag.at[k - 1], r_ag.at[k - 1], chip(0, 0, k, c)))
    for copy in p2:
        copy.start()
    for copy in q2:
        copy.wait()
    total = allx[0]
    for i in range(1, nx):
        total += allx[i]
    ally[y] = total
    q2 = []
    for j in cols:
        q2.append(remote(ally.at[y], ally.at[y], s_y.at[j - 1], r_y.at[j - 1], chip(0, j, 0, c)))
    for copy in q2:
        copy.start()

    sum_rows(1)

    p3, q3 = [], []
    for copy in p2:
        copy.wait()
    rows_p = pl.ds(pl.multiple_of(here * piece, piece), piece)
    enc_out[c, rows_p, :] = jnp.concatenate([done[k] for k in range(nz)], axis=0)
    for n, (i, j) in enumerate(plane):
        part = enc_out.at[c, rows_p, :]
        p3.append(remote(part, part, s_p3.at[n], r_p3.at[n], chip(i, j, 0, c)))
    for copy in p3:
        copy.start()
    for copy in q2:
        copy.wait()
    total = ally[0]
    for j in cols:
        total += ally[j]
    rows_q = pl.ds(pl.multiple_of(cut + z * piece, piece), piece)
    enc_out[c, rows_q, :] = total
    for k in rings:
        part = enc_out.at[c, rows_q, :]
        q3.append(remote(part, part, s_q3.at[k - 1], r_q3.at[k - 1], chip(0, 0, k, c)))
    for copy in q3:
        copy.start()

    second_rows(1)
    finish_rows(0)

    def pass_on(first, n):
        part = enc_out.at[c, pl.ds(pl.multiple_of(first, piece), piece), :]
        copy = remote(part, part, s_e.at[n], r_e.at[n], chip(0, 0, 0, 1 - c))
        copy.start()
        return copy

    handed = [pass_on(here * piece, 0), pass_on(cut + z * piece, 1)]
    for k in rings:
        q3[k - 1].wait()
        handed.append(pass_on(cut + lax.rem(z + nz - k, nz) * piece, 1 + k))
    for n, (i, j) in enumerate(plane):
        p3[n].wait()
        source = lax.rem(x + nx - i, nx) * ny + lax.rem(y + ny - j, ny)
        handed.append(pass_on(source * piece, nz + 1 + n))

    finish_rows(1)
    for copy in handed:
        copy.wait()


def body(dims, documents, enc_weight, label_slab, row_scale, shortlist, positive, request_ids, counts):
    nx, ny, nz = dims
    docs, width = documents.shape
    held = label_slab.shape[0]
    owners, cap = request_ids.shape
    picks = shortlist.shape[1]
    plane = nx * ny
    depth = held // (ny * nz)
    parts = (2 * width // 3, width // 3)
    half = width // 2
    piece = half // (plane + nz)
    share = piece // nz
    slot_count = owners * cap
    f32 = lambda *shape: pltpu.VMEM(shape, F32)
    b16 = lambda *shape: pltpu.VMEM(shape, BF16)
    i32 = lambda *shape: pltpu.VMEM(shape, I32)
    i16 = lambda *shape: pltpu.VMEM(shape, I16)
    dma = lambda n: [pltpu.SemaphoreType.DMA((n,))] * 2
    two = lambda n: [pltpu.SemaphoreType.DMA((2, n))] * 2
    vmem = pl.BlockSpec(memory_space=pltpu.VMEM)
    slab_grad, enc_grad = pl.pallas_call(
        functools.partial(step_kernel, dims),
        out_shape=(jax.ShapeDtypeStruct((depth, width), F32), jax.ShapeDtypeStruct((2, half, width), F32)),
        in_specs=[pl.BlockSpec(memory_space=pltpu.HBM)] * 8,
        out_specs=[vmem] * 2,
        scratch_shapes=[
            i32(owners, 1, cap), i32(1, owners), b16(held), b16(docs, width), b16(width, width), b16(held, width), i32(picks, docs), i32(picks, docs),
            i16(picks, docs), i16(picks, docs),
            b16(docs, width), f32(docs, width), f32(docs, width), b16(held, slot_count),
            b16(owners, cap, width), b16(owners, cap, width),
            b16(owners, 16, cap), b16(owners, 16, cap), i32(owners, 1, cap),
            i16(slot_count, docs), b16(slot_count, docs),
            *(b16(owners, cap, p) for p in parts), *(b16(owners, cap, p) for p in parts),
            f32(nz, ny, depth, width), b16(nz, ny, depth, width),
            *(b16(ny - 1, nz, depth, p // 2) for p in parts), *(b16(nz - 1, ny, depth, p // 2) for p in parts),
            *(f32(nz, depth, p // 2) for p in parts), *(f32(ny, depth, p // 2) for p in parts),
            *(f32(nz - 1, depth, p // 2) for p in parts), *(f32(ny - 1, depth, p // 2) for p in parts),
            b16(docs, width), f32(2, half, width), f32(half, width),
            b16(plane, piece, width), b16(nz, piece, width),
            b16(plane - 1, piece, width), b16(nz - 1, piece, width),
            f32(nz, share, width), f32(nz - 1, share, width), f32(nz, share, width),
            f32(nx, piece, width), f32(ny, piece, width),
            pltpu.SemaphoreType.DMA((8,)), *dma(owners), *dma(owners), *dma(owners), *two(owners),
            *two(ny - 1), *two(nz - 1), *two(nz - 1), *two(ny - 1),
            pltpu.SemaphoreType.DMA, pltpu.SemaphoreType.DMA,
            *dma(plane - 1), *dma(nz - 1), *dma(nz - 1), *dma(nz - 1), *dma(nx - 1), *dma(ny - 1), *dma(plane - 1), *dma(nz - 1),
            *dma(plane + nz),
        ],
        compiler_params=pltpu.CompilerParams(
            collective_id=1, has_side_effects=True, vmem_limit_bytes=44 * 2**20
        ),
        cost_estimate=pl.CostEstimate(flops=10**10, bytes_accessed=10**7, transcendentals=2 * 10**6),
        name="classifier_step",
    )(*(pltpu.with_memory_space_constraint(operand, pltpu.HBM) for operand in (
        documents,
        enc_weight,
        label_slab,
        row_scale,
        request_ids.reshape(owners, 1, cap),
        shortlist.T,
        positive.T,
        counts,
    )))
    return slab_grad, enc_grad.reshape(width, width)


def solution(mesh):
    return jax.shard_map(
        functools.partial(body, torus(mesh)),
        mesh=mesh,
        in_specs=(
            P(("owner", "dp"), None),
            P(),
            P("owner", None),
            P("owner"),
            P(("owner", "dp"), None),
            P(("owner", "dp"), None),
            P(("owner", "dp"), None),
            P(("owner", "dp"), None),
        ),
        out_specs=(P(("owner", "dp"), None), P()),
        check_vma=False,
    )
```

```python
import functools

import jax
import jax.numpy as jnp
from jax import lax
from jax.experimental import pallas as pl
from jax.experimental.pallas import tpu as pltpu
from jax.sharding import PartitionSpec as P

MESH = pl.DeviceIdType.MESH
F32 = jnp.float32
BF16 = jnp.bfloat16
I32 = jnp.int32
I16 = jnp.int16


def torus(mesh):
    owners, groups = mesh.shape["owner"], mesh.shape["dp"]
    ny = 4 if groups >= 16 else 2
    return owners // 2, ny, groups // ny


def remote(src, dst, send, recv, target):
    return pltpu.make_async_remote_copy(
        src_ref=src, dst_ref=dst, send_sem=send, recv_sem=recv, device_id=target, device_id_type=MESH
    )


def step_kernel(
    dims, docs_in, weight_in, slab_in, scale_in, ids_in, slots_in, on_in, counts_in, slab_out, enc_out,
    ids, counts, scale, docs, weight, slab, slots32, on32, slots, marks, emb, slope, push, onehot, srows, frows, sscale, fscale, gids, tally, dscore, grads0, grads1, back0, back1,
    own, ownb, gota0, gota1, gotb0, gotb1, acca0, acca1, accb0, accb1, gota20, gota21, gotb20, gotb21,
    inner, sinner, sdocs, enc, accp, accq, gotp, gotq, shares, gots, done, allx, ally,
    s_in, s_id, r_id, s_f, r_f, s_c, r_c, s_g, r_g,
    s_a, r_a, s_b, r_b, s_a2, r_a2, s_b2, r_b2,
    s_sib, r_sib, s_doc, r_doc, s_p, r_p, s_q, r_q, s_p2, r_p2, s_ag, r_ag, s_x, r_x, s_y, r_y, s_p3, r_p3, s_q3, r_q3, s_e, r_e,
):
    nx, ny, nz = dims
    owner, group = lax.axis_index("owner"), lax.axis_index("dp")
    x, c = owner // 2, owner % 2
    y, z = group % ny, group // ny
    here = x * ny + y
    owners = 2 * nx
    cap = srows.shape[1]
    pair = 2 * cap
    documents, width = docs.shape
    rows_held = slab.shape[0]
    depth = own.shape[-2]
    grads, back = (grads0, grads1), (back0, back1)
    gota, gotb, acca, accb = (gota0, gota1), (gotb0, gotb1), (acca0, acca1), (accb0, accb1)
    gota2, gotb2 = (gota20, gota21), (gotb20, gotb21)
    piece = accp.shape[1]
    share = shares.shape[1]
    mid = enc.shape[1]
    cut = nx * ny * piece
    strip = min(128, documents)
    far = nx - 1

    plane = [(i, j) for i in range(nx) for j in range(ny) if (i, j) != (0, 0)]
    rings = list(range(1, nz))
    cols = list(range(1, ny))

    def chip(i, j, k, core):
        return {"owner": lax.rem(x + i, nx) * 2 + core, "dp": lax.rem(z + k, nz) * ny + lax.rem(y + j, ny)}

    def spread(r):
        return r + (r // 2) * (5 - 2 * r) if nx == 4 else r

    loads = [
        pltpu.make_async_copy(src, dst, s_in.at[n])
        for n, (src, dst) in enumerate(
            (
                (docs_in, docs), (weight_in, weight), (slab_in, slab), (slots_in, slots32), (on_in, on32),
                (ids_in, ids), (counts_in, counts), (scale_in, scale),
            )
        )
    ]
    for load in loads[5:] + loads[:5]:
        load.start()

    bar = pltpu.get_barrier_semaphore()
    greeted = 0
    for i, j in plane:
        pl.semaphore_signal(bar, inc=1, device_id=chip(i, j, 0, c), device_id_type=MESH)
        greeted += 1
    for i in range(nx):
        pl.semaphore_signal(bar, inc=1, device_id=chip(i, 0, 0, 1 - c), device_id_type=MESH)
        greeted += 1
    for k in rings:
        pl.semaphore_signal(bar, inc=1, device_id=chip(0, 0, k, c), device_id_type=MESH)
        greeted += 1
    pl.semaphore_wait(bar, greeted)

    def peer(n):
        r, flip = n // 2, n % 2
        core = lax.rem(c + flip, 2)
        to = lax.rem(x + spread(r), nx) * 2 + core
        source = lax.rem(x + nx - spread(r), nx) * 2 + core
        return to, source

    def id_copy(n):
        to, _ = peer(n)
        return remote(ids.at[to], gids.at[owner], s_id.at[n], r_id.at[n], {"owner": to, "dp": group})

    loads[5].wait()
    for n in range(1, owners):
        id_copy(n).start()
    gids[owner] = ids[owner]

    loads[0].wait()
    mate = remote(docs, sdocs, s_doc, r_doc, chip(0, 0, 0, 1 - c))
    mate.start()
    loads[1].wait()
    squashed = jnp.tanh(jnp.dot(docs[...], weight[...], preferred_element_type=F32))
    emb[...] = (docs[...].astype(F32) + squashed).astype(BF16)
    slope[...] = 1.0 - squashed * squashed
    loads[2].wait()
    loads[6].wait()
    loads[7].wait()

    def row_copy(n):
        to, _ = peer(n)
        return remote(srows.at[to], frows.at[owner], s_f.at[n], r_f.at[n], {"owner": to, "dp": group})

    def scale_copy(n):
        to, _ = peer(n)
        return remote(sscale.at[to], fscale.at[owner], s_c.at[n], r_c.at[n], {"owner": to, "dp": group})

    scale_rows = jnp.broadcast_to(scale[...].reshape(1, rows_held), (16, rows_held))

    def serve(m, _):
        n = lax.rem(m + 2, owners)
        to, _source = peer(n)

        @pl.when(n > 0)
        def _():
            id_copy(n).wait_send()

        hot = jnp.where(
            lax.broadcasted_iota(I32, (rows_held, cap), 0) == gids[to], 1.0, 0.0
        ).astype(BF16)
        onehot[:, pl.ds(pl.multiple_of(to * cap, cap), cap)] = hot
        rows = lax.dot_general(hot, slab[...], (((0,), (0,)), ((), ())), preferred_element_type=F32).astype(BF16)
        sc = jnp.dot(scale_rows, hot, preferred_element_type=F32).astype(BF16)
        srows[to] = rows
        sscale[to] = sc

        @pl.when(n == 0)
        def _():
            frows[owner] = rows
            fscale[owner] = sc

        @pl.when(n > 0)
        def _():
            row_copy(n).start()
            scale_copy(n).start()

        return 0

    for n in range(1, owners):
        id_copy(n).wait_recv()
    lax.fori_loop(0, owners, serve, 0)

    parts = range(2)
    starts, widths = (0, grads0.shape[-1]), (grads0.shape[-1], grads1.shape[-1])

    def grad_copy(h, n):
        _, source = peer(n)
        return remote(
            grads[h].at[source], back[h].at[owner], s_g.at[h, n], r_g.at[h, n], {"owner": source, "dp": group}
        )

    loads[3].wait()
    loads[4].wait()
    slots[...] = slots32[...].astype(I16)
    marks[...] = (1 + 64 * on32[...]).astype(I16)
    strips = documents // strip

    def count(m, _):
        base = pl.multiple_of((m // strips) * pair, pair)
        lanes = pl.ds(pl.multiple_of((m % strips) * strip, strip), strip)
        index = (lax.broadcasted_iota(I32, (pair, strip), 0) + base).astype(I16)
        total = jnp.zeros((pair, strip), I16)
        for k in range(slots.shape[0]):
            total += jnp.where(slots[k : k + 1, lanes] == index, marks[k : k + 1, lanes], jnp.int16(0))
        tally[pl.ds(base, pair), lanes] = total
        return 0

    lax.fori_loop(0, nx * strips, count, 0)

    def group_of(r):
        first = lax.rem(x + nx - spread(r), nx) * 2
        return first, pl.ds(pl.multiple_of(first * cap, pair), pair)

    def score(r):
        first, span = group_of(r)
        rows = frows[pl.ds(first, 2)].reshape(pair, width)
        factor, live = [], []
        for q in range(2):
            line = fscale[first + q].astype(F32)[0:1]
            factor.append(jnp.broadcast_to(line, (cap, cap)).T[:, 0:1])
            lane = lax.broadcasted_iota(I32, (1, owners), 1)
            asked = jnp.sum(jnp.where(lane == first + q, counts[...].astype(F32), 0.0), axis=1, keepdims=True)
            live.append(jnp.where(lax.broadcasted_iota(I32, (cap, 1), 0).astype(F32) < asked, 1.0, 0.0))
        factor = jnp.concatenate(factor, axis=0)
        live = jnp.concatenate(live, axis=0)
        logits = lax.dot_general(rows, emb[...], (((1,), (1,)), ((), ())), preferred_element_type=F32) * factor
        chance = 0.5 * jnp.tanh(0.5 * logits) + 0.5
        mark = tally[span, :].astype(I32)
        hits = (mark & 63).astype(F32)
        on = (mark >> 6).astype(F32)
        dlogit = ((hits + live) * chance - on) * (1.0 / slots.shape[0])
        dscore[span, :] = (dlogit * factor).astype(BF16)

    def row_grads(r):
        first, span = group_of(r)
        product = jnp.dot(dscore[span, :], emb[...], preferred_element_type=F32).astype(BF16)
        for h in parts:
            mine = product[:, starts[h] : starts[h] + widths[h]]
            grads[h][pl.ds(first, 2)] = mine.reshape(2, cap, widths[h])

    def pulled(r):
        first, span = group_of(r)
        rows = frows[pl.ds(first, 2)].reshape(pair, width)
        return lax.dot_general(dscore[span, :], rows, (((0,), (0,)), ((), ())), preferred_element_type=F32)

    def arrived(n):
        row_copy(n).wait()
        scale_copy(n).wait()

    push[...] = jnp.zeros_like(push)

    def work(r, _):
        @pl.when(r > 0)
        def _():
            arrived(2 * r)

        arrived(2 * r + 1)
        score(r)
        row_grads(r)

        @pl.when(r > 0)
        def _():
            grad_copy(0, 2 * r).start()

        grad_copy(0, 2 * r + 1).start()
        push[...] += pulled(r)
        return 0

    lax.fori_loop(0, far, work, 0)
    for h in parts:
        back[h][owner] = grads[h][owner]
    arrived(2 * far)
    arrived(2 * far + 1)
    score(far)
    row_grads(far)
    grad_copy(0, 2 * far).start()
    grad_copy(0, 2 * far + 1).start()

    def finish_inner(which):
        first, span = group_of(far)
        lanes = pl.ds(pl.multiple_of(which * mid, mid), mid)
        rows = frows[pl.ds(first, 2), :, lanes].reshape(pair, mid)
        last = lax.dot_general(dscore[span, :], rows, (((0,), (0,)), ((), ())), preferred_element_type=F32)
        inner[which] = ((push[:, lanes] + last) * slope[:, lanes]).astype(BF16)

    def outer(side, other):
        return lax.dot_general(side[...], other, (((0,), (0,)), ((), ())), preferred_element_type=F32)

    finish_inner(1 - c)
    swap = remote(inner.at[1 - c], sinner, s_sib, r_sib, chip(0, 0, 0, 1 - c))
    swap.start()
    finish_inner(c)
    enc[...] = outer(docs, inner[c])
    swap.wait()
    mate.wait()
    enc[...] += outer(sdocs, sinner[...])

    def summed(first):
        return enc[pl.ds(pl.multiple_of(first, piece), piece), :]

    def join_p(q, _):
        accp[q] = summed(q * piece).astype(BF16)
        return 0

    def join_q(q, _):
        accq[q] = summed(cut + q * piece).astype(BF16)
        return 0

    lax.fori_loop(0, nx * ny, join_p, 0)
    lax.fori_loop(0, nz, join_q, 0)
    p1, q1 = [], []
    for n, (i, j) in enumerate(plane):
        to = lax.rem(x + i, nx) * ny + lax.rem(y + j, ny)
        p1.append(remote(accp.at[to], gotp.at[n], s_p.at[n], r_p.at[n], chip(i, j, 0, c)))
    for k in rings:
        to = lax.rem(z + k, nz)
        q1.append(remote(accq.at[to], gotq.at[k - 1], s_q.at[k - 1], r_q.at[k - 1], chip(0, 0, k, c)))
    for copy in p1 + q1:
        copy.start()

    for n in range(1, owners):
        grad_copy(1, n).start()

    def cols_a(h):
        return pl.ds(starts[h], gota[h].shape[-1])

    def cols_b(h):
        return pl.ds(starts[h] + gota[h].shape[-1], gotb[h].shape[-1])

    first_a, first_b, second_a, second_b = [[], []], [[], []], [[], []], [[], []]

    def sum_rows(h):
        for n in range(1, owners):
            grad_copy(h, n).wait()
        total = jnp.dot(onehot[...], back[h][...].reshape(owners * cap, widths[h]), preferred_element_type=F32)
        here_cols = pl.ds(starts[h], widths[h])
        own[:, :, :, here_cols] = total.reshape(nz, ny, depth, widths[h])
        ownb[:, :, :, here_cols] = total.astype(BF16).reshape(nz, ny, depth, widths[h])
        for j in cols:
            py = lax.rem(y + j, ny)
            first_a[h].append(remote(ownb.at[:, py, :, cols_a(h)], gota[h].at[j - 1], s_a.at[h, j - 1],
                                     r_a.at[h, j - 1], chip(0, j, 0, c)))
        for k in rings:
            pz = lax.rem(z + k, nz)
            first_b[h].append(remote(ownb.at[pz, :, :, cols_b(h)], gotb[h].at[k - 1], s_b.at[h, k - 1],
                                     r_b.at[h, k - 1], chip(0, 0, k, c)))
        for copy in first_a[h] + first_b[h]:
            copy.start()

    def second_rows(h):
        for copy in first_a[h]:
            copy.wait()

        def join_a(q, _):
            total = own[q, y, :, cols_a(h)]
            for j in cols:
                total += gota[h][j - 1, q].astype(F32)
            acca[h][q] = total
            return 0

        lax.fori_loop(0, nz, join_a, 0)
        for k in rings:
            pz = lax.rem(z + k, nz)
            second_a[h].append(remote(acca[h].at[pz], gota2[h].at[k - 1], s_a2.at[h, k - 1], r_a2.at[h, k - 1],
                                      chip(0, 0, k, c)))
        for copy in second_a[h]:
            copy.start()
        for copy in first_b[h]:
            copy.wait()

        def join_b(q, _):
            total = own[z, q, :, cols_b(h)]
            for k in rings:
                total += gotb[h][k - 1, q].astype(F32)
            accb[h][q] = total
            return 0

        lax.fori_loop(0, ny, join_b, 0)
        for j in cols:
            py = lax.rem(y + j, ny)
            second_b[h].append(remote(accb[h].at[py], gotb2[h].at[j - 1], s_b2.at[h, j - 1], r_b2.at[h, j - 1],
                                      chip(0, j, 0, c)))
        for copy in second_b[h]:
            copy.start()

    def finish_rows(h):
        for copy in second_a[h]:
            copy.wait()
        total = acca[h][z]
        for k in rings:
            total += gota2[h][k - 1]
        slab_out[:, cols_a(h)] = total
        for copy in second_b[h]:
            copy.wait()
        total = accb[h][y]
        for j in cols:
            total += gotb2[h][j - 1]
        slab_out[:, cols_b(h)] = total

    sum_rows(0)

    for copy in p1:
        copy.wait()
    total = summed(here * piece)
    for n in range(len(plane)):
        total += gotp[n].astype(F32)
    for k in range(nz):
        shares[k] = total[k * share : (k + 1) * share, :]
    p2, q2 = [], []
    for k in rings:
        pz = lax.rem(z + k, nz)
        p2.append(remote(shares.at[pz], gots.at[k - 1], s_p2.at[k - 1], r_p2.at[k - 1], chip(0, 0, k, c)))
    for copy in p2:
        copy.start()
    for copy in q1:
        copy.wait()
    total = summed(cut + z * piece)
    for k in rings:
        total += gotq[k - 1].astype(F32)
    allx[x] = total
    for i in range(1, nx):
        q2.append(remote(allx.at[x], allx.at[x], s_x.at[i - 1], r_x.at[i - 1], chip(i, 0, 0, c)))
    for copy in q2:
        copy.start()

    second_rows(0)
    for copy in p2:
        copy.wait()
    total = shares[z]
    for k in rings:
        total += gots[k - 1]
    done[z] = total
    p2 = []
    for k in rings:
        p2.append(remote(done.at[z], done.at[z], s_ag.at[k - 1], r_ag.at[k - 1], chip(0, 0, k, c)))
    for copy in p2:
        copy.start()
    for copy in q2:
        copy.wait()
    total = allx[0]
    for i in range(1, nx):
        total += allx[i]
    ally[y] = total
    q2 = []
    for j in cols:
        q2.append(remote(ally.at[y], ally.at[y], s_y.at[j - 1], r_y.at[j - 1], chip(0, j, 0, c)))
    for copy in q2:
        copy.start()

    sum_rows(1)

    p3, q3 = [], []
    for copy in p2:
        copy.wait()
    side = pl.ds(pl.multiple_of(c * mid, mid), mid)
    rows_p = pl.ds(pl.multiple_of(here * piece, piece), piece)
    enc_out[rows_p, side] = jnp.concatenate([done[k] for k in range(nz)], axis=0)
    for n, (i, j) in enumerate(plane):
        part = enc_out.at[rows_p, side]
        p3.append(remote(part, part, s_p3.at[n], r_p3.at[n], chip(i, j, 0, c)))
    for copy in p3:
        copy.start()
    for copy in q2:
        copy.wait()
    total = ally[0]
    for j in cols:
        total += ally[j]
    rows_q = pl.ds(pl.multiple_of(cut + z * piece, piece), piece)
    enc_out[rows_q, side] = total
    for k in rings:
        part = enc_out.at[rows_q, side]
        q3.append(remote(part, part, s_q3.at[k - 1], r_q3.at[k - 1], chip(0, 0, k, c)))
    for copy in q3:
        copy.start()

    second_rows(1)
    finish_rows(0)

    def pass_on(first, n):
        part = enc_out.at[pl.ds(pl.multiple_of(first, piece), piece), side]
        copy = remote(part, part, s_e.at[n], r_e.at[n], chip(0, 0, 0, 1 - c))
        copy.start()
        return copy

    handed = [pass_on(here * piece, 0), pass_on(cut + z * piece, 1)]
    for k in rings:
        q3[k - 1].wait()
        handed.append(pass_on(cut + lax.rem(z + nz - k, nz) * piece, 1 + k))
    for n, (i, j) in enumerate(plane):
        p3[n].wait()
        source = lax.rem(x + nx - i, nx) * ny + lax.rem(y + ny - j, ny)
        handed.append(pass_on(source * piece, nz + 1 + n))

    finish_rows(1)
    for copy in handed:
        copy.wait()


def body(dims, documents, enc_weight, label_slab, row_scale, shortlist, positive, request_ids, counts):
    nx, ny, nz = dims
    docs, width = documents.shape
    held = label_slab.shape[0]
    owners, cap = request_ids.shape
    picks = shortlist.shape[1]
    plane = nx * ny
    depth = held // (ny * nz)
    parts = (2 * width // 3, width // 3)
    mid = width // 2
    piece = width // (plane + nz)
    share = piece // nz
    slot_count = owners * cap
    f32 = lambda *shape: pltpu.VMEM(shape, F32)
    b16 = lambda *shape: pltpu.VMEM(shape, BF16)
    i32 = lambda *shape: pltpu.VMEM(shape, I32)
    i16 = lambda *shape: pltpu.VMEM(shape, I16)
    dma = lambda n: [pltpu.SemaphoreType.DMA((n,))] * 2
    two = lambda n: [pltpu.SemaphoreType.DMA((2, n))] * 2
    vmem = pl.BlockSpec(memory_space=pltpu.VMEM)
    slab_grad, enc_grad = pl.pallas_call(
        functools.partial(step_kernel, dims),
        out_shape=(jax.ShapeDtypeStruct((depth, width), F32), jax.ShapeDtypeStruct((width, width), F32)),
        in_specs=[pl.BlockSpec(memory_space=pltpu.HBM)] * 8,
        out_specs=[vmem] * 2,
        scratch_shapes=[
            i32(owners, 1, cap), i32(1, owners), b16(held), b16(docs, width), b16(width, width), b16(held, width), i32(picks, docs), i32(picks, docs),
            i16(picks, docs), i16(picks, docs),
            b16(docs, width), f32(docs, width), f32(docs, width), b16(held, slot_count),
            b16(owners, cap, width), b16(owners, cap, width),
            b16(owners, 16, cap), b16(owners, 16, cap), i32(owners, 1, cap),
            i16(slot_count, docs), b16(slot_count, docs),
            *(b16(owners, cap, p) for p in parts), *(b16(owners, cap, p) for p in parts),
            f32(nz, ny, depth, width), b16(nz, ny, depth, width),
            *(b16(ny - 1, nz, depth, p // 2) for p in parts), *(b16(nz - 1, ny, depth, p // 2) for p in parts),
            *(f32(nz, depth, p // 2) for p in parts), *(f32(ny, depth, p // 2) for p in parts),
            *(f32(nz - 1, depth, p // 2) for p in parts), *(f32(ny - 1, depth, p // 2) for p in parts),
            b16(2, docs, mid), b16(docs, mid), b16(docs, width), f32(width, mid),
            b16(plane, piece, mid), b16(nz, piece, mid),
            b16(plane - 1, piece, mid), b16(nz - 1, piece, mid),
            f32(nz, share, mid), f32(nz - 1, share, mid), f32(nz, share, mid),
            f32(nx, piece, mid), f32(ny, piece, mid),
            pltpu.SemaphoreType.DMA((8,)), *dma(owners), *dma(owners), *dma(owners), *two(owners),
            *two(ny - 1), *two(nz - 1), *two(nz - 1), *two(ny - 1),
            pltpu.SemaphoreType.DMA, pltpu.SemaphoreType.DMA,
            pltpu.SemaphoreType.DMA, pltpu.SemaphoreType.DMA,
            *dma(plane - 1), *dma(nz - 1), *dma(nz - 1), *dma(nz - 1), *dma(nx - 1), *dma(ny - 1), *dma(plane - 1), *dma(nz - 1),
            *dma(plane + nz),
        ],
        compiler_params=pltpu.CompilerParams(
            collective_id=1, has_side_effects=True, vmem_limit_bytes=44 * 2**20
        ),
        cost_estimate=pl.CostEstimate(flops=10**10, bytes_accessed=10**7, transcendentals=2 * 10**6),
        name="classifier_step",
    )(*(pltpu.with_memory_space_constraint(operand, pltpu.HBM) for operand in (
        documents,
        enc_weight,
        label_slab,
        row_scale,
        request_ids.reshape(owners, 1, cap),
        shortlist.T,
        positive.T,
        counts,
    )))
    return slab_grad, enc_grad


def solution(mesh):
    return jax.shard_map(
        functools.partial(body, torus(mesh)),
        mesh=mesh,
        in_specs=(
            P(("owner", "dp"), None),
            P(),
            P("owner", None),
            P("owner"),
            P(("owner", "dp"), None),
            P(("owner", "dp"), None),
            P(("owner", "dp"), None),
            P(("owner", "dp"), None),
        ),
        out_specs=(P(("owner", "dp"), None), P()),
        check_vma=False,
    )
```

```python
import functools

import jax
import jax.numpy as jnp
from jax import lax
from jax.experimental import pallas as pl
from jax.experimental.pallas import tpu as pltpu
from jax.sharding import PartitionSpec as P

MESH = pl.DeviceIdType.MESH
F32 = jnp.float32
BF16 = jnp.bfloat16
I32 = jnp.int32
I16 = jnp.int16


def torus(mesh):
    owners, groups = mesh.shape["owner"], mesh.shape["dp"]
    ny = 4 if groups >= 16 else 2
    return owners // 2, ny, groups // ny


def remote(src, dst, send, recv, target):
    return pltpu.make_async_remote_copy(
        src_ref=src, dst_ref=dst, send_sem=send, recv_sem=recv, device_id=target, device_id_type=MESH
    )


def step_kernel(
    dims, docs_in, weight_in, slab_in, scale_in, ids_in, slots_in, on_in, counts_in, slab_out, enc_out,
    ids, counts, scale, docs, weight, slab, slots32, on32, slots, marks, emb, slope, push, onehot, srows, frows, sscale, fscale, gids, tally, dscore, grads0, grads1, back0, back1,
    own, ownb, gota0, gota1, gotb0, gotb1, acca0, acca1, accb0, accb1, gota20, gota21, gotb20, gotb21,
    inner, sinner, sdocs, enc, accp, accq, gotp, gotq, shares, gots, done, allx, ally,
    s_in, s_id, r_id, s_f, r_f, s_c, r_c, s_g, r_g,
    s_a, r_a, s_b, r_b, s_a2, r_a2, s_b2, r_b2,
    s_sib, r_sib, s_doc, r_doc, s_p, r_p, s_q, r_q, s_p2, r_p2, s_ag, r_ag, s_x, r_x, s_y, r_y, s_p3, r_p3, s_q3, r_q3, s_e, r_e,
):
    nx, ny, nz = dims
    owner, group = lax.axis_index("owner"), lax.axis_index("dp")
    x, c = owner // 2, owner % 2
    y, z = group % ny, group // ny
    here = x * ny + y
    owners = 2 * nx
    cap = srows.shape[1]
    pair = 2 * cap
    documents, width = docs.shape
    rows_held = slab.shape[0]
    depth = own.shape[-2]
    grads, back = (grads0, grads1), (back0, back1)
    gota, gotb, acca, accb = (gota0, gota1), (gotb0, gotb1), (acca0, acca1), (accb0, accb1)
    gota2, gotb2 = (gota20, gota21), (gotb20, gotb21)
    piece = accp.shape[1]
    share = shares.shape[1]
    mid = enc.shape[1]
    cut = nx * ny * piece
    strip = min(128, documents)
    far = nx - 1

    plane = [(i, j) for i in range(nx) for j in range(ny) if (i, j) != (0, 0)]
    rings = list(range(1, nz))
    cols = list(range(1, ny))

    def chip(i, j, k, core):
        return {"owner": lax.rem(x + i, nx) * 2 + core, "dp": lax.rem(z + k, nz) * ny + lax.rem(y + j, ny)}

    def spread(r):
        return r + (r // 2) * (5 - 2 * r) if nx == 4 else r

    loads = [
        pltpu.make_async_copy(src, dst, s_in.at[n])
        for n, (src, dst) in enumerate(
            (
                (docs_in, docs), (weight_in, weight), (slab_in, slab), (slots_in, slots32), (on_in, on32),
                (ids_in, ids), (counts_in, counts), (scale_in, scale),
            )
        )
    ]
    for load in loads[5:] + loads[:5]:
        load.start()

    bar = pltpu.get_barrier_semaphore()
    greeted = 0
    for i, j in plane:
        pl.semaphore_signal(bar, inc=1, device_id=chip(i, j, 0, c), device_id_type=MESH)
        greeted += 1
    for i in range(nx):
        pl.semaphore_signal(bar, inc=1, device_id=chip(i, 0, 0, 1 - c), device_id_type=MESH)
        greeted += 1
    for k in rings:
        pl.semaphore_signal(bar, inc=1, device_id=chip(0, 0, k, c), device_id_type=MESH)
        greeted += 1
    pl.semaphore_wait(bar, greeted)

    def peer(n):
        r, flip = n // 2, n % 2
        core = lax.rem(c + flip, 2)
        to = lax.rem(x + spread(r), nx) * 2 + core
        source = lax.rem(x + nx - spread(r), nx) * 2 + core
        return to, source

    def id_copy(n):
        to, _ = peer(n)
        return remote(ids.at[to], gids.at[owner], s_id.at[n], r_id.at[n], {"owner": to, "dp": group})

    loads[5].wait()
    for n in range(1, owners):
        id_copy(n).start()
    gids[owner] = ids[owner]

    loads[0].wait()
    mate = remote(docs, sdocs, s_doc, r_doc, chip(0, 0, 0, 1 - c))
    mate.start()
    loads[1].wait()
    squashed = jnp.tanh(jnp.dot(docs[...], weight[...], preferred_element_type=F32))
    emb[...] = (docs[...].astype(F32) + squashed).astype(BF16)
    slope[...] = 1.0 - squashed * squashed
    loads[2].wait()
    loads[6].wait()
    loads[7].wait()

    def row_copy(n):
        to, _ = peer(n)
        return remote(srows.at[to], frows.at[owner], s_f.at[n], r_f.at[n], {"owner": to, "dp": group})

    def scale_copy(n):
        to, _ = peer(n)
        return remote(sscale.at[to], fscale.at[owner], s_c.at[n], r_c.at[n], {"owner": to, "dp": group})

    scale_rows = jnp.broadcast_to(scale[...].reshape(1, rows_held), (16, rows_held))

    def serve(m, _):
        n = lax.rem(m + 2, owners)
        to, _source = peer(n)

        @pl.when(n > 0)
        def _():
            id_copy(n).wait_send()

        hot = jnp.where(
            lax.broadcasted_iota(I32, (rows_held, cap), 0) == gids[to], 1.0, 0.0
        ).astype(BF16)
        onehot[:, pl.ds(pl.multiple_of(to * cap, cap), cap)] = hot
        rows = lax.dot_general(hot, slab[...], (((0,), (0,)), ((), ())), preferred_element_type=F32).astype(BF16)
        sc = jnp.dot(scale_rows, hot, preferred_element_type=F32).astype(BF16)
        srows[to] = rows
        sscale[to] = sc

        @pl.when(n == 0)
        def _():
            frows[owner] = rows
            fscale[owner] = sc

        @pl.when(n > 0)
        def _():
            row_copy(n).start()
            scale_copy(n).start()

        return 0

    for n in range(1, owners):
        id_copy(n).wait_recv()
    lax.fori_loop(0, owners, serve, 0)

    parts = range(2)
    starts, widths = (0, grads0.shape[-1]), (grads0.shape[-1], grads1.shape[-1])

    def grad_copy(h, n):
        _, source = peer(n)
        return remote(
            grads[h].at[source], back[h].at[owner], s_g.at[h, n], r_g.at[h, n], {"owner": source, "dp": group}
        )

    loads[3].wait()
    loads[4].wait()
    slots[...] = slots32[...].astype(I16)
    marks[...] = (1 + 64 * on32[...]).astype(I16)
    strips = documents // strip

    def count(m, _):
        base = pl.multiple_of((m // strips) * pair, pair)
        lanes = pl.ds(pl.multiple_of((m % strips) * strip, strip), strip)
        index = (lax.broadcasted_iota(I32, (pair, strip), 0) + base).astype(I16)
        total = jnp.zeros((pair, strip), I16)
        for k in range(slots.shape[0]):
            total += jnp.where(slots[k : k + 1, lanes] == index, marks[k : k + 1, lanes], jnp.int16(0))
        tally[pl.ds(base, pair), lanes] = total
        return 0

    lax.fori_loop(0, nx * strips, count, 0)

    def group_of(r):
        first = lax.rem(x + nx - spread(r), nx) * 2
        return first, pl.ds(pl.multiple_of(first * cap, pair), pair)

    def score(r):
        first, span = group_of(r)
        rows = frows[pl.ds(first, 2)].reshape(pair, width)
        factor, live = [], []
        for q in range(2):
            line = fscale[first + q].astype(F32)[0:1]
            factor.append(jnp.broadcast_to(line, (cap, cap)).T[:, 0:1])
            lane = lax.broadcasted_iota(I32, (1, owners), 1)
            asked = jnp.sum(jnp.where(lane == first + q, counts[...].astype(F32), 0.0), axis=1, keepdims=True)
            live.append(jnp.where(lax.broadcasted_iota(I32, (cap, 1), 0).astype(F32) < asked, 1.0, 0.0))
        factor = jnp.concatenate(factor, axis=0)
        live = jnp.concatenate(live, axis=0)
        logits = lax.dot_general(rows, emb[...], (((1,), (1,)), ((), ())), preferred_element_type=F32) * factor
        chance = 0.5 * jnp.tanh(0.5 * logits) + 0.5
        mark = tally[span, :].astype(I32)
        hits = (mark & 63).astype(F32)
        on = (mark >> 6).astype(F32)
        dlogit = ((hits + live) * chance - on) * (1.0 / slots.shape[0])
        dscore[span, :] = (dlogit * factor).astype(BF16)

    def row_grads(r):
        first, span = group_of(r)
        product = jnp.dot(dscore[span, :], emb[...], preferred_element_type=F32).astype(BF16)
        for h in parts:
            mine = product[:, starts[h] : starts[h] + widths[h]]
            grads[h][pl.ds(first, 2)] = mine.reshape(2, cap, widths[h])

    def pulled(r):
        first, span = group_of(r)
        rows = frows[pl.ds(first, 2)].reshape(pair, width)
        return lax.dot_general(dscore[span, :], rows, (((0,), (0,)), ((), ())), preferred_element_type=F32)

    def arrived(n):
        row_copy(n).wait()
        scale_copy(n).wait()

    push[...] = jnp.zeros_like(push)

    def work(r, _):
        @pl.when(r > 0)
        def _():
            arrived(2 * r)

        arrived(2 * r + 1)
        score(r)
        row_grads(r)

        @pl.when(r > 0)
        def _():
            grad_copy(0, 2 * r).start()

        grad_copy(0, 2 * r + 1).start()
        push[...] += pulled(r)
        return 0

    lax.fori_loop(0, far, work, 0)
    for h in parts:
        back[h][owner] = grads[h][owner]
    arrived(2 * far)
    arrived(2 * far + 1)
    score(far)

    def finish_inner(which):
        first, span = group_of(far)
        lanes = pl.ds(pl.multiple_of(which * mid, mid), mid)
        rows = frows[pl.ds(first, 2), :, lanes].reshape(pair, mid)
        last = lax.dot_general(dscore[span, :], rows, (((0,), (0,)), ((), ())), preferred_element_type=F32)
        inner[which] = ((push[:, lanes] + last) * slope[:, lanes]).astype(BF16)

    def outer(side, other):
        return lax.dot_general(side[...], other, (((0,), (0,)), ((), ())), preferred_element_type=F32)

    finish_inner(1 - c)
    swap = remote(inner.at[1 - c], sinner, s_sib, r_sib, chip(0, 0, 0, 1 - c))
    swap.start()
    row_grads(far)
    grad_copy(0, 2 * far).start()
    grad_copy(0, 2 * far + 1).start()
    finish_inner(c)
    enc[...] = outer(docs, inner[c])
    swap.wait()
    mate.wait()
    enc[...] += outer(sdocs, sinner[...])

    def summed(first):
        return enc[pl.ds(pl.multiple_of(first, piece), piece), :]

    def join_p(q, _):
        accp[q] = summed(q * piece).astype(BF16)
        return 0

    def join_q(q, _):
        accq[q] = summed(cut + q * piece).astype(BF16)
        return 0

    lax.fori_loop(0, nx * ny, join_p, 0)
    lax.fori_loop(0, nz, join_q, 0)
    p1, q1 = [], []
    for n, (i, j) in enumerate(plane):
        to = lax.rem(x + i, nx) * ny + lax.rem(y + j, ny)
        p1.append(remote(accp.at[to], gotp.at[n], s_p.at[n], r_p.at[n], chip(i, j, 0, c)))
    for k in rings:
        to = lax.rem(z + k, nz)
        q1.append(remote(accq.at[to], gotq.at[k - 1], s_q.at[k - 1], r_q.at[k - 1], chip(0, 0, k, c)))
    for copy in p1 + q1:
        copy.start()

    for n in range(1, owners):
        grad_copy(1, n).start()

    def cols_a(h):
        return pl.ds(starts[h], gota[h].shape[-1])

    def cols_b(h):
        return pl.ds(starts[h] + gota[h].shape[-1], gotb[h].shape[-1])

    first_a, first_b, second_a, second_b = [[], []], [[], []], [[], []], [[], []]

    def sum_rows(h):
        for n in range(1, owners):
            grad_copy(h, n).wait()
        total = jnp.dot(onehot[...], back[h][...].reshape(owners * cap, widths[h]), preferred_element_type=F32)
        here_cols = pl.ds(starts[h], widths[h])
        own[:, :, :, here_cols] = total.reshape(nz, ny, depth, widths[h])
        ownb[:, :, :, here_cols] = total.astype(BF16).reshape(nz, ny, depth, widths[h])
        for j in cols:
            py = lax.rem(y + j, ny)
            first_a[h].append(remote(ownb.at[:, py, :, cols_a(h)], gota[h].at[j - 1], s_a.at[h, j - 1],
                                     r_a.at[h, j - 1], chip(0, j, 0, c)))
        for k in rings:
            pz = lax.rem(z + k, nz)
            first_b[h].append(remote(ownb.at[pz, :, :, cols_b(h)], gotb[h].at[k - 1], s_b.at[h, k - 1],
                                     r_b.at[h, k - 1], chip(0, 0, k, c)))
        for copy in first_a[h] + first_b[h]:
            copy.start()

    def second_rows(h):
        for copy in first_a[h]:
            copy.wait()

        def join_a(q, _):
            total = own[q, y, :, cols_a(h)]
            for j in cols:
                total += gota[h][j - 1, q].astype(F32)
            acca[h][q] = total
            return 0

        lax.fori_loop(0, nz, join_a, 0)
        for k in rings:
            pz = lax.rem(z + k, nz)
            second_a[h].append(remote(acca[h].at[pz], gota2[h].at[k - 1], s_a2.at[h, k - 1], r_a2.at[h, k - 1],
                                      chip(0, 0, k, c)))
        for copy in second_a[h]:
            copy.start()
        for copy in first_b[h]:
            copy.wait()

        def join_b(q, _):
            total = own[z, q, :, cols_b(h)]
            for k in rings:
                total += gotb[h][k - 1, q].astype(F32)
            accb[h][q] = total
            return 0

        lax.fori_loop(0, ny, join_b, 0)
        for j in cols:
            py = lax.rem(y + j, ny)
            second_b[h].append(remote(accb[h].at[py], gotb2[h].at[j - 1], s_b2.at[h, j - 1], r_b2.at[h, j - 1],
                                      chip(0, j, 0, c)))
        for copy in second_b[h]:
            copy.start()

    def finish_rows(h):
        for copy in second_a[h]:
            copy.wait()
        total = acca[h][z]
        for k in rings:
            total += gota2[h][k - 1]
        slab_out[:, cols_a(h)] = total
        for copy in second_b[h]:
            copy.wait()
        total = accb[h][y]
        for j in cols:
            total += gotb2[h][j - 1]
        slab_out[:, cols_b(h)] = total

    sum_rows(0)

    q2 = []
    for copy in q1:
        copy.wait()
    total = summed(cut + z * piece)
    for k in rings:
        total += gotq[k - 1].astype(F32)
    allx[x] = total
    for i in range(1, nx):
        q2.append(remote(allx.at[x], allx.at[x], s_x.at[i - 1], r_x.at[i - 1], chip(i, 0, 0, c)))
    for copy in q2:
        copy.start()

    for copy in p1:
        copy.wait()
    total = summed(here * piece)
    for n in range(len(plane)):
        total += gotp[n].astype(F32)
    for k in range(nz):
        shares[k] = total[k * share : (k + 1) * share, :]
    p2 = []
    for k in rings:
        pz = lax.rem(z + k, nz)
        p2.append(remote(shares.at[pz], gots.at[k - 1], s_p2.at[k - 1], r_p2.at[k - 1], chip(0, 0, k, c)))
    for copy in p2:
        copy.start()
    second_rows(0)
    for copy in p2:
        copy.wait()
    total = shares[z]
    for k in rings:
        total += gots[k - 1]
    done[z] = total
    p2 = []
    for k in rings:
        p2.append(remote(done.at[z], done.at[z], s_ag.at[k - 1], r_ag.at[k - 1], chip(0, 0, k, c)))
    for copy in p2:
        copy.start()
    for copy in q2:
        copy.wait()
    total = allx[0]
    for i in range(1, nx):
        total += allx[i]
    ally[y] = total
    q2 = []
    for j in cols:
        q2.append(remote(ally.at[y], ally.at[y], s_y.at[j - 1], r_y.at[j - 1], chip(0, j, 0, c)))
    for copy in q2:
        copy.start()

    sum_rows(1)

    p3, q3 = [], []
    for copy in p2:
        copy.wait()
    side = pl.ds(pl.multiple_of(c * mid, mid), mid)
    rows_p = pl.ds(pl.multiple_of(here * piece, piece), piece)
    enc_out[rows_p, side] = jnp.concatenate([done[k] for k in range(nz)], axis=0)
    for n, (i, j) in enumerate(plane):
        part = enc_out.at[rows_p, side]
        p3.append(remote(part, part, s_p3.at[n], r_p3.at[n], chip(i, j, 0, c)))
    for copy in p3:
        copy.start()
    for copy in q2:
        copy.wait()
    total = ally[0]
    for j in cols:
        total += ally[j]
    rows_q = pl.ds(pl.multiple_of(cut + z * piece, piece), piece)
    enc_out[rows_q, side] = total
    for k in rings:
        part = enc_out.at[rows_q, side]
        q3.append(remote(part, part, s_q3.at[k - 1], r_q3.at[k - 1], chip(0, 0, k, c)))
    for copy in q3:
        copy.start()

    second_rows(1)
    finish_rows(0)

    def pass_on(first, n):
        part = enc_out.at[pl.ds(pl.multiple_of(first, piece), piece), side]
        copy = remote(part, part, s_e.at[n], r_e.at[n], chip(0, 0, 0, 1 - c))
        copy.start()
        return copy

    handed = [pass_on(here * piece, 0), pass_on(cut + z * piece, 1)]
    for k in rings:
        q3[k - 1].wait()
        handed.append(pass_on(cut + lax.rem(z + nz - k, nz) * piece, 1 + k))
    for n, (i, j) in enumerate(plane):
        p3[n].wait()
        source = lax.rem(x + nx - i, nx) * ny + lax.rem(y + ny - j, ny)
        handed.append(pass_on(source * piece, nz + 1 + n))

    finish_rows(1)
    for copy in handed:
        copy.wait()


def body(dims, documents, enc_weight, label_slab, row_scale, shortlist, positive, request_ids, counts):
    nx, ny, nz = dims
    docs, width = documents.shape
    held = label_slab.shape[0]
    owners, cap = request_ids.shape
    picks = shortlist.shape[1]
    plane = nx * ny
    depth = held // (ny * nz)
    parts = (2 * width // 3, width // 3)
    mid = width // 2
    piece = width // (plane + nz)
    share = piece // nz
    slot_count = owners * cap
    f32 = lambda *shape: pltpu.VMEM(shape, F32)
    b16 = lambda *shape: pltpu.VMEM(shape, BF16)
    i32 = lambda *shape: pltpu.VMEM(shape, I32)
    i16 = lambda *shape: pltpu.VMEM(shape, I16)
    dma = lambda n: [pltpu.SemaphoreType.DMA((n,))] * 2
    two = lambda n: [pltpu.SemaphoreType.DMA((2, n))] * 2
    vmem = pl.BlockSpec(memory_space=pltpu.VMEM)
    slab_grad, enc_grad = pl.pallas_call(
        functools.partial(step_kernel, dims),
        out_shape=(jax.ShapeDtypeStruct((depth, width), F32), jax.ShapeDtypeStruct((width, width), F32)),
        in_specs=[pl.BlockSpec(memory_space=pltpu.HBM)] * 8,
        out_specs=[vmem] * 2,
        scratch_shapes=[
            i32(owners, 1, cap), i32(1, owners), b16(held), b16(docs, width), b16(width, width), b16(held, width), i32(picks, docs), i32(picks, docs),
            i16(picks, docs), i16(picks, docs),
            b16(docs, width), f32(docs, width), f32(docs, width), b16(held, slot_count),
            b16(owners, cap, width), b16(owners, cap, width),
            b16(owners, 16, cap), b16(owners, 16, cap), i32(owners, 1, cap),
            i16(slot_count, docs), b16(slot_count, docs),
            *(b16(owners, cap, p) for p in parts), *(b16(owners, cap, p) for p in parts),
            f32(nz, ny, depth, width), b16(nz, ny, depth, width),
            *(b16(ny - 1, nz, depth, p // 2) for p in parts), *(b16(nz - 1, ny, depth, p // 2) for p in parts),
            *(f32(nz, depth, p // 2) for p in parts), *(f32(ny, depth, p // 2) for p in parts),
            *(f32(nz - 1, depth, p // 2) for p in parts), *(f32(ny - 1, depth, p // 2) for p in parts),
            b16(2, docs, mid), b16(docs, mid), b16(docs, width), f32(width, mid),
            b16(plane, piece, mid), b16(nz, piece, mid),
            b16(plane - 1, piece, mid), b16(nz - 1, piece, mid),
            f32(nz, share, mid), f32(nz - 1, share, mid), f32(nz, share, mid),
            f32(nx, piece, mid), f32(ny, piece, mid),
            pltpu.SemaphoreType.DMA((8,)), *dma(owners), *dma(owners), *dma(owners), *two(owners),
            *two(ny - 1), *two(nz - 1), *two(nz - 1), *two(ny - 1),
            pltpu.SemaphoreType.DMA, pltpu.SemaphoreType.DMA,
            pltpu.SemaphoreType.DMA, pltpu.SemaphoreType.DMA,
            *dma(plane - 1), *dma(nz - 1), *dma(nz - 1), *dma(nz - 1), *dma(nx - 1), *dma(ny - 1), *dma(plane - 1), *dma(nz - 1),
            *dma(plane + nz),
        ],
        compiler_params=pltpu.CompilerParams(
            collective_id=1, has_side_effects=True, vmem_limit_bytes=44 * 2**20
        ),
        cost_estimate=pl.CostEstimate(flops=10**10, bytes_accessed=10**7, transcendentals=2 * 10**6),
        name="classifier_step",
    )(*(pltpu.with_memory_space_constraint(operand, pltpu.HBM) for operand in (
        documents,
        enc_weight,
        label_slab,
        row_scale,
        request_ids.reshape(owners, 1, cap),
        shortlist.T,
        positive.T,
        counts,
    )))
    return slab_grad, enc_grad


def solution(mesh):
    return jax.shard_map(
        functools.partial(body, torus(mesh)),
        mesh=mesh,
        in_specs=(
            P(("owner", "dp"), None),
            P(),
            P("owner", None),
            P("owner"),
            P(("owner", "dp"), None),
            P(("owner", "dp"), None),
            P(("owner", "dp"), None),
            P(("owner", "dp"), None),
        ),
        out_specs=(P(("owner", "dp"), None), P()),
        check_vma=False,
    )
```

```python
import functools

import jax
import jax.numpy as jnp
from jax import lax
from jax.experimental import pallas as pl
from jax.experimental.pallas import tpu as pltpu
from jax.sharding import PartitionSpec as P

MESH = pl.DeviceIdType.MESH
F32 = jnp.float32
BF16 = jnp.bfloat16
I32 = jnp.int32
I16 = jnp.int16


def torus(mesh):
    owners, groups = mesh.shape["owner"], mesh.shape["dp"]
    ny = 4 if groups >= 16 else 2
    return owners // 2, ny, groups // ny


def remote(src, dst, send, recv, target):
    return pltpu.make_async_remote_copy(
        src_ref=src, dst_ref=dst, send_sem=send, recv_sem=recv, device_id=target, device_id_type=MESH
    )


def step_kernel(
    dims, docs_in, weight_in, slab_in, scale_in, ids_in, slots_in, on_in, counts_in, slab_out, enc_out,
    ids, counts, scale, docs, weight, slab, slots32, on32, slots, marks, emb, slope, push, onehot, srows, frows, sscale, fscale, gids, tally, dscore, grads0, grads1, back0, back1,
    own, ownb, gota0, gota1, gotb0, gotb1, acca0, acca1, accb0, accb1, gota20, gota21, gotb20, gotb21,
    inner, sinner, sdocs, enc, accp, accq, gotp, gotq, shares, gots, done, allx, ally,
    s_in, s_id, r_id, s_f, r_f, s_c, r_c, s_g, r_g,
    s_a, r_a, s_b, r_b, s_a2, r_a2, s_b2, r_b2,
    s_sib, r_sib, s_doc, r_doc, s_p, r_p, s_q, r_q, s_p2, r_p2, s_ag, r_ag, s_x, r_x, s_y, r_y, s_p3, r_p3, s_q3, r_q3, s_e, r_e,
):
    nx, ny, nz = dims
    owner, group = lax.axis_index("owner"), lax.axis_index("dp")
    x, c = owner // 2, owner % 2
    y, z = group % ny, group // ny
    here = x * ny + y
    owners = 2 * nx
    cap = srows.shape[1]
    pair = 2 * cap
    documents, width = docs.shape
    rows_held = slab.shape[0]
    depth = own.shape[-2]
    grads, back = (grads0, grads1), (back0, back1)
    gota, gotb, acca, accb = (gota0, gota1), (gotb0, gotb1), (acca0, acca1), (accb0, accb1)
    gota2, gotb2 = (gota20, gota21), (gotb20, gotb21)
    piece = accp.shape[1]
    share = shares.shape[1]
    mid = enc.shape[1]
    cut = nx * ny * piece
    strip = min(128, documents)
    far = nx - 1

    plane = [(i, j) for i in range(nx) for j in range(ny) if (i, j) != (0, 0)]
    rings = list(range(1, nz))
    cols = list(range(1, ny))

    def chip(i, j, k, core):
        return {"owner": lax.rem(x + i, nx) * 2 + core, "dp": lax.rem(z + k, nz) * ny + lax.rem(y + j, ny)}

    def spread(r):
        return r + (r // 2) * (5 - 2 * r) if nx == 4 else r

    loads = [
        pltpu.make_async_copy(src, dst, s_in.at[n])
        for n, (src, dst) in enumerate(
            (
                (docs_in, docs), (weight_in, weight), (slab_in, slab), (slots_in, slots32), (on_in, on32),
                (ids_in, ids), (counts_in, counts), (scale_in, scale),
            )
        )
    ]
    for load in loads[5:] + loads[:5]:
        load.start()

    bar = pltpu.get_barrier_semaphore()
    greeted = 0
    for i, j in plane:
        pl.semaphore_signal(bar, inc=1, device_id=chip(i, j, 0, c), device_id_type=MESH)
        greeted += 1
    for i in range(nx):
        pl.semaphore_signal(bar, inc=1, device_id=chip(i, 0, 0, 1 - c), device_id_type=MESH)
        greeted += 1
    for k in rings:
        pl.semaphore_signal(bar, inc=1, device_id=chip(0, 0, k, c), device_id_type=MESH)
        greeted += 1
    pl.semaphore_wait(bar, greeted)

    def peer(n):
        r, flip = n // 2, n % 2
        core = lax.rem(c + flip, 2)
        to = lax.rem(x + spread(r), nx) * 2 + core
        source = lax.rem(x + nx - spread(r), nx) * 2 + core
        return to, source

    def id_copy(n):
        to, _ = peer(n)
        return remote(ids.at[to], gids.at[owner], s_id.at[n], r_id.at[n], {"owner": to, "dp": group})

    loads[5].wait()
    for n in range(1, owners):
        id_copy(n).start()
    gids[owner] = ids[owner]

    loads[0].wait()
    mate = remote(docs, sdocs, s_doc, r_doc, chip(0, 0, 0, 1 - c))
    mate.start()
    loads[1].wait()
    squashed = jnp.tanh(jnp.dot(docs[...], weight[...], preferred_element_type=F32))
    emb[...] = (docs[...].astype(F32) + squashed).astype(BF16)
    slope[...] = 1.0 - squashed * squashed
    loads[2].wait()
    loads[6].wait()
    loads[7].wait()

    def row_copy(n):
        to, _ = peer(n)
        return remote(srows.at[to], frows.at[owner], s_f.at[n], r_f.at[n], {"owner": to, "dp": group})

    def scale_copy(n):
        to, _ = peer(n)
        return remote(sscale.at[to], fscale.at[owner], s_c.at[n], r_c.at[n], {"owner": to, "dp": group})

    scale_rows = jnp.broadcast_to(scale[...].reshape(1, rows_held), (16, rows_held))

    def serve(m, _):
        n = lax.rem(m + 2, owners)
        to, _source = peer(n)

        @pl.when(n > 0)
        def _():
            id_copy(n).wait_send()

        hot = jnp.where(
            lax.broadcasted_iota(I32, (rows_held, cap), 0) == gids[to], 1.0, 0.0
        ).astype(BF16)
        onehot[:, pl.ds(pl.multiple_of(to * cap, cap), cap)] = hot
        rows = lax.dot_general(hot, slab[...], (((0,), (0,)), ((), ())), preferred_element_type=F32).astype(BF16)
        sc = jnp.dot(scale_rows, hot, preferred_element_type=F32).astype(BF16)
        srows[to] = rows
        sscale[to] = sc

        @pl.when(n == 0)
        def _():
            frows[owner] = rows
            fscale[owner] = sc

        @pl.when(n > 0)
        def _():
            row_copy(n).start()
            scale_copy(n).start()

        return 0

    for n in range(1, owners):
        id_copy(n).wait_recv()
    lax.fori_loop(0, owners, serve, 0)

    parts = range(2)
    starts, widths = (0, grads0.shape[-1]), (grads0.shape[-1], grads1.shape[-1])

    def grad_copy(h, n):
        _, source = peer(n)
        return remote(
            grads[h].at[source], back[h].at[owner], s_g.at[h, n], r_g.at[h, n], {"owner": source, "dp": group}
        )

    loads[3].wait()
    loads[4].wait()
    slots[...] = slots32[...].astype(I16)
    marks[...] = (1 + 64 * on32[...]).astype(I16)
    strips = documents // strip

    def count(m, _):
        base = pl.multiple_of((m // strips) * pair, pair)
        lanes = pl.ds(pl.multiple_of((m % strips) * strip, strip), strip)
        index = (lax.broadcasted_iota(I32, (pair, strip), 0) + base).astype(I16)
        total = jnp.zeros((pair, strip), I16)
        for k in range(slots.shape[0]):
            total += jnp.where(slots[k : k + 1, lanes] == index, marks[k : k + 1, lanes], jnp.int16(0))
        tally[pl.ds(base, pair), lanes] = total
        return 0

    lax.fori_loop(0, nx * strips, count, 0)

    def group_of(r):
        first = lax.rem(x + nx - spread(r), nx) * 2
        return first, pl.ds(pl.multiple_of(first * cap, pair), pair)

    def score(r):
        first, span = group_of(r)
        rows = frows[pl.ds(first, 2)].reshape(pair, width)
        factor, live = [], []
        for q in range(2):
            line = fscale[first + q].astype(F32)[0:1]
            factor.append(jnp.broadcast_to(line, (cap, cap)).T[:, 0:1])
            lane = lax.broadcasted_iota(I32, (1, owners), 1)
            asked = jnp.sum(jnp.where(lane == first + q, counts[...].astype(F32), 0.0), axis=1, keepdims=True)
            live.append(jnp.where(lax.broadcasted_iota(I32, (cap, 1), 0).astype(F32) < asked, 1.0, 0.0))
        factor = jnp.concatenate(factor, axis=0)
        live = jnp.concatenate(live, axis=0)
        logits = lax.dot_general(rows, emb[...], (((1,), (1,)), ((), ())), preferred_element_type=F32) * factor
        chance = 0.5 * jnp.tanh(0.5 * logits) + 0.5
        mark = tally[span, :].astype(I32)
        hits = (mark & 63).astype(F32)
        on = (mark >> 6).astype(F32)
        dlogit = ((hits + live) * chance - on) * (1.0 / slots.shape[0])
        dscore[span, :] = (dlogit * factor).astype(BF16)

    def row_grads(r):
        first, span = group_of(r)
        product = jnp.dot(dscore[span, :], emb[...], preferred_element_type=F32).astype(BF16)
        for h in parts:
            mine = product[:, starts[h] : starts[h] + widths[h]]
            grads[h][pl.ds(first, 2)] = mine.reshape(2, cap, widths[h])

    def pulled(r):
        first, span = group_of(r)
        rows = frows[pl.ds(first, 2)].reshape(pair, width)
        return lax.dot_general(dscore[span, :], rows, (((0,), (0,)), ((), ())), preferred_element_type=F32)

    def arrived(n):
        row_copy(n).wait()
        scale_copy(n).wait()

    push[...] = jnp.zeros_like(push)

    def work(r, _):
        @pl.when(r > 0)
        def _():
            arrived(2 * r)

        arrived(2 * r + 1)
        score(r)
        row_grads(r)

        @pl.when(r > 0)
        def _():
            grad_copy(0, 2 * r).start()

        grad_copy(0, 2 * r + 1).start()
        push[...] += pulled(r)
        return 0

    lax.fori_loop(0, far, work, 0)
    for h in parts:
        back[h][owner] = grads[h][owner]
    arrived(2 * far)
    arrived(2 * far + 1)
    score(far)

    def finish_inner(which):
        first, span = group_of(far)
        lanes = pl.ds(pl.multiple_of(which * mid, mid), mid)
        rows = frows[pl.ds(first, 2), :, lanes].reshape(pair, mid)
        last = lax.dot_general(dscore[span, :], rows, (((0,), (0,)), ((), ())), preferred_element_type=F32)
        inner[which] = ((push[:, lanes] + last) * slope[:, lanes]).astype(BF16)

    def outer(side, other):
        return lax.dot_general(side[...], other, (((0,), (0,)), ((), ())), preferred_element_type=F32)

    finish_inner(1 - c)
    swap = remote(inner.at[1 - c], sinner, s_sib, r_sib, chip(0, 0, 0, 1 - c))
    swap.start()
    row_grads(far)
    grad_copy(0, 2 * far).start()
    grad_copy(0, 2 * far + 1).start()
    finish_inner(c)
    enc[...] = outer(docs, inner[c])
    swap.wait()
    mate.wait()
    enc[...] += outer(sdocs, sinner[...])

    def summed(first):
        return enc[pl.ds(pl.multiple_of(first, piece), piece), :]

    def join_p(q, _):
        accp[q] = summed(q * piece).astype(BF16)
        return 0

    def join_q(q, _):
        accq[q] = summed(cut + q * piece).astype(BF16)
        return 0

    lax.fori_loop(0, nx * ny, join_p, 0)
    lax.fori_loop(0, nz, join_q, 0)
    p1, q1 = [], []
    for n, (i, j) in enumerate(plane):
        to = lax.rem(x + i, nx) * ny + lax.rem(y + j, ny)
        p1.append(remote(accp.at[to], gotp.at[n], s_p.at[n], r_p.at[n], chip(i, j, 0, c)))
    for k in rings:
        to = lax.rem(z + k, nz)
        q1.append(remote(accq.at[to], gotq.at[k - 1], s_q.at[k - 1], r_q.at[k - 1], chip(0, 0, k, c)))
    for copy in p1 + q1:
        copy.start()

    for n in range(1, owners):
        grad_copy(1, n).start()

    def cols_a(h):
        return pl.ds(starts[h], gota[h].shape[-1])

    def cols_b(h):
        return pl.ds(starts[h] + gota[h].shape[-1], gotb[h].shape[-1])

    first_a, first_b, second_a, second_b = [[], []], [[], []], [[], []], [[], []]

    def sum_rows(h):
        for n in range(1, owners):
            grad_copy(h, n).wait()
        total = jnp.dot(onehot[...], back[h][...].reshape(owners * cap, widths[h]), preferred_element_type=F32)
        here_cols = pl.ds(starts[h], widths[h])
        own[:, :, :, here_cols] = total.reshape(nz, ny, depth, widths[h])
        ownb[:, :, :, here_cols] = total.astype(BF16).reshape(nz, ny, depth, widths[h])
        for j in cols:
            py = lax.rem(y + j, ny)
            first_a[h].append(remote(ownb.at[:, py, :, cols_a(h)], gota[h].at[j - 1], s_a.at[h, j - 1],
                                     r_a.at[h, j - 1], chip(0, j, 0, c)))
        for k in rings:
            pz = lax.rem(z + k, nz)
            first_b[h].append(remote(ownb.at[pz, :, :, cols_b(h)], gotb[h].at[k - 1], s_b.at[h, k - 1],
                                     r_b.at[h, k - 1], chip(0, 0, k, c)))
        for copy in first_a[h] + first_b[h]:
            copy.start()

    def second_rows(h):
        for copy in first_a[h]:
            copy.wait()

        def join_a(q, _):
            total = own[q, y, :, cols_a(h)]
            for j in cols:
                total += gota[h][j - 1, q].astype(F32)
            acca[h][q] = total
            return 0

        lax.fori_loop(0, nz, join_a, 0)
        for k in rings:
            pz = lax.rem(z + k, nz)
            second_a[h].append(remote(acca[h].at[pz], gota2[h].at[k - 1], s_a2.at[h, k - 1], r_a2.at[h, k - 1],
                                      chip(0, 0, k, c)))
        for copy in second_a[h]:
            copy.start()
        for copy in first_b[h]:
            copy.wait()

        def join_b(q, _):
            total = own[z, q, :, cols_b(h)]
            for k in rings:
                total += gotb[h][k - 1, q].astype(F32)
            accb[h][q] = total
            return 0

        lax.fori_loop(0, ny, join_b, 0)
        for j in cols:
            py = lax.rem(y + j, ny)
            second_b[h].append(remote(accb[h].at[py], gotb2[h].at[j - 1], s_b2.at[h, j - 1], r_b2.at[h, j - 1],
                                      chip(0, j, 0, c)))
        for copy in second_b[h]:
            copy.start()

    def finish_rows(h):
        for copy in second_a[h]:
            copy.wait()
        total = acca[h][z]
        for k in rings:
            total += gota2[h][k - 1]
        slab_out[:, cols_a(h)] = total
        for copy in second_b[h]:
            copy.wait()
        total = accb[h][y]
        for j in cols:
            total += gotb2[h][j - 1]
        slab_out[:, cols_b(h)] = total

    sum_rows(0)

    q2 = []
    for copy in q1:
        copy.wait()
    total = summed(cut + z * piece)
    for k in rings:
        total += gotq[k - 1].astype(F32)
    allx[x] = total
    for i in range(1, nx):
        q2.append(remote(allx.at[x], allx.at[x], s_x.at[i - 1], r_x.at[i - 1], chip(i, 0, 0, c)))
    for copy in q2:
        copy.start()

    for copy in p1:
        copy.wait()
    total = summed(here * piece)
    for n in range(len(plane)):
        total += gotp[n].astype(F32)
    for k in range(nz):
        shares[k] = total[k * share : (k + 1) * share, :]
    p2 = []
    for k in rings:
        pz = lax.rem(z + k, nz)
        p2.append(remote(shares.at[pz], gots.at[k - 1], s_p2.at[k - 1], r_p2.at[k - 1], chip(0, 0, k, c)))
    for copy in p2:
        copy.start()
    for copy in p2:
        copy.wait()
    total = shares[z]
    for k in rings:
        total += gots[k - 1]
    done[z] = total
    p2 = []
    for k in rings:
        p2.append(remote(done.at[z], done.at[z], s_ag.at[k - 1], r_ag.at[k - 1], chip(0, 0, k, c)))
    for copy in p2:
        copy.start()
    for copy in q2:
        copy.wait()
    total = allx[0]
    for i in range(1, nx):
        total += allx[i]
    ally[y] = total
    q2 = []
    for j in cols:
        q2.append(remote(ally.at[y], ally.at[y], s_y.at[j - 1], r_y.at[j - 1], chip(0, j, 0, c)))
    for copy in q2:
        copy.start()

    second_rows(0)
    sum_rows(1)

    p3, q3 = [], []
    for copy in p2:
        copy.wait()
    side = pl.ds(pl.multiple_of(c * mid, mid), mid)
    rows_p = pl.ds(pl.multiple_of(here * piece, piece), piece)
    enc_out[rows_p, side] = jnp.concatenate([done[k] for k in range(nz)], axis=0)
    for n, (i, j) in enumerate(plane):
        part = enc_out.at[rows_p, side]
        p3.append(remote(part, part, s_p3.at[n], r_p3.at[n], chip(i, j, 0, c)))
    for copy in p3:
        copy.start()
    for copy in q2:
        copy.wait()
    total = ally[0]
    for j in cols:
        total += ally[j]
    rows_q = pl.ds(pl.multiple_of(cut + z * piece, piece), piece)
    enc_out[rows_q, side] = total
    for k in rings:
        part = enc_out.at[rows_q, side]
        q3.append(remote(part, part, s_q3.at[k - 1], r_q3.at[k - 1], chip(0, 0, k, c)))
    for copy in q3:
        copy.start()

    second_rows(1)
    finish_rows(0)

    def pass_on(first, n):
        part = enc_out.at[pl.ds(pl.multiple_of(first, piece), piece), side]
        copy = remote(part, part, s_e.at[n], r_e.at[n], chip(0, 0, 0, 1 - c))
        copy.start()
        return copy

    handed = [pass_on(here * piece, 0), pass_on(cut + z * piece, 1)]
    for k in rings:
        q3[k - 1].wait()
        handed.append(pass_on(cut + lax.rem(z + nz - k, nz) * piece, 1 + k))
    for n, (i, j) in enumerate(plane):
        p3[n].wait()
        source = lax.rem(x + nx - i, nx) * ny + lax.rem(y + ny - j, ny)
        handed.append(pass_on(source * piece, nz + 1 + n))

    finish_rows(1)
    for copy in handed:
        copy.wait()


def body(dims, documents, enc_weight, label_slab, row_scale, shortlist, positive, request_ids, counts):
    nx, ny, nz = dims
    docs, width = documents.shape
    held = label_slab.shape[0]
    owners, cap = request_ids.shape
    picks = shortlist.shape[1]
    plane = nx * ny
    depth = held // (ny * nz)
    parts = (2 * width // 3, width // 3)
    mid = width // 2
    piece = width // (plane + nz)
    share = piece // nz
    slot_count = owners * cap
    f32 = lambda *shape: pltpu.VMEM(shape, F32)
    b16 = lambda *shape: pltpu.VMEM(shape, BF16)
    i32 = lambda *shape: pltpu.VMEM(shape, I32)
    i16 = lambda *shape: pltpu.VMEM(shape, I16)
    dma = lambda n: [pltpu.SemaphoreType.DMA((n,))] * 2
    two = lambda n: [pltpu.SemaphoreType.DMA((2, n))] * 2
    vmem = pl.BlockSpec(memory_space=pltpu.VMEM)
    slab_grad, enc_grad = pl.pallas_call(
        functools.partial(step_kernel, dims),
        out_shape=(jax.ShapeDtypeStruct((depth, width), F32), jax.ShapeDtypeStruct((width, width), F32)),
        in_specs=[pl.BlockSpec(memory_space=pltpu.HBM)] * 8,
        out_specs=[vmem] * 2,
        scratch_shapes=[
            i32(owners, 1, cap), i32(1, owners), b16(held), b16(docs, width), b16(width, width), b16(held, width), i32(picks, docs), i32(picks, docs),
            i16(picks, docs), i16(picks, docs),
            b16(docs, width), f32(docs, width), f32(docs, width), b16(held, slot_count),
            b16(owners, cap, width), b16(owners, cap, width),
            b16(owners, 16, cap), b16(owners, 16, cap), i32(owners, 1, cap),
            i16(slot_count, docs), b16(slot_count, docs),
            *(b16(owners, cap, p) for p in parts), *(b16(owners, cap, p) for p in parts),
            f32(nz, ny, depth, width), b16(nz, ny, depth, width),
            *(b16(ny - 1, nz, depth, p // 2) for p in parts), *(b16(nz - 1, ny, depth, p // 2) for p in parts),
            *(f32(nz, depth, p // 2) for p in parts), *(f32(ny, depth, p // 2) for p in parts),
            *(f32(nz - 1, depth, p // 2) for p in parts), *(f32(ny - 1, depth, p // 2) for p in parts),
            b16(2, docs, mid), b16(docs, mid), b16(docs, width), f32(width, mid),
            b16(plane, piece, mid), b16(nz, piece, mid),
            b16(plane - 1, piece, mid), b16(nz - 1, piece, mid),
            f32(nz, share, mid), f32(nz - 1, share, mid), f32(nz, share, mid),
            f32(nx, piece, mid), f32(ny, piece, mid),
            pltpu.SemaphoreType.DMA((8,)), *dma(owners), *dma(owners), *dma(owners), *two(owners),
            *two(ny - 1), *two(nz - 1), *two(nz - 1), *two(ny - 1),
            pltpu.SemaphoreType.DMA, pltpu.SemaphoreType.DMA,
            pltpu.SemaphoreType.DMA, pltpu.SemaphoreType.DMA,
            *dma(plane - 1), *dma(nz - 1), *dma(nz - 1), *dma(nz - 1), *dma(nx - 1), *dma(ny - 1), *dma(plane - 1), *dma(nz - 1),
            *dma(plane + nz),
        ],
        compiler_params=pltpu.CompilerParams(
            collective_id=1, has_side_effects=True, vmem_limit_bytes=44 * 2**20
        ),
        cost_estimate=pl.CostEstimate(flops=10**10, bytes_accessed=10**7, transcendentals=2 * 10**6),
        name="classifier_step",
    )(*(pltpu.with_memory_space_constraint(operand, pltpu.HBM) for operand in (
        documents,
        enc_weight,
        label_slab,
        row_scale,
        request_ids.reshape(owners, 1, cap),
        shortlist.T,
        positive.T,
        counts,
    )))
    return slab_grad, enc_grad


def solution(mesh):
    return jax.shard_map(
        functools.partial(body, torus(mesh)),
        mesh=mesh,
        in_specs=(
            P(("owner", "dp"), None),
            P(),
            P("owner", None),
            P("owner"),
            P(("owner", "dp"), None),
            P(("owner", "dp"), None),
            P(("owner", "dp"), None),
            P(("owner", "dp"), None),
        ),
        out_specs=(P(("owner", "dp"), None), P()),
        check_vma=False,
    )
```
